32 devices in a mesh: section: 2 (over core), chan: 4 (over z), dp: 4 (over y, x).
Axes of the slice: x: 2, y: 2, z: 4, core: 2. Of those that a mesh axis runs over, the one named last changes fastest.
Arguments:
- inputs: bfloat16 [2, 16, 1024, 768], P(None, ('dp', 'chan')), may hold values from -6 to 6
- lengths: int32 [2, 16], P(None, ('dp', 'chan')), may hold values from 512 to 1024, as said below
- out_grad: bfloat16 [2, 16, 1024, 768], P(None, ('dp', 'chan')), may hold values from -6 to 6
- ln_mix_gain: bfloat16 [1, 768], P(None, 'chan'), may hold values from 0.5 to 1.5
- w_in: bfloat16 [1, 768, 2304], P(None, 'chan'), may hold values from -0.21875 to 0.21875
- short_taps: bfloat16 [1, 3, 2304], P(None, None, 'chan'), may hold values from -3 to 3
- long_taps: bfloat16 [1, 1024, 768], P(None, None, 'chan'), may hold values from -0.5 to 0.5
- w_out: bfloat16 [1, 768, 768], P(None, 'chan'), may hold values from -0.21875 to 0.21875
- ln_mlp_gain: bfloat16 [1, 768], P(None, 'chan'), may hold values from 0.5 to 1.5
- w_up: bfloat16 [1, 768, 3072], P(None, 'chan'), may hold values from -0.21875 to 0.21875
- w_down: bfloat16 [1, 3072, 768], P(None, 'chan'), may hold values from -0.109375 to 0.109375
Outputs:
- activations: bfloat16 [2, 2, 16, 1024, 768], P('section', None, ('dp', 'chan'))
- act_grads: float32 [2, 2, 16, 1024, 768], P('section', None, ('dp', 'chan'))
- grad_ln_mix_gain: float32 [1, 768], P(None, 'chan')
- grad_w_in: float32 [1, 768, 2304], P(None, 'chan')
- grad_short_taps: float32 [1, 3, 2304], P(None, None, 'chan')
- grad_long_taps: float32 [1, 1024, 768], P(None, None, 'chan')
- grad_w_out: float32 [1, 768, 768], P(None, 'chan')
- grad_ln_mlp_gain: float32 [1, 768], P(None, 'chan')
- grad_w_up: float32 [1, 768, 3072], P(None, 'chan')
- grad_w_down: float32 [1, 3072, 768], P(None, 'chan')
The draws below stay inside these ranges and needn't reach their ends.
Inputs may be any that keep to these rules, and one draw needn't show every extreme that they name: `lengths`: in every micro-batch one slot holds 1024 live positions and another holds 512.
All inputs are finite; a program needn't handle non-finite values.
Results may differ from the reference program's by a relative error of at most 0.015.
Values may be sent and summed in bfloat16 or wider, within the bound.
No kernel may reach another device: no remote copies, remote signals or barrier semaphores. Data moves between devices by JAX's collectives and lax.ppermute only.
A program may use at most 384 MiB of HBM per device.

```python
import jax
import jax.numpy as jnp
from jax import lax

D = 768
FF = 3072
SEQ = 1024
MB = 2
LAYERS = 1
SLOTS = 16
N_SECTION = 2


def draw_lengths(key, part):
    key = jax.random.fold_in(key, 11)
    drawn = jax.random.randint(key, (MB, SLOTS), SEQ // 2, SEQ + 1)
    longest = jax.random.randint(jax.random.fold_in(key, 1), (MB, 1), 0, SLOTS)
    offset_draw = jax.random.randint(jax.random.fold_in(key, 2), (MB, 1), 1, SLOTS)
    shortest = (longest + offset_draw) % SLOTS
    column_ids = jnp.arange(SLOTS, dtype=jnp.int32)[None, :]
    drawn = jnp.where(column_ids == longest, SEQ, drawn)
    drawn = jnp.where(column_ids == shortest, SEQ // 2, drawn)
    return drawn.astype(jnp.int32)


def block_scale(stream_key, shape, pieces, least, high):
    loudness, own = 1.0, jax.random.fold_in(stream_key, 6)
    for axis_at, parts in pieces:
        heights = jnp.exp(jax.random.uniform(jax.random.fold_in(own, axis_at), (parts,), jnp.float32, least / len(pieces), high / len(pieces)))
        loudness = loudness * jnp.repeat(heights, shape[axis_at] // parts).reshape([-1 if axis == axis_at else 1 for axis in range(len(shape))])
    return loudness


def centred(rng, dims, scale, reach, cuts=(), kind=jnp.bfloat16):
    array = scale * jax.random.normal(rng, dims, jnp.float32)
    if cuts:
        array = array * block_scale(rng, dims, cuts, -0.22, 0.18)
    return jnp.clip(array, -reach, reach).astype(kind)


def setup_inputs(seed: int = 0) -> dict:
    key_list = jax.random.split(jax.random.key(seed), 12)
    return {
        "inputs": centred(key_list[0], (MB, SLOTS, SEQ, D), 1.0, 6.0, ((1, 16),)),
        "lengths": draw_lengths(jax.random.fold_in(key_list[11], 71), 0),
        "out_grad": centred(key_list[2], (MB, SLOTS, SEQ, D), 1.0, 6.0, ((1, 16),)),
        "ln_mix_gain": jnp.clip(1.0 + 0.1 * jax.random.normal(key_list[3], (LAYERS, D), jnp.float32), 0.5, 1.5).astype(jnp.bfloat16),
        "w_in": centred(key_list[4], (LAYERS, D, 3 * D), D ** -0.5, 0.21875, ((1, 4),)),
        "short_taps": centred(key_list[5], (LAYERS, 3, 3 * D), 0.6, 3.0, ((2, 4),)),
        "long_taps": centred(key_list[6], (LAYERS, SEQ, D), 0.08, 0.5, ((2, 4),)),
        "w_out": centred(key_list[7], (LAYERS, D, D), D ** -0.5, 0.21875, ((1, 4),)),
        "ln_mlp_gain": jnp.clip(1.0 + 0.1 * jax.random.normal(key_list[8], (LAYERS, D), jnp.float32), 0.5, 1.5).astype(jnp.bfloat16),
        "w_up": centred(key_list[9], (LAYERS, D, FF), D ** -0.5, 0.21875, ((1, 4),)),
        "w_down": centred(key_list[10], (LAYERS, FF, D), FF ** -0.5, 0.109375, ((1, 4),)),
    }


decay_rate = 0.003
highest = lax.Precision.HIGHEST

@jax.custom_vjp
def low(v):
    return lax.optimization_barrier(v.astype(jnp.bfloat16)).astype(jnp.float32)

@jax.custom_vjp
def low_back(v):
    return v

def low_keep(v):
    return (low(v), None)

def low_pass(kept, grad):
    return (grad,)

def back_keep(v):
    return (v, None)

def back_low(kept, grad):
    return (low(grad),)
low.defvjp(low_keep, low_pass)
low_back.defvjp(back_keep, back_low)

def layer_norm(values, gain_vec):
    centered = values - lax.optimization_barrier(jnp.mean(values, axis=-1, keepdims=True))
    spread = lax.optimization_barrier(jnp.mean(centered * centered, axis=-1, keepdims=True))
    return centered * lax.rsqrt(spread + 1e-05) * gain_vec

def causal_conv(signal, kernel):
    length = signal.shape[0]
    spectrum = jnp.fft.rfft(signal, n=2 * length, axis=0) * jnp.fft.rfft(kernel, n=2 * length, axis=0)
    return jnp.fft.irfft(spectrum, n=2 * length, axis=0)[:length]

def short_conv(values, short_taps):
    length = values.shape[0]
    padded = jnp.pad(values, ((2, 0), (0, 0)))
    return short_taps[0] * padded[2:] + short_taps[1] * padded[1:length + 1] + short_taps[2] * padded[:length]

def mixer(values, live_mask, gain_vec, proj_in, short_taps, long_taps, proj_out):
    normed = low(layer_norm(values, gain_vec))
    mixed = low_back(jnp.dot(normed, proj_in, precision=highest))
    mixed = short_conv(mixed, short_taps)
    query, key_part, value_part = jnp.split(mixed, 3, axis=1)
    position = jnp.arange(SEQ, dtype=jnp.float32)
    kernel = long_taps * jnp.exp(-decay_rate * position)[:, None]
    gated = low(query * causal_conv(key_part * value_part, kernel))
    branch = low_back(jnp.dot(gated, proj_out, precision=highest))
    return live_mask * (values + branch)

def feed_forward(values, live_mask, gain_vec, proj_up, proj_down):
    normed = low(layer_norm(values, gain_vec))
    pre_act = low_back(jnp.dot(normed, proj_up, precision=highest))
    hidden = low(jax.nn.gelu(pre_act, approximate=False))
    branch = low_back(jnp.dot(hidden, proj_down, precision=highest))
    return live_mask * (values + branch)

def run_sequence(values, offsets, live_mask, params):
    gain_mix, proj_in, short_all, taps_all, proj_out, gain_mlp, proj_up, proj_down = params
    current = values + offsets[0]
    sent_list = []
    for segment in range(N_SECTION):
        layer = segment // 2
        if segment % 2 == 0:
            result = mixer(current, live_mask, gain_mix[layer], proj_in[layer], short_all[layer], taps_all[layer], proj_out[layer])
        else:
            result = feed_forward(current, live_mask, gain_mlp[layer], proj_up[layer], proj_down[layer])
        sent = low(result)
        sent_list.append(sent)
        if segment + 1 < N_SECTION:
            current = low_back(sent) + offsets[segment + 1]
    return jnp.stack(sent_list)

def reference(inputs, lengths, out_grad, ln_mix_gain, w_in, short_taps, long_taps, w_out, ln_mlp_gain, w_up, w_down):
    params = tuple((weight.astype(jnp.float32) for weight in (ln_mix_gain, w_in, short_taps, long_taps, w_out, ln_mlp_gain, w_up, w_down)))
    count = MB * SLOTS
    values = inputs.astype(jnp.float32).reshape(count, SEQ, D)
    position = jnp.arange(SEQ, dtype=jnp.int32)
    live_masks = (position[None, :] < lengths.reshape(count)[:, None]).astype(jnp.float32)[:, :, None]
    offsets = jnp.zeros((count, N_SECTION, SEQ, D), jnp.float32)

    def forward(values, offsets, params):

        def one_item(item):
            return run_sequence(item[0], item[1], item[2], params)
        return lax.map(jax.checkpoint(one_item), (values, offsets, live_masks))
    outputs, pullback = jax.vjp(forward, values, offsets, params)
    cotangent = jnp.zeros_like(outputs).at[:, N_SECTION - 1].set(out_grad.astype(jnp.float32).reshape(count, SEQ, D))
    unused_grad, offset_grads, param_grads = pullback(cotangent)
    activations = jnp.transpose(outputs.reshape(MB, SLOTS, N_SECTION, SEQ, D), (2, 0, 1, 3, 4)).astype(jnp.bfloat16)
    act_grads = jnp.transpose(offset_grads.reshape(MB, SLOTS, N_SECTION, SEQ, D), (2, 0, 1, 3, 4))
    return (activations, act_grads, param_grads[0], param_grads[1], param_grads[2], param_grads[3], param_grads[4], param_grads[5], param_grads[6], param_grads[7])
```

```python
import math

import jax
import jax.numpy as jnp
import ml_dtypes
import numpy as np
from jax import lax
from jax.sharding import PartitionSpec as P

D = 768
FF = 3072
decay_rate = 0.003
bf16 = jnp.bfloat16
f32 = jnp.float32


def odd_basis(length):
    phase = (2 * np.arange(length)[:, None] + 1) * np.arange(length)[None, :] % (4 * length)
    angle = phase * (math.pi / (2 * length))
    return np.concatenate([np.cos(angle), np.sin(angle)], 0).astype(ml_dtypes.bfloat16)


def dot(a, b, ca=1, cb=0):
    return lax.dot_general(a, b, (((ca,), (cb,)), ((), ())), preferred_element_type=f32)


def shift_down(v, n):
    return jnp.pad(v, ((n, 0), (0, 0)))[: v.shape[0]]


def shift_up(v, n):
    return jnp.pad(v, ((0, n), (0, 0)))[n:]


def norm_parts(values):
    centered = values - jnp.mean(values, axis=-1, keepdims=True)
    spread = jnp.mean(centered * centered, axis=-1, keepdims=True)
    inv = lax.rsqrt(spread + 1e-05)
    return centered * inv, inv


def norm_back(grad_normed, hat, inv, gain):
    grad_hat = grad_normed * gain
    return inv * (
        grad_hat
        - jnp.mean(grad_hat, axis=-1, keepdims=True)
        - hat * jnp.mean(grad_hat * hat, axis=-1, keepdims=True)
    )


def body(inputs, lengths, out_grad, ln_mix_gain, w_in, short_taps, long_taps, w_out, ln_mlp_gain, w_up, w_down):
    chans = lax.axis_size("chan")
    own = lax.axis_index("section")
    length = inputs.shape[2]
    position = lax.broadcasted_iota(jnp.int32, (length, 1), 0)
    x = lax.dynamic_index_in_dim(inputs[:, 0], own, 0, keepdims=False).astype(f32)
    og = lax.dynamic_index_in_dim(out_grad[:, 0], own, 0, keepdims=False)
    live = (position < lax.dynamic_index_in_dim(lengths[:, 0], own, 0, keepdims=False)).astype(f32)

    def rows(w):
        return lax.all_gather(w[0], "chan", axis=0, tiled=True)

    def cols(w):
        return lax.all_gather(w[0], "chan", axis=1, tiled=True)

    gain_mix = cols(ln_mix_gain[None])[0].astype(f32)
    gain_mlp = cols(ln_mlp_gain[None])[0].astype(f32)
    taps = cols(short_taps).astype(f32)
    kern = cols(long_taps).astype(f32)
    proj_in, proj_out, proj_up, proj_down = rows(w_in), rows(w_out), rows(w_up), rows(w_down)

    basis = jnp.asarray(odd_basis(length))
    decay = jnp.exp(-decay_rate * position.astype(f32))
    half = length

    def spectrum(v):
        both = dot(basis, v)
        return both[:half], both[half:]

    def back(cos_part, sin_part):
        return dot(basis, jnp.concatenate([cos_part, sin_part], 0).astype(bf16), 0, 0)

    kc, ks = spectrum((kern * decay).astype(bf16))
    kc, ks = kc / length, ks / length
    hat0, inv0 = norm_parts(x)
    normed0 = (hat0 * gain_mix).astype(bf16)
    mixed = dot(normed0, proj_in)
    smooth = taps[0] * mixed + taps[1] * shift_down(mixed, 1) + taps[2] * shift_down(mixed, 2)
    query, key, value = smooth[:, :D], smooth[:, D : 2 * D], smooth[:, 2 * D :]
    sc, ss = spectrum((key * value).astype(bf16))
    conv = back(sc * kc - ss * ks, sc * ks + ss * kc)
    gated = (query * conv).astype(bf16)
    act0 = (live * (x + dot(gated, proj_out))).astype(bf16)
    x1 = act0.astype(f32)
    hat1, inv1 = norm_parts(x1)
    normed1 = (hat1 * gain_mlp).astype(bf16)
    pre = dot(normed1, proj_up)
    cdf = 0.5 * (1.0 + lax.erf(pre * math.sqrt(0.5)))
    hidden = (pre * cdf).astype(bf16)
    act1 = (live * (x1 + dot(hidden, proj_down))).astype(bf16)
    masked1 = live * og.astype(f32)
    branch1 = masked1.astype(bf16)
    g_down = dot(hidden, branch1, 0, 0)
    slope = cdf + pre * (jnp.exp(-0.5 * pre * pre) * (1.0 / math.sqrt(2.0 * math.pi)))
    pre_grad = (slope * dot(branch1, proj_down, 1, 1)).astype(bf16)
    g_up = dot(normed1, pre_grad, 0, 0)
    gn1 = dot(pre_grad, proj_up, 1, 1)
    g_gain_mlp = jnp.sum(gn1 * hat1, axis=0)
    ag1 = masked1 + norm_back(gn1, hat1, inv1, gain_mlp)
    ag1_low = ag1.astype(bf16)
    masked0 = live * ag1_low.astype(f32)
    branch0 = masked0.astype(bf16)
    g_out = dot(gated, branch0, 0, 0)
    grad_gated = dot(branch0, proj_out, 1, 1)
    gc, gs = spectrum((grad_gated * query).astype(bf16))
    g_kern = back(sc * gc + ss * gs, sc * gs - ss * gc) * (decay / length)
    g_sig = back(kc * gc + ks * gs, kc * gs - ks * gc)
    g_smooth = jnp.concatenate([grad_gated * conv, g_sig * value, g_sig * key], 1)
    g_taps = jnp.stack([jnp.sum(g_smooth * shift_down(mixed, n), axis=0) if n else jnp.sum(g_smooth * mixed, axis=0) for n in range(3)])
    g_mixed = (taps[0] * g_smooth + taps[1] * shift_up(g_smooth, 1) + taps[2] * shift_up(g_smooth, 2)).astype(bf16)
    g_in = dot(normed0, g_mixed, 0, 0)
    gn0 = dot(g_mixed, proj_in, 1, 1)
    g_gain_mix = jnp.sum(gn0 * hat0, axis=0)
    ag0 = masked0 + norm_back(gn0, hat0, inv0, gain_mix)

    swap = [(0, 1), (1, 0)]
    first = own == 0

    def exchange(own_first, own_second, dtype):
        keep = jnp.where(first, own_first, own_second).astype(dtype)
        other = lax.ppermute(jnp.where(first, own_second, own_first).astype(bf16), "section", swap).astype(dtype)
        both = jnp.stack([jnp.where(first, keep, other), jnp.where(first, other, keep)])
        return both[None, :, None]

    def reduced(g, dim):
        part = lax.psum_scatter(g.astype(bf16), "chan", scatter_dimension=dim, tiled=True)
        return lax.psum(part, ("section", "dp")).astype(f32)[None]

    return (
        exchange(act0, act1, bf16),
        exchange(ag0, ag1, f32),
        reduced(g_gain_mix, 0),
        reduced(g_in, 0),
        reduced(g_taps, 1),
        reduced(g_kern, 1),
        reduced(g_out, 0),
        reduced(g_gain_mlp, 0),
        reduced(g_up, 0),
        reduced(g_down, 0),
    )


def solution(mesh):
    return jax.shard_map(
        body,
        mesh=mesh,
        in_specs=(
            P(None, ("dp", "chan"), None, None),
            P(None, ("dp", "chan")),
            P(None, ("dp", "chan"), None, None),
            P(None, "chan"),
            P(None, "chan", None),
            P(None, None, "chan"),
            P(None, None, "chan"),
            P(None, "chan", None),
            P(None, "chan"),
            P(None, "chan", None),
            P(None, "chan", None),
        ),
        out_specs=(
            P("section", None, ("dp", "chan"), None, None),
            P("section", None, ("dp", "chan"), None, None),
            P(None, "chan"),
            P(None, "chan", None),
            P(None, None, "chan"),
            P(None, None, "chan"),
            P(None, "chan", None),
            P(None, "chan"),
            P(None, "chan", None),
            P(None, "chan", None),
        ),
        check_vma=False,
    )
```

```python
import math

import jax
import jax.numpy as jnp
import ml_dtypes
import numpy as np
from jax import lax
from jax.experimental import pallas as pl
from jax.experimental.pallas import tpu as pltpu
from jax.sharding import PartitionSpec as P

decay_rate = 0.003
bf16 = jnp.bfloat16
f32 = jnp.float32
MIB = 1 << 20


def odd_basis(length):
    phase = (2 * np.arange(length)[:, None] + 1) * np.arange(length)[None, :] % (4 * length)
    angle = phase * (math.pi / (2 * length))
    return np.concatenate([np.cos(angle), np.sin(angle)], 0).astype(ml_dtypes.bfloat16)


def dot(a, b, ca=1, cb=0):
    return lax.dot_general(a, b, (((ca,), (cb,)), ((), ())), preferred_element_type=f32)


def norm_parts(values):
    centered = values - jnp.mean(values, axis=-1, keepdims=True)
    spread = jnp.mean(centered * centered, axis=-1, keepdims=True)
    inv = lax.rsqrt(spread + 1e-05)
    return centered * inv, inv


def norm_back(grad_normed, hat, inv, gain):
    grad_hat = grad_normed * gain
    return inv * (
        grad_hat
        - jnp.mean(grad_hat, axis=-1, keepdims=True)
        - hat * jnp.mean(grad_hat * hat, axis=-1, keepdims=True)
    )


def call(kernel, grid, in_specs, out_specs, out_shape, scratch, args, flops, nbytes, limit=56, prefetch=0):
    spec = pltpu.PrefetchScalarGridSpec(
        num_scalar_prefetch=prefetch, grid=grid, in_specs=in_specs, out_specs=out_specs, scratch_shapes=scratch
    )
    return pl.pallas_call(
        kernel,
        grid_spec=spec,
        out_shape=out_shape,
        compiler_params=pltpu.CompilerParams(
            dimension_semantics=("arbitrary",) * len(grid), vmem_limit_bytes=limit * MIB
        ),
        cost_estimate=pl.CostEstimate(flops=flops, bytes_accessed=nbytes, transcendentals=0),
    )(*args)


def whole(shape):
    return pl.BlockSpec(shape, lambda *_: (0,) * len(shape), pipeline_mode=pl.Buffered(1))


def rows_of(r, c):
    return pl.BlockSpec((r, c), lambda i, *_: (i, 0))


def cols_of(r, c, start=0):
    return pl.BlockSpec((r, c), lambda i, *_: (0, i + start))


def sds(shape, dtype):
    return jax.ShapeDtypeStruct(shape, dtype)


ANY = pl.BlockSpec(memory_space=pl.ANY)
SHIFTS = (1, 3, 2)


def start_all(copies, sems):
    for n, (a, b) in enumerate(copies):
        pltpu.make_async_copy(a, b, sems.at[n]).start()


def wait_all(copies, sems):
    for n, (a, b) in enumerate(copies):
        pltpu.make_async_copy(a, b, sems.at[n]).wait()


def sources(idx, mine, other):
    z, d, s = idx[0], idx[1], idx[2]
    for e in range(4):
        for j, k in enumerate(SHIFTS):
            for ref, side in ((mine[e], s), (other[e], 1 - s)):
                yield ref, j, lax.rem(z + 4 - k, 4), d ^ e, side


def in_copies(idx, own, mine, other, dst):
    part, half = own.shape[0], own.shape[1] // 2
    r = part // 4
    out = [(own, dst.at[pl.ds(pl.multiple_of(idx[0] * part, 16), part), :])]
    for ref, j, z, d, side in sources(idx, mine, other):
        out.append((ref.at[pl.ds(j * r, r), :],
                    dst.at[pl.ds(pl.multiple_of(z * part + d * r, 16), r), pl.ds(pl.multiple_of(side * half, 128), half)]))
    return out


def mlp_copies(idx, own_up, own_down, mine, other, up, down):
    part, ff = own_up.shape
    width = down.shape[1]
    q = ff // 4
    c = ff // 8
    h = width // 2
    ups = [(own_up, up.at[pl.ds(pl.multiple_of(idx[0] * part, 16), part), :])]
    downs = [(own_down, down.at[pl.ds(pl.multiple_of(idx[0] * q, 16), q), :])]
    for ref, j, z, d, side in sources(idx, mine, other):
        base = j * 2 * part
        ups.append((ref.at[pl.ds(base + part, part), :],
                    up.at[pl.ds(pl.multiple_of(z * part, 16), part), pl.ds(pl.multiple_of(side * 4 * c + d * c, 128), c)]))
        downs.append((ref.at[pl.ds(base, part), :],
                      down.at[pl.ds(pl.multiple_of(z * q + d * part, 16), part), pl.ds(pl.multiple_of(side * h, 128), h)]))
    return ups, downs


def rest_copies(idx, own, mine, other, dst, start, half):
    part = own.shape[0]
    r = part // 4
    out = [(own, dst.at[pl.ds(pl.multiple_of(idx[0] * part, 16), part), :])]
    for ref, j, z, d, side in sources(idx, mine, other):
        out.append((ref.at[pl.ds(j * r, r), pl.ds(start, half)],
                    dst.at[pl.ds(pl.multiple_of(z * part + d * r, 16), r), pl.ds(pl.multiple_of(side * half, 128), half)]))
    return out


SEMS = pltpu.SemaphoreType.DMA((25,))


CH = 256


def spectra_kernel(idx, *refs):
    held, (own_taps, own_small, basis_ref, out_ref, small_ref, taps, small, sig, sems, sems2) = refs[:8], refs[8:]
    mine, other = held[:4], held[4:]
    length = taps.shape[1]

    @pl.when(pl.program_id(0) == 0)
    def _():
        copies = rest_copies(idx, own_taps, mine, other, taps, REST_TAPS, length // 2)
        part = own_small.shape[0]
        r = part // 4
        copies2 = [(own_small, small.at[pl.ds(pl.multiple_of(idx[0] * part, 16), part), :])]
        for e in range(4):
            for j, k in enumerate(SHIFTS):
                z = lax.rem(idx[0] + 4 - k, 4)
                copies2.append((mine[e].at[pl.ds(j * r, r), pl.ds(REST_SMALL, 128)],
                                small.at[pl.ds(pl.multiple_of(z * part + (idx[1] ^ e) * r, 16), r), :]))
        start_all(copies, sems)
        start_all(copies2, sems2)
        wait_all(copies2, sems2)
        wait_all(copies, sems)
        small_ref[...] = small[...].astype(f32).T[0:16]

    position = lax.broadcasted_iota(jnp.int32, (1, length), 1).astype(f32)
    rows = pl.ds(pl.multiple_of(pl.program_id(0) * CH, CH), CH)
    sig[...] = (taps[rows, :].astype(f32) * (jnp.exp(-decay_rate * position) / length)).astype(bf16)
    out_ref[...] = dot(basis_ref[...], sig[...], 1, 1).astype(bf16)


REST_TAPS, REST_SMALL = 384, 896


def kernel_spectra(idx, rest, own_taps, own_small, basis):
    length = own_taps.shape[1]
    width = own_taps.shape[0] * 4
    return call(
        spectra_kernel,
        (width // CH,),
        [ANY] * 10 + [whole(basis.shape)],
        [cols_of(2 * length, CH), pl.BlockSpec((16, width), lambda *_: (0, 0))],
        [sds((2 * length, width), bf16), sds((16, width), f32)],
        [pltpu.VMEM((width, length), bf16), pltpu.VMEM((width, 128), bf16), pltpu.VMEM((CH, length), bf16), SEMS, SEMS],
        (idx, *rest, own_taps, own_small, basis),
        4 * length * length * width,
        basis.size * 2 + 6 * length * width,
        prefetch=1,
    )


def front_kernel(idx, *refs):
    held, (own_ref, x_ref, gain_ref, tq, tk, tv, spec_ref, basis_ref, back_ref,
           normed_ref, mq, mk, mv, sspec_ref, conv_ref, gated_ref, pad, q_s, sig, s_s, y_s, w_s, sems) = refs[:8], refs[8:]
    length, width = x_ref.shape
    R = 256

    @pl.when(pl.program_id(0) == 0)
    def _():
        copies = in_copies(idx, own_ref, held[:4], held[4:], w_s)
        start_all(copies, sems)
        for r in range(0, length, R):
            hat, _ = norm_parts(x_ref[r : r + R].astype(f32))
            normed_ref[r : r + R] = (hat * gain_ref[...]).astype(bf16)
        pad[0:8] = jnp.zeros((8, 3 * CH), f32)
        wait_all(copies, sems)

    cols = [pl.ds(pl.multiple_of(p * width + pl.program_id(0) * CH, CH), CH) for p in range(3)]
    pad[8:] = dot(normed_ref[...], jnp.concatenate([w_s[:, c] for c in cols], 1))
    for r in range(0, length, R):
        now = []
        for p, (t, m) in enumerate(((tq, mq), (tk, mk), (tv, mv))):
            c = slice(p * CH, (p + 1) * CH)
            m[r : r + R] = pad[8 + r : 8 + r + R, c].astype(bf16)
            now.append(t[0:1] * pad[8 + r : 8 + r + R, c] + t[1:2] * pad[7 + r : 7 + r + R, c] + t[2:3] * pad[6 + r : 6 + r + R, c])
        q_s[r : r + R] = now[0]
        sig[r : r + R] = (now[1] * now[2]).astype(bf16)
    s_s[...] = dot(basis_ref[...], sig[...])
    for r in range(0, length, R):
        at, lo = slice(r, r + R), slice(length + r, length + r + R)
        sc, ss = s_s[at], s_s[lo]
        sspec_ref[at] = sc.astype(bf16)
        sspec_ref[lo] = ss.astype(bf16)
        kc, ks = spec_ref[at].astype(f32), spec_ref[lo].astype(f32)
        y_s[at] = (sc * kc - ss * ks).astype(bf16)
        y_s[lo] = (sc * ks + ss * kc).astype(bf16)
    conv = dot(back_ref[...], y_s[...])
    conv_ref[...] = conv.astype(bf16)
    gated_ref[...] = (q_s[...] * conv).astype(bf16)


def mixer_front(idx, held, own_in, x, gain, taps, spec, basis, back):
    length, width = x.shape[1:]
    nb = width // CH
    block = cols_of(length, CH)
    full = sds((length, width), bf16)
    return call(
        front_kernel,
        (nb,),
        [ANY] * 9 + [pl.BlockSpec((None, length, width), lambda i, idx: (idx[2], 0, 0)), whole((1, width))]
        + [cols_of(3, CH, p * nb) for p in range(3)]
        + [cols_of(2 * length, CH), whole(basis.shape), whole(back.shape)],
        [whole((length, width)), block, block, block, cols_of(2 * length, CH), block, block],
        [full, full, full, full, sds((2 * length, width), bf16), full, full],
        [pltpu.VMEM((length + 8, 3 * CH), f32), pltpu.VMEM((length, CH), f32), pltpu.VMEM((length, CH), bf16),
         pltpu.VMEM((2 * length, CH), f32), pltpu.VMEM((2 * length, CH), bf16), pltpu.VMEM((width, 3 * width), bf16), SEMS],
        (idx, *held, own_in, x, gain, taps, taps, taps, spec, basis, back),
        6 * length * width * width + 8 * length * length * width,
        2 * (10 * length * width + 3 * width * width + 2 * basis.size),
        prefetch=1,
    )


def gelu_parts(pre):
    cdf = 0.5 * (1.0 + lax.erf(pre * math.sqrt(0.5)))
    slope = cdf + pre * (jnp.exp(-0.5 * pre * pre) * (1.0 / math.sqrt(2.0 * math.pi)))
    return pre * cdf, slope


def live_rows(idx, rows):
    return (lax.broadcasted_iota(jnp.int32, (rows, 1), 0) < idx[3]).astype(f32)


def near_first(idx, ref, half):
    return (pl.ds(pl.multiple_of(idx[2] * half, 128), half), pl.ds(pl.multiple_of((1 - idx[2]) * half, 128), half))


def mlp_kernel(idx, *refs):
    rest, held, (own_out, own_up, own_down, x_ref, gated_ref, og_ref, gain_ref,
                 act0_ref, act1_ref, normed_ref, slope_ref, near_ref, away_ref,
                 wo_ref, wu_ref, wd_ref, acc, turned, sem_o, sem_u, sem_d) = refs[:8], refs[8:16], refs[16:]
    length, width = x_ref.shape
    half = width // 2
    c = pl.program_id(0)
    live = live_rows(idx, length)

    @pl.when(c == 0)
    def _():
        outs = rest_copies(idx, own_out, rest[:4], rest[4:], wo_ref, 0, half)
        ups, downs = mlp_copies(idx, own_up, own_down, held[:4], held[4:], wu_ref, wd_ref)
        start_all(outs, sem_o)
        start_all(ups, sem_u)
        start_all(downs, sem_d)
        for n, cols in enumerate(near_first(idx, og_ref, half)):
            turned[:, n * half : (n + 1) * half] = (live * og_ref[:, cols].astype(f32)).astype(bf16)
        wait_all(outs, sem_o)
        act0 = (live * (x_ref[...].astype(f32) + dot(gated_ref[...], wo_ref[...]))).astype(bf16)
        act0_ref[...] = act0
        x1 = act0.astype(f32)
        hat, _ = norm_parts(x1)
        normed_ref[...] = (hat * gain_ref[...]).astype(bf16)
        acc[...] = x1
        wait_all(ups, sem_u)
        wait_all(downs, sem_d)

    at = pl.ds(pl.multiple_of(c * width, width), width)
    hid, slope = gelu_parts(dot(normed_ref[...], wu_ref[:, at]))
    hid = hid.astype(bf16)
    slope_ref[...] = slope.astype(bf16)
    acc[...] += dot(hid, wd_ref[at, :])
    grad = dot(hid, turned[...], 0, 0).astype(bf16)
    near_ref[...] = grad[:, :half]
    away_ref[...] = grad[:, half:]

    @pl.when(c == pl.num_programs(0) - 1)
    def _():
        act1_ref[...] = (live * acc[...]).astype(bf16)


def mlp_forward(idx, rest, held, own_out, own_up, own_down, x, gated, og, gain):
    length, width = gated.shape
    ff = own_up.shape[1]
    half = width // 2
    full = sds((length, width), bf16)
    picked = pl.BlockSpec((None, length, width), lambda i, idx: (idx[2], 0, 0), pipeline_mode=pl.Buffered(1))
    return call(
        mlp_kernel,
        (ff // width,),
        [ANY] * 19 + [picked, whole((length, width)), picked, whole(gain.shape)],
        [whole((length, width))] * 3 + [cols_of(length, width), rows_of(width, half), rows_of(width, half)],
        [full, full, full, sds((length, ff), bf16), sds((ff, half), bf16), sds((ff, half), bf16)],
        [pltpu.VMEM((width, width), bf16), pltpu.VMEM((width, ff), bf16), pltpu.VMEM((ff, width), bf16),
         pltpu.VMEM((length, width), f32), pltpu.VMEM((length, width), bf16), SEMS, SEMS, SEMS],
        (idx, *rest, *held, own_out, own_up, own_down, x, gated, og, gain),
        2 * length * width * (width + 3 * ff),
        2 * (5 * length * width + 3 * width * ff + 2 * length * ff),
        prefetch=1,
    )


def mlp_back_kernel(idx, *refs):
    held, (own_up, own_down, og_ref, act0_ref, normed_ref, slope_ref, gain_ref,
           ag_ref, branch_ref, gg_ref, near_ref, away_ref,
           wu_ref, wd_ref, gn, branch, turned, sem_u, sem_d) = refs[:8], refs[8:]
    length, width = og_ref.shape
    half = width // 2
    c = pl.program_id(0)
    live = live_rows(idx, length)

    @pl.when(c == 0)
    def _():
        ups, downs = mlp_copies(idx, own_up, own_down, held[:4], held[4:], wu_ref, wd_ref)
        start_all(downs, sem_d)
        start_all(ups, sem_u)
        branch[...] = (live * og_ref[...].astype(f32)).astype(bf16)
        gn[...] = jnp.zeros((length, width), f32)
        wait_all(downs, sem_d)
        wait_all(ups, sem_u)

    at = pl.ds(pl.multiple_of(c * width, width), width)
    pre = (slope_ref[...].astype(f32) * dot(branch[...], wd_ref[at, :], 1, 1)).astype(bf16)
    for n, cols in enumerate(near_first(idx, turned, half)):
        turned[:, cols] = pre[:, n * half : (n + 1) * half]
    gn[...] += dot(pre, wu_ref[:, at], 1, 1)
    grad = dot(normed_ref[...], turned[...], 0, 0).astype(bf16)
    near_ref[...] = grad[:, :half]
    away_ref[...] = grad[:, half:]

    @pl.when(c == pl.num_programs(0) - 1)
    def _():
        hat, inv = norm_parts(act0_ref[...].astype(f32))
        gg_ref[...] = jnp.sum(gn[...] * hat, axis=0, keepdims=True)
        ag = live * og_ref[...].astype(f32) + norm_back(gn[...], hat, inv, gain_ref[...])
        ag_ref[...] = ag
        branch_ref[...] = (live * ag).astype(bf16)


def mlp_backward(idx, held, own_up, own_down, og, act0, normed, slope, gain):
    length, width = act0.shape
    ff = own_up.shape[1]
    half = width // 2
    picked = pl.BlockSpec((None, length, width), lambda i, idx: (idx[2], 0, 0), pipeline_mode=pl.Buffered(1))
    one = whole((length, width))
    return call(
        mlp_back_kernel,
        (ff // width,),
        [ANY] * 10 + [picked, one, one, cols_of(length, width), whole(gain.shape)],
        [one, one, whole((1, width)), cols_of(width, half), cols_of(width, half)],
        [sds((length, width), f32), sds((length, width), bf16), sds((1, width), f32),
         sds((width, ff // 2), bf16), sds((width, ff // 2), bf16)],
        [pltpu.VMEM((width, ff), bf16), pltpu.VMEM((ff, width), bf16), pltpu.VMEM((length, width), f32),
         pltpu.VMEM((length, width), bf16), pltpu.VMEM((length, width), bf16), SEMS, SEMS],
        (idx, *held, own_up, own_down, og, act0, normed, slope, gain),
        6 * length * width * ff,
        2 * (6 * length * width + 3 * width * ff + length * ff),
        prefetch=1,
    )


def conv_back_kernel(idx, *refs):
    rest, (own_out, branch_ref, normed_ref, gated_ref, mq, mk, mv, tq, tk, tv, conv_ref, spec_ref, sspec_ref, basis_ref, back_ref,
           g_ref, near_ref, away_ref, gtaps_ref, pad, gpad, smooth, sig, s_s, y_s, gm, turned, kern, w_s, sems) = refs[:8], refs[8:]
    length, width = branch_ref.shape
    half = width // 2
    hl = length // 2
    R = 256
    i = pl.program_id(0)
    mine, other = near_first(idx, turned, half)

    @pl.when(i == 0)
    def _():
        copies = rest_copies(idx, own_out, rest[:4], rest[4:], w_s, 0, half)
        start_all(copies, sems)
        pad[0:8] = jnp.zeros((8, 3 * CH), f32)
        gpad[length : length + 8] = jnp.zeros((8, 3 * CH), f32)
        turned[:, :half] = branch_ref[:, mine]
        turned[:, half:] = branch_ref[:, other]
        wait_all(copies, sems)

    rows = pl.ds(pl.multiple_of(i * CH, CH), CH)
    for p, m in enumerate((mq, mk, mv)):
        pad[8:, p * CH : (p + 1) * CH] = m[...].astype(f32)
    gg = dot(branch_ref[...], w_s[rows, :], 1, 1)
    gpad[0:length, 0:CH] = gg * conv_ref[...].astype(f32)
    s_s[0:length] = gg
    for r in range(0, length, R):
        for p, t in enumerate((tq, tk, tv)):
            c = slice(p * CH, (p + 1) * CH)
            now = t[0:1] * pad[8 + r : 8 + r + R, c] + t[1:2] * pad[7 + r : 7 + r + R, c] + t[2:3] * pad[6 + r : 6 + r + R, c]
            if p == 0:
                sig[r : r + R] = (s_s[r : r + R] * now).astype(bf16)
            else:
                smooth[r : r + R, (p - 1) * CH : p * CH] = now
    s_s[...] = dot(basis_ref[...], sig[...])
    for r in range(0, length, R):
        at, lo = slice(r, r + R), slice(length + r, length + r + R)
        gc, gs = s_s[at], s_s[lo]
        kc, ks = spec_ref[at].astype(f32), spec_ref[lo].astype(f32)
        y_s[at, 0:CH] = (kc * gc + ks * gs).astype(bf16)
        y_s[lo, 0:CH] = (kc * gs - ks * gc).astype(bf16)
        sc, ss = sspec_ref[at].astype(f32), sspec_ref[lo].astype(f32)
        y_s[at, CH:] = (sc * gc + ss * gs).astype(bf16)
        y_s[lo, CH:] = (sc * gs - ss * gc).astype(bf16)
    both = dot(back_ref[...], y_s[...])
    gpad[0:length, CH : 2 * CH] = both[:, :CH] * smooth[:, CH:]
    gpad[0:length, 2 * CH :] = both[:, :CH] * smooth[:, :CH]
    position = lax.broadcasted_iota(jnp.int32, (length, 1), 0).astype(f32)
    kern[...] = (both[:, CH:] * (jnp.exp(-decay_rate * position) / length)).T.astype(bf16)
    sums = [[jnp.zeros((1, CH), f32)] * 3 for _ in range(3)]
    for r in range(0, length, R):
        for p, t in enumerate((tq, tk, tv)):
            c = slice(p * CH, (p + 1) * CH)
            g0 = gpad[r : r + R, c]
            g = (t[0:1] * g0 + t[1:2] * gpad[r + 1 : r + 1 + R, c] + t[2:3] * gpad[r + 2 : r + 2 + R, c]).astype(bf16)
            g_ref[p, r : r + R] = g
            for n in range(2):
                at = jnp.where(idx[2] == n, 0, half) + p * (CH // 2)
                gm[r : r + R, pl.ds(pl.multiple_of(at, 128), CH // 2)] = g[:, n * (CH // 2) : (n + 1) * (CH // 2)]
            sums[p] = [sums[p][n] + jnp.sum(g0 * pad[8 - n + r : 8 - n + r + R, c], axis=0, keepdims=True) for n in range(3)]
    for p in range(3):
        for n in range(3):
            gtaps_ref[3 * p + n : 3 * p + n + 1] = sums[p][n]
    g_in = dot(normed_ref[...], gm[...], 0, 0).astype(bf16)
    cols = pl.ds(pl.multiple_of(i * half, 128), half)
    near_ref[:, cols] = g_in[:, :half]
    away_ref[:, cols] = g_in[:, half:]
    g_out = dot(gated_ref[...], turned[...], 0, 0).astype(bf16)
    near_ref[rows, 3 * half : 4 * half] = g_out[:, :half]
    away_ref[rows, 3 * half : 4 * half] = g_out[:, half:]
    near_ref[rows, 4 * half :] = kern[:, pl.ds(pl.multiple_of(idx[2] * hl, 128), hl)]
    away_ref[rows, 4 * half :] = kern[:, pl.ds(pl.multiple_of((1 - idx[2]) * hl, 128), hl)]


def conv_backward(idx, rest, own_out, branch, normed, gated, mixed, taps, conv, spec, sspec, basis, back):
    length, width = branch.shape
    nb = width // CH
    block = cols_of(length, CH)
    tall = cols_of(2 * length, CH)
    mix = (width, 2 * width + length // 2)
    wide = pltpu.VMEM((length + 8, 3 * CH), f32)
    return call(
        conv_back_kernel,
        (nb,),
        [ANY] * 9 + [whole(branch.shape), whole(branch.shape), block, block, block, block]
        + [cols_of(3, CH, p * nb) for p in range(3)]
        + [block, tall, tall, whole(basis.shape), whole(back.shape)],
        [pl.BlockSpec((3, length, CH), lambda i, *_: (0, 0, i)), whole(mix), whole(mix), cols_of(9, CH)],
        [sds((3, length, width), bf16), sds(mix, bf16), sds(mix, bf16), sds((9, width), f32)],
        [wide, wide, pltpu.VMEM((length, 2 * CH), f32), pltpu.VMEM((length, CH), bf16), pltpu.VMEM((2 * length, CH), f32),
         pltpu.VMEM((2 * length, 2 * CH), bf16), pltpu.VMEM((length, 3 * CH), bf16), pltpu.VMEM((length, width), bf16),
         pltpu.VMEM((CH, length), bf16), pltpu.VMEM((width, width), bf16), SEMS],
        (idx, *rest, own_out, branch, normed, gated, *mixed, taps, taps, taps, conv, spec, sspec, basis, back),
        10 * length * width * width + 12 * length * length * width,
        2 * (14 * branch.size + 2 * basis.size + 2 * mix[0] * mix[1]),
        prefetch=1,
    )


def norm_back_kernel(idx, *refs):
    held, (own_ref, g_ref, x_ref, masked_ref, gain_ref, ag_ref, gg_ref, wi_ref, sems) = refs[:8], refs[8:]
    width = x_ref.shape[1]

    @pl.when(pl.program_id(0) == 0)
    def _():
        copies = in_copies(idx, own_ref, held[:4], held[4:], wi_ref)
        start_all(copies, sems)
        wait_all(copies, sems)

    gn = dot(jnp.concatenate([g_ref[p] for p in range(3)], 1), wi_ref[...], 1, 1)
    hat, inv = norm_parts(x_ref[...].astype(f32))
    part = jnp.sum(gn * hat, axis=0, keepdims=True)

    @pl.when(pl.program_id(0) == 0)
    def _():
        gg_ref[...] = part

    @pl.when(pl.program_id(0) > 0)
    def _():
        gg_ref[...] += part

    ag_ref[...] = masked_ref[...].astype(f32) + norm_back(gn, hat, inv, gain_ref[...])


def input_backward(idx, held, own_in, g_mixed, x, masked, gain):
    length, width = masked.shape
    R = 512
    blk = rows_of(R, width)
    return call(
        norm_back_kernel,
        (length // R,),
        [ANY] * 9 + [pl.BlockSpec((3, R, width), lambda i, *_: (0, i, 0)),
                     pl.BlockSpec((None, R, width), lambda i, idx: (idx[2], i, 0)), blk, whole(gain.shape)],
        [blk, pl.BlockSpec((1, width), lambda *_: (0, 0))],
        [sds((length, width), f32), sds((1, width), f32)],
        [pltpu.VMEM((width, 3 * width), bf16), SEMS],
        (idx, *held, own_in, g_mixed, x, masked, gain),
        6 * length * width * width,
        2 * (7 * length * width + 3 * width * width),
        prefetch=1,
    )


def unpack_mlp_kernel(idx, *refs):
    held, (up, down) = refs[:8], refs[8:]
    part = up.shape[0]
    q = up.shape[1] // 4
    h = down.shape[1] // 2
    for e in range(4):
        d = idx[1] ^ e
        for ref, side in ((held[e], idx[2]), (held[4 + e], 1 - idx[2])):
            down[pl.ds(pl.multiple_of(d * part, 16), part), pl.ds(pl.multiple_of(side * h, 128), h)] = ref[0:part].astype(f32)
            up[:, pl.ds(pl.multiple_of(d * q + side * h, 128), h)] = ref[part : 2 * part].astype(f32)


def unpack_mix_kernel(idx, *refs):
    held, (g_in, g_out, g_kern) = refs[:8], refs[8:]
    part, width = g_out.shape
    length = g_kern.shape[1]
    r = part // 4
    h = width // 2
    b = CH // 2
    for e in range(4):
        at = pl.ds(pl.multiple_of((idx[1] ^ e) * r, 16), r)
        for ref, side in ((held[e], idx[2]), (held[4 + e], 1 - idx[2])):
            for i in range(width // CH):
                for p in range(3):
                    c = i * h + p * b
                    g_in[at, pl.ds(pl.multiple_of(p * width + i * CH + side * b, 128), b)] = ref[:, c : c + b].astype(f32)
            g_out[at, pl.ds(pl.multiple_of(side * h, 128), h)] = ref[:, 3 * h : 4 * h].astype(f32)
            g_kern[at, pl.ds(pl.multiple_of(side * (length // 2), 128), length // 2)] = ref[:, 4 * h : 4 * h + length // 2].astype(f32)


def unpack(kernel, idx, held, shapes):
    return call(
        kernel,
        (1,),
        [whole(h.shape) for h in held],
        [whole(s) for s in shapes],
        [sds(s, f32) for s in shapes],
        [],
        (idx, *held),
        0,
        sum(6 * math.prod(s) for s in shapes),
        prefetch=1,
    )


SWAP = [(0, 1), (1, 0)]


def shift(k):
    return [(i, (i + k) % 4) for i in range(4)]


def flip(e):
    return [(i, i ^ e) for i in range(4)]


def tie(value, *others):
    return lax.optimization_barrier((value, *others))[0]


def over_line(piece):
    return jnp.concatenate([lax.ppermute(piece, "chan", shift(k)) for k in SHIFTS], 0)


def over_plane(near):
    return [near] + [lax.ppermute(near, "dp", flip(e)) for e in (1, 2, 3)]


def over_chip(mine):
    return mine + [lax.ppermute(m, "section", SWAP) for m in mine]


def total(parts):
    out = parts[0].astype(f32)
    for p in parts[1:]:
        out += p.astype(f32)
    return out.astype(bf16)


def fold_plane(parts):
    return total([parts[0]] + [lax.ppermute(parts[e], "dp", flip(e)) for e in (1, 2, 3)])


def fold_line(held, z):
    def at(k):
        return lax.dynamic_index_in_dim(held, (z + k) % 4, 0, keepdims=False)

    return total([at(0)] + [lax.ppermute(at(k), "chan", shift(k)) for k in SHIFTS])


def cut(v, at, size, axis):
    return lax.dynamic_slice_in_dim(v, at, size, axis)


def fast_body(inputs, lengths, out_grad, ln_mix_gain, w_in, short_taps, long_taps, w_out, ln_mlp_gain, w_up, w_down):
    z, d, s = lax.axis_index("chan"), lax.axis_index("dp"), lax.axis_index("section")
    length = inputs.shape[2]
    width = inputs.shape[3]
    part = w_in.shape[1]
    ff = w_up.shape[2]
    half = width // 2
    hl = length // 2
    r = part // 4
    count = lax.dynamic_index_in_dim(lengths[:, 0], s, 0, keepdims=False)
    idx = jnp.stack([z, d, s, count]).astype(jnp.int32)
    x, og = inputs[:, 0], out_grad[:, 0]
    table = odd_basis(length)
    basis, back = jnp.asarray(table), jnp.asarray(np.ascontiguousarray(table.T))
    first = s == 0

    def after(parts, values):
        return lax.optimization_barrier((list(parts), list(values)))

    own_in, own_out, own_up, own_down = w_in[0], w_out[0], w_up[0], w_down[0]
    piece_mlp = jnp.concatenate(
        [cut(cut(own_down, d * part, part, 0), s * half, half, 1), cut(own_up, s * (ff // 2) + d * (ff // 8), ff // 8, 1)], 0
    )
    line_mlp = lax.all_gather(piece_mlp, "chan", axis=0)
    own_taps = long_taps[0].T
    small = jnp.concatenate([ln_mix_gain, ln_mlp_gain, short_taps[0].reshape(9, part)], 0)
    own_small = jnp.pad(small.T, ((0, 0), (0, 128 - 11)))
    piece = jnp.concatenate([cut(own_out, s * half, half, 1), cut(own_taps, s * hl, hl, 1), own_small], 1)
    piece_rest = cut(piece, d * r, r, 0)
    piece_in = cut(cut(own_in, d * r, r, 0), s * 3 * half, 3 * half, 1)
    near_rest = over_line(piece_rest)
    near_in = over_line(piece_in)
    plane_rest = over_plane(near_rest)
    near_in = tie(near_in, near_rest)
    plane_in = over_plane(near_in)
    held_rest = over_chip(plane_rest)

    plane_in, (spec, small) = after(plane_in, kernel_spectra(idx, held_rest, own_taps, own_small, basis))
    held_in = over_chip(plane_in)
    gain_mix, gain_mlp = small[0:1], small[1:2]
    taps = small[2:11].reshape(3, 3, 4, part).transpose(0, 2, 1, 3).reshape(3, 3 * width)
    near_mlp = jnp.concatenate([lax.dynamic_index_in_dim(line_mlp, (z + 4 - k) % 4, 0, keepdims=False) for k in SHIFTS], 0)
    plane_mlp = over_plane(near_mlp)
    plane_mlp, (normed0, mq, mk, mv, sspec, conv, gated) = after(
        plane_mlp, mixer_front(idx, held_in, own_in, x, gain_mix, taps, tie(spec, near_mlp), basis, back)
    )
    held_mlp = over_chip(plane_mlp)
    act0, act1, normed1, slope, near, away = mlp_forward(
        idx, held_rest, held_mlp, own_out, own_up, own_down, x, gated, og, gain_mlp
    )

    def both_cores(near, away):
        return total([near, lax.ppermute(away, "section", SWAP)])

    def exchange(own_first, own_second, dtype):
        keep = jnp.where(first, own_first, own_second).astype(dtype)
        other = lax.ppermute(jnp.where(first, own_second, own_first).astype(bf16), "section", SWAP).astype(dtype)
        both = jnp.stack([jnp.where(first, keep, other), jnp.where(first, other, keep)])
        return both[None, :, None]

    def to_plane(parts):
        return [parts[0]] + [lax.ppermute(parts[e], "dp", flip(e)) for e in (1, 2, 3)]

    def line_sum(held):
        return lax.psum_scatter(held, "chan", scatter_dimension=0, tiled=False)

    h_down = both_cores(near, away).reshape(4, 4, part, half)
    sent_down = [lax.dynamic_index_in_dim(h_down, d ^ e, 1, keepdims=False) for e in range(4)]
    got_down = to_plane(sent_down)
    got_down, (ag1, branch0, g_gain_mlp, near, away) = after(
        got_down, mlp_backward(idx, held_mlp, own_up, own_down, og, act0, normed1, tie(slope, *sent_down), gain_mlp)
    )
    p_down = line_sum(total(got_down))
    h_up = both_cores(near, away).reshape(4, part, ff // 2)
    sent_up = [cut(h_up, (d ^ e) * half, half, 2) for e in range(4)]
    got_up = to_plane(sent_up)

    branch_late = tie(branch0, *sent_up)
    got_up, (g_mixed, near, away, g_taps) = after(
        got_up,
        conv_backward(idx, held_rest, own_out, branch_late, normed0, gated, (mq, mk, mv), taps, conv, spec, sspec, basis, back),
    )
    p_up = line_sum(total(got_up))
    h_mix = both_cores(near, away).reshape(4, 4, r, 2 * width + hl)
    sent_mix = [lax.dynamic_index_in_dim(h_mix, d ^ e, 1, keepdims=False) for e in range(4)]
    got_mix = to_plane(sent_mix)
    got_mix, (ag0, g_gain_mix) = after(
        got_mix, input_backward(idx, held_in, own_in, tie(g_mixed, *sent_mix), x, branch0, gain_mix)
    )
    p_mix = fold_line(total(got_mix), z)
    g_in, g_out, g_kern = unpack(
        unpack_mix_kernel, idx, over_chip(over_plane(p_mix)), [(part, 3 * width), (part, width), (part, length)]
    )
    p_mlp = jnp.concatenate([p_down, p_up], 0)
    g_up, g_down = unpack(unpack_mlp_kernel, idx, over_chip(over_plane(p_mlp)), [(part, ff), (4 * part, width)])

    tiny = jnp.concatenate([g_gain_mix, g_gain_mlp, g_taps], 0)
    tiny += lax.ppermute(tiny, "section", SWAP)
    for axis in ("dp", "chan"):
        for e in (1, 2):
            tiny += lax.ppermute(tiny, axis, flip(e))
    mine = cut(tiny[0:2], z * part, part, 1)
    g_taps = tiny[2:11].reshape(3, 3, width).transpose(1, 0, 2).reshape(3, 3 * width)
    g_taps = cut(g_taps, z * 3 * part, 3 * part, 1)

    return (
        exchange(act0, act1, bf16),
        exchange(ag0, ag1, f32),
        mine[0:1],
        g_in[None],
        g_taps[None],
        g_kern.T[None],
        g_out[None],
        mine[1:2],
        g_up[None],
        g_down[None],
    )


def fits(mesh):
    return mesh.shape["chan"] == 4 and mesh.shape["dp"] == 4 and mesh.shape["section"] == 2


def shift_down(v, n):
    return jnp.pad(v, ((n, 0), (0, 0)))[: v.shape[0]]


def shift_up(v, n):
    return jnp.pad(v, ((0, n), (0, 0)))[n:]


def plain_body(inputs, lengths, out_grad, ln_mix_gain, w_in, short_taps, long_taps, w_out, ln_mlp_gain, w_up, w_down):
    own = lax.axis_index("section")
    length, width = inputs.shape[2:]
    position = lax.broadcasted_iota(jnp.int32, (length, 1), 0)
    x = lax.dynamic_index_in_dim(inputs[:, 0], own, 0, keepdims=False).astype(f32)
    og = lax.dynamic_index_in_dim(out_grad[:, 0], own, 0, keepdims=False)
    live = (position < lax.dynamic_index_in_dim(lengths[:, 0], own, 0, keepdims=False)).astype(f32)

    def rows(w):
        return lax.all_gather(w[0], "chan", axis=0, tiled=True)

    def cols(w):
        return lax.all_gather(w[0], "chan", axis=1, tiled=True)

    gain_mix = cols(ln_mix_gain[None])[0].astype(f32)
    gain_mlp = cols(ln_mlp_gain[None])[0].astype(f32)
    taps = cols(short_taps).astype(f32)
    kern = cols(long_taps).astype(f32)
    proj_in, proj_out, proj_up, proj_down = rows(w_in), rows(w_out), rows(w_up), rows(w_down)

    basis = jnp.asarray(odd_basis(length))
    decay = jnp.exp(-decay_rate * position.astype(f32))
    half = length

    def spectrum(v):
        both = dot(basis, v)
        return both[:half], both[half:]

    def back(cos_part, sin_part):
        return dot(basis, jnp.concatenate([cos_part, sin_part], 0).astype(bf16), 0, 0)

    kc, ks = spectrum((kern * decay).astype(bf16))
    kc, ks = kc / length, ks / length
    hat0, inv0 = norm_parts(x)
    normed0 = (hat0 * gain_mix).astype(bf16)
    mixed = dot(normed0, proj_in)
    smooth = taps[0] * mixed + taps[1] * shift_down(mixed, 1) + taps[2] * shift_down(mixed, 2)
    query, key, value = smooth[:, :width], smooth[:, width : 2 * width], smooth[:, 2 * width :]
    sc, ss = spectrum((key * value).astype(bf16))
    conv = back(sc * kc - ss * ks, sc * ks + ss * kc)
    gated = (query * conv).astype(bf16)
    act0 = (live * (x + dot(gated, proj_out))).astype(bf16)
    x1 = act0.astype(f32)
    hat1, inv1 = norm_parts(x1)
    normed1 = (hat1 * gain_mlp).astype(bf16)
    pre = dot(normed1, proj_up)
    cdf = 0.5 * (1.0 + lax.erf(pre * math.sqrt(0.5)))
    hidden = (pre * cdf).astype(bf16)
    act1 = (live * (x1 + dot(hidden, proj_down))).astype(bf16)
    masked1 = live * og.astype(f32)
    branch1 = masked1.astype(bf16)
    g_down = dot(hidden, branch1, 0, 0)
    slope = cdf + pre * (jnp.exp(-0.5 * pre * pre) * (1.0 / math.sqrt(2.0 * math.pi)))
    pre_grad = (slope * dot(branch1, proj_down, 1, 1)).astype(bf16)
    g_up = dot(normed1, pre_grad, 0, 0)
    gn1 = dot(pre_grad, proj_up, 1, 1)
    g_gain_mlp = jnp.sum(gn1 * hat1, axis=0)
    ag1 = masked1 + norm_back(gn1, hat1, inv1, gain_mlp)
    ag1_low = ag1.astype(bf16)
    masked0 = live * ag1_low.astype(f32)
    branch0 = masked0.astype(bf16)
    g_out = dot(gated, branch0, 0, 0)
    grad_gated = dot(branch0, proj_out, 1, 1)
    gc, gs = spectrum((grad_gated * query).astype(bf16))
    g_kern = back(sc * gc + ss * gs, sc * gs - ss * gc) * (decay / length)
    g_sig = back(kc * gc + ks * gs, kc * gs - ks * gc)
    g_smooth = jnp.concatenate([grad_gated * conv, g_sig * value, g_sig * key], 1)
    g_taps = jnp.stack([jnp.sum(g_smooth * shift_down(mixed, n), axis=0) if n else jnp.sum(g_smooth * mixed, axis=0) for n in range(3)])
    g_mixed = (taps[0] * g_smooth + taps[1] * shift_up(g_smooth, 1) + taps[2] * shift_up(g_smooth, 2)).astype(bf16)
    g_in = dot(normed0, g_mixed, 0, 0)
    gn0 = dot(g_mixed, proj_in, 1, 1)
    g_gain_mix = jnp.sum(gn0 * hat0, axis=0)
    ag0 = masked0 + norm_back(gn0, hat0, inv0, gain_mix)

    swap = [(0, 1), (1, 0)]
    first = own == 0

    def exchange(own_first, own_second, dtype):
        keep = jnp.where(first, own_first, own_second).astype(dtype)
        other = lax.ppermute(jnp.where(first, own_second, own_first).astype(bf16), "section", swap).astype(dtype)
        both = jnp.stack([jnp.where(first, keep, other), jnp.where(first, other, keep)])
        return both[None, :, None]

    def reduced(g, dim):
        part = lax.psum_scatter(g.astype(bf16), "chan", scatter_dimension=dim, tiled=True)
        return lax.psum(part, ("section", "dp")).astype(f32)[None]

    return (
        exchange(act0, act1, bf16),
        exchange(ag0, ag1, f32),
        reduced(g_gain_mix, 0),
        reduced(g_in, 0),
        reduced(g_taps, 1),
        reduced(g_kern, 1),
        reduced(g_out, 0),
        reduced(g_gain_mlp, 0),
        reduced(g_up, 0),
        reduced(g_down, 0),
    )


def solution(mesh):
    return jax.shard_map(
        fast_body if fits(mesh) else plain_body,
        mesh=mesh,
        in_specs=(
            P(None, ("dp", "chan"), None, None),
            P(None, ("dp", "chan")),
            P(None, ("dp", "chan"), None, None),
            P(None, "chan"),
            P(None, "chan", None),
            P(None, None, "chan"),
            P(None, None, "chan"),
            P(None, "chan", None),
            P(None, "chan"),
            P(None, "chan", None),
            P(None, "chan", None),
        ),
        out_specs=(
            P("section", None, ("dp", "chan"), None, None),
            P("section", None, ("dp", "chan"), None, None),
            P(None, "chan"),
            P(None, "chan", None),
            P(None, None, "chan"),
            P(None, None, "chan"),
            P(None, "chan", None),
            P(None, "chan"),
            P(None, "chan", None),
            P(None, "chan", None),
        ),
        check_vma=False,
    )
```

```python
import math

import jax
import jax.numpy as jnp
import ml_dtypes
import numpy as np
from jax import lax
from jax.experimental import pallas as pl
from jax.experimental.pallas import tpu as pltpu
from jax.sharding import PartitionSpec as P

decay_rate = 0.003
bf16 = jnp.bfloat16
f32 = jnp.float32
MIB = 1 << 20


def odd_basis(length):
    phase = (2 * np.arange(length)[:, None] + 1) * np.arange(length)[None, :] % (4 * length)
    angle = phase * (math.pi / (2 * length))
    return np.concatenate([np.cos(angle), np.sin(angle)], 0).astype(ml_dtypes.bfloat16)


def dot(a, b, ca=1, cb=0):
    return lax.dot_general(a, b, (((ca,), (cb,)), ((), ())), preferred_element_type=f32)


def norm_parts(values):
    centered = values - jnp.mean(values, axis=-1, keepdims=True)
    spread = jnp.mean(centered * centered, axis=-1, keepdims=True)
    inv = lax.rsqrt(spread + 1e-05)
    return centered * inv, inv


def norm_back(grad_normed, hat, inv, gain):
    grad_hat = grad_normed * gain
    return inv * (
        grad_hat
        - jnp.mean(grad_hat, axis=-1, keepdims=True)
        - hat * jnp.mean(grad_hat * hat, axis=-1, keepdims=True)
    )


def call(kernel, grid, in_specs, out_specs, out_shape, scratch, args, flops, nbytes, limit=56, prefetch=0):
    spec = pltpu.PrefetchScalarGridSpec(
        num_scalar_prefetch=prefetch, grid=grid, in_specs=in_specs, out_specs=out_specs, scratch_shapes=scratch
    )
    return pl.pallas_call(
        kernel,
        grid_spec=spec,
        out_shape=out_shape,
        compiler_params=pltpu.CompilerParams(
            dimension_semantics=("arbitrary",) * len(grid), vmem_limit_bytes=limit * MIB
        ),
        cost_estimate=pl.CostEstimate(flops=flops, bytes_accessed=nbytes, transcendentals=0),
    )(*args)


def whole(shape):
    return pl.BlockSpec(shape, lambda *_: (0,) * len(shape), pipeline_mode=pl.Buffered(1))


def rows_of(r, c):
    return pl.BlockSpec((r, c), lambda i, *_: (i, 0))


def cols_of(r, c, start=0):
    return pl.BlockSpec((r, c), lambda i, *_: (0, i + start))


def sds(shape, dtype):
    return jax.ShapeDtypeStruct(shape, dtype)


ANY = pl.BlockSpec(memory_space=pl.ANY)
SHIFTS = (1, 3, 2)


def start_all(copies, sems):
    for n, (a, b) in enumerate(copies):
        pltpu.make_async_copy(a, b, sems.at[n]).start()


def wait_all(copies, sems):
    for n, (a, b) in enumerate(copies):
        pltpu.make_async_copy(a, b, sems.at[n]).wait()


def sources(idx, mine, other):
    z, d, s = idx[0], idx[1], idx[2]
    for e in range(4):
        for j, k in enumerate(SHIFTS):
            for ref, side in ((mine[e], s), (other[e], 1 - s)):
                yield ref, j, lax.rem(z + 4 - k, 4), d ^ e, side


def in_copies(idx, own, mine, other, dst):
    part, half = own.shape[0], own.shape[1] // 2
    r = part // 4
    out = [(own, dst.at[pl.ds(pl.multiple_of(idx[0] * part, 16), part), :])]
    for ref, j, z, d, side in sources(idx, mine, other):
        out.append((ref.at[pl.ds(j * r, r), :],
                    dst.at[pl.ds(pl.multiple_of(z * part + d * r, 16), r), pl.ds(pl.multiple_of(side * half, 128), half)]))
    return out


def up_copies(idx, own, mine, other, dst):
    part, ff = own.shape
    c = ff // 8
    out = [(own, dst.at[pl.ds(pl.multiple_of(idx[0] * part, 16), part), :])]
    for ref, j, z, d, side in sources(idx, mine, other):
        out.append((ref.at[pl.ds(j * part, part), :],
                    dst.at[pl.ds(pl.multiple_of(z * part, 16), part), pl.ds(pl.multiple_of(side * 4 * c + d * c, 128), c)]))
    return out


def down_copies(idx, own, mine, other, dst):
    q, width = own.shape
    r = q // 4
    h = width // 2
    out = [(own, dst.at[pl.ds(pl.multiple_of(idx[0] * q, 16), q), :])]
    for ref, j, z, d, side in sources(idx, mine, other):
        out.append((ref.at[pl.ds(j * r, r), :],
                    dst.at[pl.ds(pl.multiple_of(z * q + d * r, 16), r), pl.ds(pl.multiple_of(side * h, 128), h)]))
    return out


def out_copies(idx, own, mine, other, dst):
    part, width = own.shape
    r = part // 4
    h = width // 2
    out = [(own, dst.at[pl.ds(pl.multiple_of(idx[0] * part, 16), part), :])]
    for ref, j, z, d, side in sources(idx, mine, other):
        out.append((ref.at[pl.ds(3 * part + j * r, r), :],
                    dst.at[pl.ds(pl.multiple_of(z * part + d * r, 16), r), pl.ds(pl.multiple_of(side * h, 128), h)]))
    return out


def rest_copies(idx, own, mine, other, dst, start, half):
    part = own.shape[0]
    r = part // 4
    out = [(own, dst.at[pl.ds(pl.multiple_of(idx[0] * part, 16), part), :])]
    for ref, j, z, d, side in sources(idx, mine, other):
        out.append((ref.at[pl.ds(j * r, r), pl.ds(start, half)],
                    dst.at[pl.ds(pl.multiple_of(z * part + d * r, 16), r), pl.ds(pl.multiple_of(side * half, 128), half)]))
    return out


SEMS = pltpu.SemaphoreType.DMA((25,))


CH = 256


def spectra_kernel(idx, *refs):
    held, (own_taps, own_small, basis_ref, out_ref, small_ref, taps, small, sig, sems, sems2) = refs[:8], refs[8:]
    mine, other = held[:4], held[4:]
    length = taps.shape[1]

    @pl.when(pl.program_id(0) == 0)
    def _():
        copies = rest_copies(idx, own_taps, mine, other, taps, REST_TAPS, length // 2)
        part = own_small.shape[0]
        r = part // 4
        copies2 = [(own_small, small.at[pl.ds(pl.multiple_of(idx[0] * part, 16), part), :])]
        for e in range(4):
            for j, k in enumerate(SHIFTS):
                z = lax.rem(idx[0] + 4 - k, 4)
                copies2.append((mine[e].at[pl.ds(j * r, r), pl.ds(REST_SMALL, 128)],
                                small.at[pl.ds(pl.multiple_of(z * part + (idx[1] ^ e) * r, 16), r), :]))
        start_all(copies, sems)
        start_all(copies2, sems2)
        wait_all(copies2, sems2)
        wait_all(copies, sems)
        small_ref[...] = small[...].astype(f32).T[0:16]

    position = lax.broadcasted_iota(jnp.int32, (1, length), 1).astype(f32)
    rows = pl.ds(pl.multiple_of(pl.program_id(0) * CH, CH), CH)
    sig[...] = (taps[rows, :].astype(f32) * (jnp.exp(-decay_rate * position) / length)).astype(bf16)
    out_ref[...] = dot(basis_ref[...], sig[...], 1, 1).astype(bf16)


REST_TAPS, REST_SMALL = 0, 512


def kernel_spectra(idx, rest, own_taps, own_small, basis):
    length = own_taps.shape[1]
    width = own_taps.shape[0] * 4
    return call(
        spectra_kernel,
        (width // CH,),
        [ANY] * 10 + [whole(basis.shape)],
        [cols_of(2 * length, CH), pl.BlockSpec((16, width), lambda *_: (0, 0))],
        [sds((2 * length, width), bf16), sds((16, width), f32)],
        [pltpu.VMEM((width, length), bf16), pltpu.VMEM((width, 128), bf16), pltpu.VMEM((CH, length), bf16), SEMS, SEMS],
        (idx, *rest, own_taps, own_small, basis),
        4 * length * length * width,
        basis.size * 2 + 6 * length * width,
        prefetch=1,
    )


def front_kernel(idx, *refs):
    held, (own_ref, x_ref, gain_ref, tq, tk, tv, spec_ref, basis_ref, back_ref,
           normed_ref, mq, mk, mv, sspec_ref, conv_ref, gated_ref, pad, q_s, sig, s_s, y_s, w_s, sems) = refs[:8], refs[8:]
    length, width = x_ref.shape
    R = 256

    @pl.when(pl.program_id(0) == 0)
    def _():
        copies = in_copies(idx, own_ref, held[:4], held[4:], w_s)
        start_all(copies, sems)
        for r in range(0, length, R):
            hat, _ = norm_parts(x_ref[r : r + R].astype(f32))
            normed_ref[r : r + R] = (hat * gain_ref[...]).astype(bf16)
        pad[0:8] = jnp.zeros((8, 3 * CH), f32)
        wait_all(copies, sems)

    cols = [pl.ds(pl.multiple_of(p * width + pl.program_id(0) * CH, CH), CH) for p in range(3)]
    pad[8:] = dot(normed_ref[...], jnp.concatenate([w_s[:, c] for c in cols], 1))
    for r in range(0, length, R):
        now = []
        for p, (t, m) in enumerate(((tq, mq), (tk, mk), (tv, mv))):
            c = slice(p * CH, (p + 1) * CH)
            m[r : r + R] = pad[8 + r : 8 + r + R, c].astype(bf16)
            now.append(t[0:1] * pad[8 + r : 8 + r + R, c] + t[1:2] * pad[7 + r : 7 + r + R, c] + t[2:3] * pad[6 + r : 6 + r + R, c])
        q_s[r : r + R] = now[0]
        sig[r : r + R] = (now[1] * now[2]).astype(bf16)
    s_s[...] = dot(basis_ref[...], sig[...])
    for r in range(0, length, R):
        at, lo = slice(r, r + R), slice(length + r, length + r + R)
        sc, ss = s_s[at], s_s[lo]
        sspec_ref[at] = sc.astype(bf16)
        sspec_ref[lo] = ss.astype(bf16)
        kc, ks = spec_ref[at].astype(f32), spec_ref[lo].astype(f32)
        y_s[at] = (sc * kc - ss * ks).astype(bf16)
        y_s[lo] = (sc * ks + ss * kc).astype(bf16)
    conv = dot(back_ref[...], y_s[...])
    conv_ref[...] = conv.astype(bf16)
    gated_ref[...] = (q_s[...] * conv).astype(bf16)


def mixer_front(idx, held, own_in, x, gain, taps, spec, basis, back):
    length, width = x.shape[1:]
    nb = width // CH
    block = cols_of(length, CH)
    full = sds((length, width), bf16)
    return call(
        front_kernel,
        (nb,),
        [ANY] * 9 + [pl.BlockSpec((None, length, width), lambda i, idx: (idx[2], 0, 0)), whole((1, width))]
        + [cols_of(3, CH, p * nb) for p in range(3)]
        + [cols_of(2 * length, CH), whole(basis.shape), whole(back.shape)],
        [whole((length, width)), block, block, block, cols_of(2 * length, CH), block, block],
        [full, full, full, full, sds((2 * length, width), bf16), full, full],
        [pltpu.VMEM((length + 8, 3 * CH), f32), pltpu.VMEM((length, CH), f32), pltpu.VMEM((length, CH), bf16),
         pltpu.VMEM((2 * length, CH), f32), pltpu.VMEM((2 * length, CH), bf16), pltpu.VMEM((width, 3 * width), bf16), SEMS],
        (idx, *held, own_in, x, gain, taps, taps, taps, spec, basis, back),
        6 * length * width * width + 8 * length * length * width,
        2 * (10 * length * width + 3 * width * width + 2 * basis.size),
        prefetch=1,
    )


def gelu_parts(pre):
    cdf = 0.5 * (1.0 + lax.erf(pre * math.sqrt(0.5)))
    slope = cdf + pre * (jnp.exp(-0.5 * pre * pre) * (1.0 / math.sqrt(2.0 * math.pi)))
    return pre * cdf, slope


def live_rows(idx, rows, start=0):
    return (lax.broadcasted_iota(jnp.int32, (rows, 1), 0) + start < idx[3]).astype(f32)


def near_first(idx, ref, half):
    return (pl.ds(pl.multiple_of(idx[2] * half, 128), half), pl.ds(pl.multiple_of((1 - idx[2]) * half, 128), half))


def out_kernel(idx, *refs):
    rest, (own_out, x_ref, gated_ref, gain_ref, act0_ref, normed_ref, wo_ref, sem_o) = refs[:8], refs[8:]
    R, width = x_ref.shape
    start = pl.program_id(0) * R

    @pl.when(pl.program_id(0) == 0)
    def _():
        outs = out_copies(idx, own_out, rest[:4], rest[4:], wo_ref)
        start_all(outs, sem_o)
        wait_all(outs, sem_o)

    live = live_rows(idx, R, start)
    act0 = (live * (x_ref[...].astype(f32) + dot(gated_ref[...], wo_ref[...]))).astype(bf16)
    act0_ref[...] = act0
    hat, _ = norm_parts(act0.astype(f32))
    normed_ref[...] = (hat * gain_ref[...]).astype(bf16)


def mixer_out(idx, rest, own_out, x, gated, gain):
    length, width = gated.shape
    R = 512
    blk = rows_of(R, width)
    return call(
        out_kernel,
        (length // R,),
        [ANY] * 9 + [pl.BlockSpec((None, R, width), lambda i, idx: (idx[2], i, 0)), blk, whole(gain.shape)],
        [blk, blk],
        [sds((length, width), bf16)] * 2,
        [pltpu.VMEM((width, width), bf16), SEMS],
        (idx, *rest, own_out, x, gated, gain),
        2 * length * width * width,
        2 * (4 * length * width + width * width),
        prefetch=1,
    )


def up_kernel(idx, *refs):
    held, (own_up, og_ref, normed_ref, hidden_ref, slope_ref, near_ref, away_ref, wu_ref, turned, sem_u) = refs[:8], refs[8:]
    length, width = og_ref.shape
    half = width // 2
    c = pl.program_id(0)

    @pl.when(c == 0)
    def _():
        ups = up_copies(idx, own_up, held[:4], held[4:], wu_ref)
        start_all(ups, sem_u)
        live = live_rows(idx, length)
        for n, cols in enumerate(near_first(idx, og_ref, half)):
            turned[:, n * half : (n + 1) * half] = (live * og_ref[:, cols].astype(f32)).astype(bf16)
        wait_all(ups, sem_u)

    at = pl.ds(pl.multiple_of(c * width, width), width)
    hid, slope = gelu_parts(dot(normed_ref[...], wu_ref[:, at]))
    hid = hid.astype(bf16)
    hidden_ref[...] = hid
    slope_ref[...] = slope.astype(bf16)
    grad = dot(hid, turned[...], 0, 0).astype(bf16)
    near_ref[...] = grad[:, :half]
    away_ref[...] = grad[:, half:]


def mlp_up(idx, held, own_up, og, normed):
    length, width = normed.shape
    ff = own_up.shape[1]
    half = width // 2
    wide = cols_of(length, width)
    picked = pl.BlockSpec((None, length, width), lambda i, idx: (idx[2], 0, 0), pipeline_mode=pl.Buffered(1))
    return call(
        up_kernel,
        (ff // width,),
        [ANY] * 9 + [picked, whole((length, width))],
        [wide, wide, rows_of(width, half), rows_of(width, half)],
        [sds((length, ff), bf16), sds((length, ff), bf16), sds((ff, half), bf16), sds((ff, half), bf16)],
        [pltpu.VMEM((width, ff), bf16), pltpu.VMEM((length, width), bf16), SEMS],
        (idx, *held, own_up, og, normed),
        4 * length * width * ff,
        2 * (2 * length * width + 2 * width * ff + 2 * length * ff),
        prefetch=1,
    )


def down_kernel(idx, *refs):
    held, (own_up, own_down, og_ref, act0_ref, normed_ref, hidden_ref, slope_ref, gated_ref, gain_ref,
           act1_ref, ag_ref, branch_ref, gg_ref, near_ref, away_ref, near_out, away_out,
           wu_ref, wd_ref, acc, gn, branch, turned, sem_u, sem_d) = refs[:16], refs[16:]
    length, width = og_ref.shape
    half = width // 2
    c = pl.program_id(0)
    live = live_rows(idx, length)

    @pl.when(c == 0)
    def _():
        ups = up_copies(idx, own_up, held[:4], held[4:8], wu_ref)
        downs = down_copies(idx, own_down, held[8:12], held[12:], wd_ref)
        start_all(downs, sem_d)
        start_all(ups, sem_u)
        branch[...] = (live * og_ref[...].astype(f32)).astype(bf16)
        acc[...] = act0_ref[...].astype(f32)
        gn[...] = jnp.zeros((length, width), f32)
        wait_all(downs, sem_d)
        wait_all(ups, sem_u)

    at = pl.ds(pl.multiple_of(c * width, width), width)
    pre = (slope_ref[...].astype(f32) * dot(branch[...], wd_ref[at, :], 1, 1)).astype(bf16)
    for n, cols in enumerate(near_first(idx, turned, half)):
        turned[:, cols] = pre[:, n * half : (n + 1) * half]
    acc[...] += dot(hidden_ref[...], wd_ref[at, :])
    gn[...] += dot(pre, wu_ref[:, at], 1, 1)
    grad = dot(normed_ref[...], turned[...], 0, 0).astype(bf16)
    near_ref[...] = grad[:, :half]
    away_ref[...] = grad[:, half:]

    @pl.when(c == pl.num_programs(0) - 1)
    def _():
        act1_ref[...] = (live * acc[...]).astype(bf16)
        hat, inv = norm_parts(act0_ref[...].astype(f32))
        gg_ref[...] = jnp.sum(gn[...] * hat, axis=0, keepdims=True)
        ag = live * og_ref[...].astype(f32) + norm_back(gn[...], hat, inv, gain_ref[...])
        ag_ref[...] = ag
        branch_ref[...] = (live * ag).astype(bf16)
        for n, cols in enumerate(near_first(idx, branch_ref, half)):
            turned[:, n * half : (n + 1) * half] = branch_ref[:, cols]
        g_out = dot(gated_ref[...], turned[...], 0, 0).astype(bf16)
        near_out[...] = g_out[:, :half]
        away_out[...] = g_out[:, half:]


def mlp_down(idx, held_up, held_down, own_up, own_down, og, act0, normed, hidden, slope, gated, gain):
    length, width = act0.shape
    ff = own_up.shape[1]
    half = width // 2
    picked = pl.BlockSpec((None, length, width), lambda i, idx: (idx[2], 0, 0), pipeline_mode=pl.Buffered(1))
    one = whole((length, width))
    wide = cols_of(length, width)
    full = sds((length, width), bf16)
    col = pltpu.VMEM((length, width), f32)
    low = pltpu.VMEM((length, width), bf16)
    return call(
        down_kernel,
        (ff // width,),
        [ANY] * 18 + [picked, one, one, wide, wide, one, whole(gain.shape)],
        [one, one, one, whole((1, width)), cols_of(width, half), cols_of(width, half), whole((width, half)), whole((width, half))],
        [full, sds((length, width), f32), full, sds((1, width), f32), sds((width, ff // 2), bf16), sds((width, ff // 2), bf16),
         sds((width, half), bf16), sds((width, half), bf16)],
        [pltpu.VMEM((width, ff), bf16), pltpu.VMEM((ff, width), bf16), col, col, low, low, SEMS, SEMS],
        (idx, *held_up, *held_down, own_up, own_down, og, act0, normed, hidden, slope, gated, gain),
        8 * length * width * ff,
        2 * (8 * length * width + 3 * width * ff + 2 * length * ff),
        prefetch=1,
    )


def conv_back_kernel(idx, *refs):
    rest, (own_out, branch_ref, normed_ref, mq, mk, mv, tq, tk, tv, conv_ref, spec_ref, sspec_ref, basis_ref, back_ref,
           g_ref, near_ref, away_ref, gtaps_ref, pad, gpad, smooth, sig, s_s, y_s, gm, kern, w_s, sems) = refs[:8], refs[8:]
    length, width = branch_ref.shape
    half = width // 2
    hl = length // 2
    R = 256
    i = pl.program_id(0)

    @pl.when(i == 0)
    def _():
        copies = out_copies(idx, own_out, rest[:4], rest[4:], w_s)
        start_all(copies, sems)
        pad[0:8] = jnp.zeros((8, 3 * CH), f32)
        gpad[length : length + 8] = jnp.zeros((8, 3 * CH), f32)
        wait_all(copies, sems)

    rows = pl.ds(pl.multiple_of(i * CH, CH), CH)
    for p, m in enumerate((mq, mk, mv)):
        pad[8:, p * CH : (p + 1) * CH] = m[...].astype(f32)
    gg = dot(branch_ref[...], w_s[rows, :], 1, 1)
    gpad[0:length, 0:CH] = gg * conv_ref[...].astype(f32)
    s_s[0:length] = gg
    for r in range(0, length, R):
        for p, t in enumerate((tq, tk, tv)):
            c = slice(p * CH, (p + 1) * CH)
            now = t[0:1] * pad[8 + r : 8 + r + R, c] + t[1:2] * pad[7 + r : 7 + r + R, c] + t[2:3] * pad[6 + r : 6 + r + R, c]
            if p == 0:
                sig[r : r + R] = (s_s[r : r + R] * now).astype(bf16)
            else:
                smooth[r : r + R, (p - 1) * CH : p * CH] = now
    s_s[...] = dot(basis_ref[...], sig[...])
    for r in range(0, length, R):
        at, lo = slice(r, r + R), slice(length + r, length + r + R)
        gc, gs = s_s[at], s_s[lo]
        kc, ks = spec_ref[at].astype(f32), spec_ref[lo].astype(f32)
        y_s[at, 0:CH] = (kc * gc + ks * gs).astype(bf16)
        y_s[lo, 0:CH] = (kc * gs - ks * gc).astype(bf16)
        sc, ss = sspec_ref[at].astype(f32), sspec_ref[lo].astype(f32)
        y_s[at, CH:] = (sc * gc + ss * gs).astype(bf16)
        y_s[lo, CH:] = (sc * gs - ss * gc).astype(bf16)
    both = dot(back_ref[...], y_s[...])
    gpad[0:length, CH : 2 * CH] = both[:, :CH] * smooth[:, CH:]
    gpad[0:length, 2 * CH :] = both[:, :CH] * smooth[:, :CH]
    position = lax.broadcasted_iota(jnp.int32, (length, 1), 0).astype(f32)
    kern[...] = (both[:, CH:] * (jnp.exp(-decay_rate * position) / length)).T.astype(bf16)
    sums = [[jnp.zeros((1, CH), f32)] * 3 for _ in range(3)]
    for r in range(0, length, R):
        for p, t in enumerate((tq, tk, tv)):
            c = slice(p * CH, (p + 1) * CH)
            g0 = gpad[r : r + R, c]
            g = (t[0:1] * g0 + t[1:2] * gpad[r + 1 : r + 1 + R, c] + t[2:3] * gpad[r + 2 : r + 2 + R, c]).astype(bf16)
            g_ref[p, r : r + R] = g
            for n in range(2):
                at = jnp.where(idx[2] == n, 0, half) + p * (CH // 2)
                gm[r : r + R, pl.ds(pl.multiple_of(at, 128), CH // 2)] = g[:, n * (CH // 2) : (n + 1) * (CH // 2)]
            sums[p] = [sums[p][n] + jnp.sum(g0 * pad[8 - n + r : 8 - n + r + R, c], axis=0, keepdims=True) for n in range(3)]
    for p in range(3):
        for n in range(3):
            gtaps_ref[3 * p + n : 3 * p + n + 1] = sums[p][n]
    g_in = dot(normed_ref[...], gm[...], 0, 0).astype(bf16)
    cols = pl.ds(pl.multiple_of(i * half, 128), half)
    near_ref[:, cols] = g_in[:, :half]
    away_ref[:, cols] = g_in[:, half:]
    near_ref[rows, 3 * half :] = kern[:, pl.ds(pl.multiple_of(idx[2] * hl, 128), hl)]
    away_ref[rows, 3 * half :] = kern[:, pl.ds(pl.multiple_of((1 - idx[2]) * hl, 128), hl)]


def conv_backward(idx, rest, own_out, branch, normed, mixed, taps, conv, spec, sspec, basis, back):
    length, width = branch.shape
    nb = width // CH
    block = cols_of(length, CH)
    tall = cols_of(2 * length, CH)
    mix = (width, 3 * width // 2 + length // 2)
    wide = pltpu.VMEM((length + 8, 3 * CH), f32)
    return call(
        conv_back_kernel,
        (nb,),
        [ANY] * 9 + [whole(branch.shape), whole(branch.shape), block, block, block]
        + [cols_of(3, CH, p * nb) for p in range(3)]
        + [block, tall, tall, whole(basis.shape), whole(back.shape)],
        [pl.BlockSpec((3, length, CH), lambda i, *_: (0, 0, i)), whole(mix), whole(mix), cols_of(9, CH)],
        [sds((3, length, width), bf16), sds(mix, bf16), sds(mix, bf16), sds((9, width), f32)],
        [wide, wide, pltpu.VMEM((length, 2 * CH), f32), pltpu.VMEM((length, CH), bf16), pltpu.VMEM((2 * length, CH), f32),
         pltpu.VMEM((2 * length, 2 * CH), bf16), pltpu.VMEM((length, 3 * CH), bf16),
         pltpu.VMEM((CH, length), bf16), pltpu.VMEM((width, width), bf16), SEMS],
        (idx, *rest, own_out, branch, normed, *mixed, taps, taps, taps, conv, spec, sspec, basis, back),
        10 * length * width * width + 12 * length * length * width,
        2 * (14 * branch.size + 2 * basis.size + 2 * mix[0] * mix[1]),
        prefetch=1,
    )


def norm_back_kernel(idx, *refs):
    held, (own_ref, g_ref, x_ref, masked_ref, gain_ref, ag_ref, gg_ref, wi_ref, sems) = refs[:8], refs[8:]
    width = x_ref.shape[1]

    @pl.when(pl.program_id(0) == 0)
    def _():
        copies = in_copies(idx, own_ref, held[:4], held[4:], wi_ref)
        start_all(copies, sems)
        wait_all(copies, sems)

    gn = dot(jnp.concatenate([g_ref[p] for p in range(3)], 1), wi_ref[...], 1, 1)
    hat, inv = norm_parts(x_ref[...].astype(f32))
    part = jnp.sum(gn * hat, axis=0, keepdims=True)

    @pl.when(pl.program_id(0) == 0)
    def _():
        gg_ref[...] = part

    @pl.when(pl.program_id(0) > 0)
    def _():
        gg_ref[...] += part

    ag_ref[...] = masked_ref[...].astype(f32) + norm_back(gn, hat, inv, gain_ref[...])


def input_backward(idx, held, own_in, g_mixed, x, masked, gain):
    length, width = masked.shape
    R = 512
    blk = rows_of(R, width)
    return call(
        norm_back_kernel,
        (length // R,),
        [ANY] * 9 + [pl.BlockSpec((3, R, width), lambda i, *_: (0, i, 0)),
                     pl.BlockSpec((None, R, width), lambda i, idx: (idx[2], i, 0)), blk, whole(gain.shape)],
        [blk, pl.BlockSpec((1, width), lambda *_: (0, 0))],
        [sds((length, width), f32), sds((1, width), f32)],
        [pltpu.VMEM((width, 3 * width), bf16), SEMS],
        (idx, *held, own_in, g_mixed, x, masked, gain),
        6 * length * width * width,
        2 * (7 * length * width + 3 * width * width),
        prefetch=1,
    )


def unpack_mlp_kernel(idx, all_ref, up, down, out):
    part = up.shape[0]
    q = up.shape[1] // 4
    h = down.shape[1] // 2
    r = part // 4
    for n in range(8):
        d, side = n // 2, n % 2
        cols = slice(side * h, side * h + h)
        down[d * part : (d + 1) * part, cols] = all_ref[n, 0:part].astype(f32)
        up[:, d * q + side * h : d * q + side * h + h] = all_ref[n, part : 2 * part].astype(f32)
        out[d * r : (d + 1) * r, cols] = all_ref[n, 2 * part :].astype(f32)


def unpack_mix_kernel(idx, *refs):
    held, (g_in, g_kern) = refs[:8], refs[8:]
    part, length = g_kern.shape
    width = 4 * part
    r = part // 4
    h = width // 2
    b = CH // 2
    for e in range(4):
        at = pl.ds(pl.multiple_of((idx[1] ^ e) * r, 16), r)
        for ref, side in ((held[e], idx[2]), (held[4 + e], 1 - idx[2])):
            for i in range(width // CH):
                for p in range(3):
                    c = i * h + p * b
                    g_in[at, pl.ds(pl.multiple_of(p * width + i * CH + side * b, 128), b)] = ref[:, c : c + b].astype(f32)
            g_kern[at, pl.ds(pl.multiple_of(side * (length // 2), 128), length // 2)] = ref[:, 3 * h :].astype(f32)


def unpack(kernel, idx, held, shapes):
    return call(
        kernel,
        (1,),
        [whole(h.shape) for h in held],
        [whole(s) for s in shapes],
        [sds(s, f32) for s in shapes],
        [],
        (idx, *held),
        0,
        sum(6 * math.prod(s) for s in shapes),
        prefetch=1,
    )


SWAP = [(0, 1), (1, 0)]


def shift(k):
    return [(i, (i + k) % 4) for i in range(4)]


def flip(e):
    return [(i, i ^ e) for i in range(4)]


def tie(value, *others):
    return lax.optimization_barrier((value, *others))[0]


def over_line(piece):
    return jnp.concatenate([lax.ppermute(piece, "chan", shift(k)) for k in SHIFTS], 0)


def over_plane(near):
    return [near] + [lax.ppermute(near, "dp", flip(e)) for e in (1, 2, 3)]


def over_chip(mine):
    return mine + [lax.ppermute(m, "section", SWAP) for m in mine]


def total(parts):
    out = parts[0].astype(f32)
    for p in parts[1:]:
        out += p.astype(f32)
    return out.astype(bf16)


def fold_plane(parts):
    return total([parts[0]] + [lax.ppermute(parts[e], "dp", flip(e)) for e in (1, 2, 3)])


def fold_line(held, z):
    def at(k):
        return lax.dynamic_index_in_dim(held, (z + k) % 4, 0, keepdims=False)

    return total([at(0)] + [lax.ppermute(at(k), "chan", shift(k)) for k in SHIFTS])


def cut(v, at, size, axis):
    return lax.dynamic_slice_in_dim(v, at, size, axis)


def fast_body(inputs, lengths, out_grad, ln_mix_gain, w_in, short_taps, long_taps, w_out, ln_mlp_gain, w_up, w_down):
    z, d, s = lax.axis_index("chan"), lax.axis_index("dp"), lax.axis_index("section")
    length = inputs.shape[2]
    width = inputs.shape[3]
    part = w_in.shape[1]
    ff = w_up.shape[2]
    half = width // 2
    hl = length // 2
    r = part // 4
    count = lax.dynamic_index_in_dim(lengths[:, 0], s, 0, keepdims=False)
    idx = jnp.stack([z, d, s, count]).astype(jnp.int32)
    x, og = inputs[:, 0], out_grad[:, 0]
    table = odd_basis(length)
    basis, back = jnp.asarray(table), jnp.asarray(np.ascontiguousarray(table.T))
    first = s == 0

    def after(parts, values):
        return lax.optimization_barrier((list(parts), list(values)))

    def both_cores(near, away):
        return total([near, lax.ppermute(away, "section", SWAP)])

    def handed(own_first, own_second):
        return lax.ppermute(jnp.where(first, own_second, own_first).astype(bf16), "section", SWAP)

    def stacked(own_first, own_second, other, dtype):
        keep = jnp.where(first, own_first, own_second).astype(dtype)
        other = other.astype(dtype)
        both = jnp.stack([jnp.where(first, keep, other), jnp.where(first, other, keep)])
        return both[None, :, None]

    def to_plane(parts):
        return [parts[0]] + [lax.ppermute(parts[e], "dp", flip(e)) for e in (1, 2, 3)]

    def line_sum(held):
        return lax.psum_scatter(held, "chan", scatter_dimension=0, tiled=False)

    own_in, own_out, own_up, own_down = w_in[0], w_out[0], w_up[0], w_down[0]
    own_taps = long_taps[0].T
    small = jnp.concatenate([ln_mix_gain, ln_mlp_gain, short_taps[0].reshape(9, part)], 0)
    own_small = jnp.pad(small.T, ((0, 0), (0, 128 - 11)))
    piece = jnp.concatenate([cut(own_taps, s * hl, hl, 1), own_small], 1)
    split = piece.shape[1]
    piece = jnp.concatenate([cut(piece, d * r, r, 0), cut(cut(own_in, d * r, r, 0), s * 3 * half, 3 * half, 1)], 1)
    near = over_line(piece)
    near_rest, near_in = near[:, :split], near[:, split:]
    plane_rest = over_plane(near_rest)
    plane_in = over_plane(near_in)
    piece_mlp = jnp.concatenate(
        [
            cut(cut(own_down, d * part, part, 0), s * half, half, 1),
            cut(own_up, s * (ff // 2) + d * (ff // 8), ff // 8, 1),
            cut(cut(own_out, d * r, r, 0), s * half, half, 1),
        ],
        0,
    )
    line_mlp = lax.all_gather(tie(piece_mlp, near), "chan", axis=0)
    held_rest = over_chip(plane_rest)

    plane_in, (spec, small) = after(
        plane_in, kernel_spectra(idx, held_rest, tie(own_taps, near_in), own_small, basis)
    )
    held_in = over_chip(plane_in)
    gain_mix, gain_mlp = small[0:1], small[1:2]
    taps = small[2:11].reshape(3, 3, 4, part).transpose(0, 2, 1, 3).reshape(3, 3 * width)
    line_mlp = [lax.dynamic_index_in_dim(line_mlp, (z + 4 - k) % 4, 0, keepdims=False) for k in SHIFTS]
    near_up = jnp.concatenate([v[part : 2 * part] for v in line_mlp] + [v[2 * part :] for v in line_mlp], 0)
    near_down = jnp.concatenate([v[:part] for v in line_mlp], 0)
    plane_up = over_plane(near_up)
    plane_down = over_plane(near_down)
    plane_up, (normed0, mq, mk, mv, sspec, conv, gated) = after(
        plane_up, mixer_front(idx, held_in, own_in, x, gain_mix, taps, tie(spec, near_up, near_down), basis, back)
    )
    held_up = over_chip(plane_up)
    act0, normed1 = mixer_out(idx, held_up, own_out, x, gated, gain_mlp)
    plane_down, (hidden, slope, near, away) = after(plane_down, mlp_up(idx, held_up, own_up, og, normed1))
    held_down = over_chip(plane_down)

    h_down = both_cores(near, away).reshape(4, 4, part, half)
    sent_down = [lax.dynamic_index_in_dim(h_down, d ^ e, 1, keepdims=False) for e in range(4)]
    got_down = to_plane(sent_down)
    got_down, (act1, ag1, branch0, g_gain_mlp, near, away, near_out, away_out) = after(
        got_down,
        mlp_down(
            idx, held_up, held_down, own_up, own_down, og, act0, normed1, hidden, tie(slope, *sent_down), gated, gain_mlp
        ),
    )
    u_down = total(got_down)
    p_down = line_sum(u_down)
    h_up = both_cores(near, away).reshape(4, part, ff // 2)
    h_out = both_cores(near_out, away_out).reshape(4, 4, r, half)
    sent_up = [
        jnp.concatenate([cut(h_up, (d ^ e) * half, half, 2), lax.dynamic_index_in_dim(h_out, d ^ e, 1, keepdims=False)], 1)
        for e in range(4)
    ]
    got_up = to_plane(sent_up)

    branch_late = tie(branch0, u_down, *sent_up)
    got_act = handed(act0, act1)
    (*got_up, p_down, got_act), (g_mixed, near, away, g_taps) = after(
        [*got_up, p_down, got_act],
        conv_backward(idx, held_up, own_out, branch_late, normed0, (mq, mk, mv), taps, conv, spec, sspec, basis, back),
    )
    u_up = total(got_up)
    p_up = line_sum(u_up)
    h_mix = both_cores(near, away).reshape(4, 4, r, 3 * half + hl)
    sent_mix = [lax.dynamic_index_in_dim(h_mix, d ^ e, 1, keepdims=False) for e in range(4)]
    got_mix = to_plane(sent_mix)
    ag0, g_gain_mix = input_backward(idx, held_in, own_in, tie(g_mixed, u_up, *sent_mix), x, branch0, gain_mix)
    (p_up,), (ag0, g_gain_mix) = after([p_up], [ag0, g_gain_mix])
    p_mlp = jnp.concatenate([p_down, p_up], 0)
    all_mlp = lax.all_gather(p_mlp, ("dp", "section"), axis=0)
    got_mix, (ag0, g_gain_mix) = after(got_mix, [ag0, tie(g_gain_mix, p_mlp)])
    u_mix = total(got_mix)
    sent_line = [lax.dynamic_index_in_dim(u_mix, (z + k) % 4, 0, keepdims=False) for k in (0, *SHIFTS)]
    got_line = [sent_line[0]] + [lax.ppermute(v, "chan", shift(k)) for k, v in zip(SHIFTS, sent_line[1:])]
    tiny = tie(jnp.concatenate([g_gain_mix, g_gain_mlp, g_taps], 0), *sent_line)
    tiny += lax.ppermute(tiny, "section", SWAP)
    tiny += lax.ppermute(tiny, "dp", flip(1))
    ag0_late = tie(ag0, *sent_line)
    out_act = stacked(act0, act1, tie(got_act, ag0_late), bf16)
    out_ag = stacked(ag0_late, ag1, handed(ag0_late, ag1), f32)
    got_line, (tiny, out_act, out_ag) = after(got_line, [tiny, out_act, out_ag])
    g_up, g_down, g_out = unpack(unpack_mlp_kernel, idx, [all_mlp], [(part, ff), (4 * part, width), (part, width)])
    p_mix = total(got_line)
    plane_mix = over_plane(p_mix)
    tiny = tie(tiny, p_mix)
    tiny += lax.ppermute(tiny, "dp", flip(2))
    plane_mix, (tiny, g_up, g_down, g_out) = after(plane_mix, [tiny, g_up, g_down, g_out])
    got_tiny = [lax.ppermute(tiny, "chan", flip(e)) for e in (1, 2, 3)]
    g_in, g_kern = unpack(unpack_mix_kernel, idx, over_chip(plane_mix), [(part, 3 * width), (part, length)])
    got_tiny, (g_in, g_kern) = after(got_tiny, [g_in, g_kern])
    tiny = (tiny + got_tiny[0]) + (got_tiny[1] + got_tiny[2])

    mine = cut(tiny[0:2], z * part, part, 1)
    g_taps = tiny[2:11].reshape(3, 3, width).transpose(1, 0, 2).reshape(3, 3 * width)
    g_taps = cut(g_taps, z * 3 * part, 3 * part, 1)

    return (
        out_act,
        out_ag,
        mine[0:1],
        g_in[None],
        g_taps[None],
        g_kern.T[None],
        g_out[None],
        mine[1:2],
        g_up[None],
        g_down[None],
    )


def fits(mesh):
    return mesh.shape["chan"] == 4 and mesh.shape["dp"] == 4 and mesh.shape["section"] == 2


def shift_down(v, n):
    return jnp.pad(v, ((n, 0), (0, 0)))[: v.shape[0]]


def shift_up(v, n):
    return jnp.pad(v, ((0, n), (0, 0)))[n:]


def plain_body(inputs, lengths, out_grad, ln_mix_gain, w_in, short_taps, long_taps, w_out, ln_mlp_gain, w_up, w_down):
    own = lax.axis_index("section")
    length, width = inputs.shape[2:]
    position = lax.broadcasted_iota(jnp.int32, (length, 1), 0)
    x = lax.dynamic_index_in_dim(inputs[:, 0], own, 0, keepdims=False).astype(f32)
    og = lax.dynamic_index_in_dim(out_grad[:, 0], own, 0, keepdims=False)
    live = (position < lax.dynamic_index_in_dim(lengths[:, 0], own, 0, keepdims=False)).astype(f32)

    def rows(w):
        return lax.all_gather(w[0], "chan", axis=0, tiled=True)

    def cols(w):
        return lax.all_gather(w[0], "chan", axis=1, tiled=True)

    gain_mix = cols(ln_mix_gain[None])[0].astype(f32)
    gain_mlp = cols(ln_mlp_gain[None])[0].astype(f32)
    taps = cols(short_taps).astype(f32)
    kern = cols(long_taps).astype(f32)
    proj_in, proj_out, proj_up, proj_down = rows(w_in), rows(w_out), rows(w_up), rows(w_down)

    basis = jnp.asarray(odd_basis(length))
    decay = jnp.exp(-decay_rate * position.astype(f32))
    half = length

    def spectrum(v):
        both = dot(basis, v)
        return both[:half], both[half:]

    def back(cos_part, sin_part):
        return dot(basis, jnp.concatenate([cos_part, sin_part], 0).astype(bf16), 0, 0)

    kc, ks = spectrum((kern * decay).astype(bf16))
    kc, ks = kc / length, ks / length
    hat0, inv0 = norm_parts(x)
    normed0 = (hat0 * gain_mix).astype(bf16)
    mixed = dot(normed0, proj_in)
    smooth = taps[0] * mixed + taps[1] * shift_down(mixed, 1) + taps[2] * shift_down(mixed, 2)
    query, key, value = smooth[:, :width], smooth[:, width : 2 * width], smooth[:, 2 * width :]
    sc, ss = spectrum((key * value).astype(bf16))
    conv = back(sc * kc - ss * ks, sc * ks + ss * kc)
    gated = (query * conv).astype(bf16)
    act0 = (live * (x + dot(gated, proj_out))).astype(bf16)
    x1 = act0.astype(f32)
    hat1, inv1 = norm_parts(x1)
    normed1 = (hat1 * gain_mlp).astype(bf16)
    pre = dot(normed1, proj_up)
    cdf = 0.5 * (1.0 + lax.erf(pre * math.sqrt(0.5)))
    hidden = (pre * cdf).astype(bf16)
    act1 = (live * (x1 + dot(hidden, proj_down))).astype(bf16)
    masked1 = live * og.astype(f32)
    branch1 = masked1.astype(bf16)
    g_down = dot(hidden, branch1, 0, 0)
    slope = cdf + pre * (jnp.exp(-0.5 * pre * pre) * (1.0 / math.sqrt(2.0 * math.pi)))
    pre_grad = (slope * dot(branch1, proj_down, 1, 1)).astype(bf16)
    g_up = dot(normed1, pre_grad, 0, 0)
    gn1 = dot(pre_grad, proj_up, 1, 1)
    g_gain_mlp = jnp.sum(gn1 * hat1, axis=0)
    ag1 = masked1 + norm_back(gn1, hat1, inv1, gain_mlp)
    ag1_low = ag1.astype(bf16)
    masked0 = live * ag1_low.astype(f32)
    branch0 = masked0.astype(bf16)
    g_out = dot(gated, branch0, 0, 0)
    grad_gated = dot(branch0, proj_out, 1, 1)
    gc, gs = spectrum((grad_gated * query).astype(bf16))
    g_kern = back(sc * gc + ss * gs, sc * gs - ss * gc) * (decay / length)
    g_sig = back(kc * gc + ks * gs, kc * gs - ks * gc)
    g_smooth = jnp.concatenate([grad_gated * conv, g_sig * value, g_sig * key], 1)
    g_taps = jnp.stack([jnp.sum(g_smooth * shift_down(mixed, n), axis=0) if n else jnp.sum(g_smooth * mixed, axis=0) for n in range(3)])
    g_mixed = (taps[0] * g_smooth + taps[1] * shift_up(g_smooth, 1) + taps[2] * shift_up(g_smooth, 2)).astype(bf16)
    g_in = dot(normed0, g_mixed, 0, 0)
    gn0 = dot(g_mixed, proj_in, 1, 1)
    g_gain_mix = jnp.sum(gn0 * hat0, axis=0)
    ag0 = masked0 + norm_back(gn0, hat0, inv0, gain_mix)

    swap = [(0, 1), (1, 0)]
    first = own == 0

    def exchange(own_first, own_second, dtype):
        keep = jnp.where(first, own_first, own_second).astype(dtype)
        other = lax.ppermute(jnp.where(first, own_second, own_first).astype(bf16), "section", swap).astype(dtype)
        both = jnp.stack([jnp.where(first, keep, other), jnp.where(first, other, keep)])
        return both[None, :, None]

    def reduced(g, dim):
        part = lax.psum_scatter(g.astype(bf16), "chan", scatter_dimension=dim, tiled=True)
        return lax.psum(part, ("section", "dp")).astype(f32)[None]

    return (
        exchange(act0, act1, bf16),
        exchange(ag0, ag1, f32),
        reduced(g_gain_mix, 0),
        reduced(g_in, 0),
        reduced(g_taps, 1),
        reduced(g_kern, 1),
        reduced(g_out, 0),
        reduced(g_gain_mlp, 0),
        reduced(g_up, 0),
        reduced(g_down, 0),
    )


def solution(mesh):
    return jax.shard_map(
        fast_body if fits(mesh) else plain_body,
        mesh=mesh,
        in_specs=(
            P(None, ("dp", "chan"), None, None),
            P(None, ("dp", "chan")),
            P(None, ("dp", "chan"), None, None),
            P(None, "chan"),
            P(None, "chan", None),
            P(None, None, "chan"),
            P(None, None, "chan"),
            P(None, "chan", None),
            P(None, "chan"),
            P(None, "chan", None),
            P(None, "chan", None),
        ),
        out_specs=(
            P("section", None, ("dp", "chan"), None, None),
            P("section", None, ("dp", "chan"), None, None),
            P(None, "chan"),
            P(None, "chan", None),
            P(None, None, "chan"),
            P(None, None, "chan"),
            P(None, "chan", None),
            P(None, "chan"),
            P(None, "chan", None),
            P(None, "chan", None),
        ),
        check_vma=False,
    )
```

```python
import math

import jax
import jax.numpy as jnp
import ml_dtypes
import numpy as np
from jax import lax
from jax.experimental import pallas as pl
from jax.experimental.pallas import tpu as pltpu
from jax.sharding import PartitionSpec as P

decay_rate = 0.003
bf16 = jnp.bfloat16
f32 = jnp.float32
MIB = 1 << 20


def odd_basis(length):
    phase = (2 * np.arange(length)[:, None] + 1) * np.arange(length)[None, :] % (4 * length)
    angle = phase * (math.pi / (2 * length))
    return np.concatenate([np.cos(angle), np.sin(angle)], 0).astype(ml_dtypes.bfloat16)


def dot(a, b, ca=1, cb=0):
    return lax.dot_general(a, b, (((ca,), (cb,)), ((), ())), preferred_element_type=f32)


def norm_parts(values):
    centered = values - jnp.mean(values, axis=-1, keepdims=True)
    spread = jnp.mean(centered * centered, axis=-1, keepdims=True)
    inv = lax.rsqrt(spread + 1e-05)
    return centered * inv, inv


def norm_back(grad_normed, hat, inv, gain):
    grad_hat = grad_normed * gain
    return inv * (
        grad_hat
        - jnp.mean(grad_hat, axis=-1, keepdims=True)
        - hat * jnp.mean(grad_hat * hat, axis=-1, keepdims=True)
    )


def call(kernel, grid, in_specs, out_specs, out_shape, scratch, args, flops, nbytes, limit=56, prefetch=0):
    spec = pltpu.PrefetchScalarGridSpec(
        num_scalar_prefetch=prefetch, grid=grid, in_specs=in_specs, out_specs=out_specs, scratch_shapes=scratch
    )
    return pl.pallas_call(
        kernel,
        grid_spec=spec,
        out_shape=out_shape,
        compiler_params=pltpu.CompilerParams(
            dimension_semantics=("arbitrary",) * len(grid), vmem_limit_bytes=limit * MIB
        ),
        cost_estimate=pl.CostEstimate(flops=flops, bytes_accessed=nbytes, transcendentals=0),
    )(*args)


def whole(shape):
    return pl.BlockSpec(shape, lambda *_: (0,) * len(shape), pipeline_mode=pl.Buffered(1))


def rows_of(r, c):
    return pl.BlockSpec((r, c), lambda i, *_: (i, 0))


def cols_of(r, c, start=0):
    return pl.BlockSpec((r, c), lambda i, *_: (0, i + start))


def sds(shape, dtype):
    return jax.ShapeDtypeStruct(shape, dtype)


ANY = pl.BlockSpec(memory_space=pl.ANY)
SHIFTS = (1, 3, 2)


def start_all(copies, sems):
    for n, (a, b) in enumerate(copies):
        pltpu.make_async_copy(a, b, sems.at[n]).start()


def wait_all(copies, sems):
    for n, (a, b) in enumerate(copies):
        pltpu.make_async_copy(a, b, sems.at[n]).wait()


def sources(idx, mine, other):
    z, d, s = idx[0], idx[1], idx[2]
    for e in range(4):
        for j, k in enumerate(SHIFTS):
            for ref, side in ((mine[e], s), (other[e], 1 - s)):
                yield ref, j, lax.rem(z + 4 - k, 4), d ^ e, side


def in_copies(idx, own, mine, other, dst):
    part, half = own.shape[0], own.shape[1] // 2
    r = part // 4
    out = [(own, dst.at[pl.ds(pl.multiple_of(idx[0] * part, 16), part), :])]
    for ref, j, z, d, side in sources(idx, mine, other):
        out.append((ref.at[pl.ds(j * r, r), :],
                    dst.at[pl.ds(pl.multiple_of(z * part + d * r, 16), r), pl.ds(pl.multiple_of(side * half, 128), half)]))
    return out


def up_copies(idx, own, mine, other, dst):
    part, ff = own.shape
    c = ff // 8
    step = part + part // 4
    out = [(own, dst.at[pl.ds(pl.multiple_of(idx[0] * part, 16), part), :])]
    for ref, j, z, d, side in sources(idx, mine, other):
        out.append((ref.at[pl.ds(j * step, part), :],
                    dst.at[pl.ds(pl.multiple_of(z * part, 16), part), pl.ds(pl.multiple_of(side * 4 * c + d * c, 128), c)]))
    return out


def down_copies(idx, own, mine, other, dst):
    q, width = own.shape
    r = q // 4
    h = width // 2
    out = [(own, dst.at[pl.ds(pl.multiple_of(idx[0] * q, 16), q), :])]
    for ref, j, z, d, side in sources(idx, mine, other):
        out.append((ref.at[pl.ds(j * r, r), :],
                    dst.at[pl.ds(pl.multiple_of(z * q + d * r, 16), r), pl.ds(pl.multiple_of(side * h, 128), h)]))
    return out


def out_copies(idx, own, mine, other, dst):
    part, width = own.shape
    r = part // 4
    h = width // 2
    out = [(own, dst.at[pl.ds(pl.multiple_of(idx[0] * part, 16), part), :])]
    for ref, j, z, d, side in sources(idx, mine, other):
        out.append((ref.at[pl.ds(j * 5 * r + part, r), :],
                    dst.at[pl.ds(pl.multiple_of(z * part + d * r, 16), r), pl.ds(pl.multiple_of(side * h, 128), h)]))
    return out


def rest_copies(idx, own, mine, other, dst, start, half):
    part = own.shape[0]
    r = part // 4
    out = [(own, dst.at[pl.ds(pl.multiple_of(idx[0] * part, 16), part), :])]
    for ref, j, z, d, side in sources(idx, mine, other):
        out.append((ref.at[pl.ds(j * r, r), pl.ds(start, half)],
                    dst.at[pl.ds(pl.multiple_of(z * part + d * r, 16), r), pl.ds(pl.multiple_of(side * half, 128), half)]))
    return out


SEMS = pltpu.SemaphoreType.DMA((25,))


CH = 256


def spectra_kernel(idx, *refs):
    held, (own_taps, own_small, basis_ref, out_ref, small_ref, taps_ref, taps, small, tall, sig, sems, sems2) = refs[:8], refs[8:]
    mine, other = held[:4], held[4:]
    length = taps.shape[1]

    @pl.when(pl.program_id(0) == 0)
    def _():
        copies = rest_copies(idx, own_taps, mine, other, taps, REST_TAPS, length // 2)
        part = own_small.shape[0]
        r = part // 4
        copies2 = [(own_small, small.at[pl.ds(pl.multiple_of(idx[0] * part, 16), part), :])]
        for e in range(4):
            for j, k in enumerate(SHIFTS):
                z = lax.rem(idx[0] + 4 - k, 4)
                copies2.append((mine[e].at[pl.ds(j * r, r), pl.ds(REST_SMALL, 128)],
                                small.at[pl.ds(pl.multiple_of(z * part + (idx[1] ^ e) * r, 16), r), :]))
        start_all(copies, sems)
        start_all(copies2, sems2)
        wait_all(copies2, sems2)
        wait_all(copies, sems)
        wide = small[...].astype(f32)
        small_ref[...] = wide.T[0:8]
        for z in range(4):
            for q in range(3):
                tall[(3 * z + q) * part : (3 * z + q + 1) * part] = pltpu.roll(wide[z * part : (z + 1) * part], 126 - q, 1)
        taps_ref[...] = tall[...].T[0:8]

    position = lax.broadcasted_iota(jnp.int32, (1, length), 1).astype(f32)
    rows = pl.ds(pl.multiple_of(pl.program_id(0) * CH, CH), CH)
    sig[...] = (taps[rows, :].astype(f32) * (jnp.exp(-decay_rate * position) / length)).astype(bf16)
    out_ref[...] = dot(basis_ref[...], sig[...], 1, 1).astype(bf16)


REST_TAPS, REST_SMALL = 0, 512


def kernel_spectra(idx, rest, own_taps, own_small, basis):
    length = own_taps.shape[1]
    width = own_taps.shape[0] * 4
    return call(
        spectra_kernel,
        (width // CH,),
        [ANY] * 10 + [whole(basis.shape)],
        [cols_of(2 * length, CH), whole((8, width)), whole((8, 3 * width))],
        [sds((2 * length, width), bf16), sds((8, width), f32), sds((8, 3 * width), f32)],
        [pltpu.VMEM((width, length), bf16), pltpu.VMEM((width, 128), bf16), pltpu.VMEM((3 * width, 128), f32), pltpu.VMEM((CH, length), bf16), SEMS, SEMS],
        (idx, *rest, own_taps, own_small, basis),
        4 * length * length * width,
        basis.size * 2 + 6 * length * width,
        prefetch=1,
    )


class Mover:
    def __init__(self, sems):
        self.sems, self.used = sems, 0

    def start(self, src, dst):
        copy = pltpu.make_async_copy(src, dst, self.sems.at[self.used])
        self.used += 1
        copy.start()
        return copy

    def pieces(self, pairs):
        return [self.start(a, b) for a, b in pairs]


def settle(*copies):
    for c in copies:
        if isinstance(c, list):
            settle(*c)
        else:
            c.wait()


def manual(kernel, n_in, vmem_in, out_shapes, out_specs, scratch, sems, args, flops, nbytes):
    return call(
        kernel,
        (1,),
        [ANY] * n_in + [whole(v.shape) for v in vmem_in],
        out_specs,
        out_shapes,
        [*scratch, pltpu.SemaphoreType.DMA((sems,))],
        (*args, *vmem_in),
        flops,
        nbytes,
        limit=60,
        prefetch=1,
    )


def blocks_of(i):
    return slice(i * CH, (i + 1) * CH)


def front_kernel(idx, *refs):
    held, (own, x_in, spec_in, basis_in, back_in, gain, taps, normed_o, m_o, qkv_o, sspec_o, conv_o, gated_o,
           x_s, w_s, spec_s, basis_s, back_s, normed_s, m_s, qkv_s, sspec_s, conv_s, gated_s,
           pad0, pad1, sig_s, s0, s1, y0, y1, sems) = refs[:8], refs[8:]
    pads, s_s, y_s = (pad0, pad1), (s0, s1), (y0, y1)
    length, width = x_s.shape
    R = 256
    go = Mover(sems)
    x_c = go.start(x_in.at[idx[2]], x_s)
    w_c = go.pieces(in_copies(idx, own, held[:4], held[4:], w_s))
    sent = []
    for p in pads:
        p[0:8] = jnp.zeros((8, 3 * CH), f32)
    settle(x_c)
    for r in range(0, length, R):
        hat, _ = norm_parts(x_s[r : r + R].astype(f32))
        normed_s[r : r + R] = (hat * gain[...]).astype(bf16)
    settle(w_c)
    basis_c = go.start(basis_in, basis_s)

    def mix(i):
        w = jnp.concatenate([w_s[:, p * width + i * CH : p * width + (i + 1) * CH] for p in range(3)], 1)
        pads[i % 2][8:] = dot(normed_s[...], w)

    def smooth(i):
        pad = pads[i % 2]
        for r in range(0, length, R):
            now = []
            for p in range(3):
                c = blocks_of(p)
                g = slice(p * width + i * CH, p * width + (i + 1) * CH)
                m_s[p, r : r + R, blocks_of(i)] = pad[8 + r : 8 + r + R, c].astype(bf16)
                now.append(taps[0:1, g] * pad[8 + r : 8 + r + R, c] + taps[3:4, g] * pad[7 + r : 7 + r + R, c]
                           + taps[6:7, g] * pad[6 + r : 6 + r + R, c])
                qkv_s[p, r : r + R, blocks_of(i)] = now[p].astype(bf16)
            sig_s[r : r + R, blocks_of(i)] = (now[1] * now[2]).astype(bf16)
        sent.append(go.start(m_s.at[:, :, blocks_of(i)], m_o.at[:, :, blocks_of(i)]))
        sent.append(go.start(qkv_s.at[:, :, blocks_of(i)], qkv_o.at[:, :, blocks_of(i)]))

    def forth(i):
        s_s[i % 2][...] = dot(basis_s[...], sig_s[:, blocks_of(i)])

    def times(i):
        c = blocks_of(i)
        for r in range(0, length, R):
            at, lo = slice(r, r + R), slice(length + r, length + r + R)
            sc, ss = s_s[i % 2][at], s_s[i % 2][lo]
            sspec_s[at, c] = sc.astype(bf16)
            sspec_s[lo, c] = ss.astype(bf16)
            kc, ks = spec_s[at, c].astype(f32), spec_s[lo, c].astype(f32)
            y_s[i % 2][at] = (sc * kc - ss * ks).astype(bf16)
            y_s[i % 2][lo] = (sc * ks + ss * kc).astype(bf16)
        sent.append(go.start(sspec_s.at[:, c], sspec_o.at[:, c]))

    def back(i):
        c = blocks_of(i)
        conv = dot(back_s[...], y_s[i % 2][...])
        conv_s[:, c] = conv.astype(bf16)
        gated_s[:, c] = (qkv_s[0, :, c].astype(f32) * conv).astype(bf16)
        sent.append(go.start(conv_s.at[:, c], conv_o.at[:, c]))
        sent.append(go.start(gated_s.at[:, c], gated_o.at[:, c]))

    mix(0)
    mix(1)
    settle(basis_c)
    spec_c = go.start(spec_in, spec_s)
    smooth(0)
    forth(0)
    mix(2)
    settle(spec_c)
    back_c = go.start(back_in, back_s)
    sent.append(go.start(normed_s, normed_o))
    smooth(1)
    times(0)
    forth(1)
    settle(back_c)
    back(0)
    smooth(2)
    times(1)
    forth(2)
    back(1)
    times(2)
    back(2)
    settle(sent)


def mixer_front(idx, held, own_in, x, gain, taps, spec, basis, back):
    length, width = x.shape[1:]
    V = pltpu.VMEM
    low, three, tall = (length, width), (3, length, width), (2 * length, width)
    outs = [low, three, three, tall, low, low]
    return manual(
        front_kernel,
        13,
        (gain, taps),
        [sds(s, bf16) for s in outs],
        [ANY] * 6,
        [V(s, bf16) for s in (low, (width, 3 * width), tall, basis.shape, back.shape, *outs)]
        + [V((length + 8, 3 * CH), f32)] * 2 + [V(low, bf16)] + [V((2 * length, CH), f32)] * 2 + [V((2 * length, CH), bf16)] * 2,
        48,
        (idx, *held, own_in, x, spec, basis, back),
        6 * length * width * width + 8 * length * length * width,
        2 * (16 * length * width + 3 * width * width + 2 * basis.size),
    )


def gelu_parts(pre):
    cdf = 0.5 * (1.0 + lax.erf(pre * math.sqrt(0.5)))
    slope = cdf + pre * (jnp.exp(-0.5 * pre * pre) * (1.0 / math.sqrt(2.0 * math.pi)))
    return pre * cdf, slope


def live_rows(idx, rows, start=0):
    return (lax.broadcasted_iota(jnp.int32, (rows, 1), 0) + start < idx[3]).astype(f32)


def near_first(idx, ref, half):
    return (pl.ds(pl.multiple_of(idx[2] * half, 128), half), pl.ds(pl.multiple_of((1 - idx[2]) * half, 128), half))


def out_kernel(idx, *refs):
    rest, (own_out, x_ref, gated_ref, gain_ref, act0_ref, normed_ref, wo_ref, sem_o) = refs[:8], refs[8:]
    R, width = x_ref.shape
    start = pl.program_id(0) * R

    @pl.when(pl.program_id(0) == 0)
    def _():
        outs = out_copies(idx, own_out, rest[:4], rest[4:], wo_ref)
        start_all(outs, sem_o)
        wait_all(outs, sem_o)

    live = live_rows(idx, R, start)
    act0 = (live * (x_ref[...].astype(f32) + dot(gated_ref[...], wo_ref[...]))).astype(bf16)
    act0_ref[...] = act0
    hat, _ = norm_parts(act0.astype(f32))
    normed_ref[...] = (hat * gain_ref[...]).astype(bf16)


def mixer_out(idx, rest, own_out, x, gated, gain):
    length, width = gated.shape
    R = 512
    blk = rows_of(R, width)
    return call(
        out_kernel,
        (length // R,),
        [ANY] * 9 + [pl.BlockSpec((None, R, width), lambda i, idx: (idx[2], i, 0)), blk, whole(gain.shape)],
        [blk, blk],
        [sds((length, width), bf16)] * 2,
        [pltpu.VMEM((width, width), bf16), SEMS],
        (idx, *rest, own_out, x, gated, gain),
        2 * length * width * width,
        2 * (4 * length * width + width * width),
        prefetch=1,
    )


def up_kernel(idx, *refs):
    held, (own_up, og_ref, normed_ref, hidden_ref, slope_ref, near_ref, away_ref, wu_ref, turned, sem_u) = refs[:8], refs[8:]
    length, width = og_ref.shape
    half = width // 2
    c = pl.program_id(0)

    @pl.when(c == 0)
    def _():
        ups = up_copies(idx, own_up, held[:4], held[4:], wu_ref)
        start_all(ups, sem_u)
        live = live_rows(idx, length)
        for n, cols in enumerate(near_first(idx, og_ref, half)):
            turned[:, n * half : (n + 1) * half] = (live * og_ref[:, cols].astype(f32)).astype(bf16)
        wait_all(ups, sem_u)

    at = pl.ds(pl.multiple_of(c * width, width), width)
    hid, slope = gelu_parts(dot(normed_ref[...], wu_ref[:, at]))
    hid = hid.astype(bf16)
    hidden_ref[...] = hid
    slope_ref[...] = slope.astype(bf16)
    grad = dot(hid, turned[...], 0, 0).astype(bf16)
    near_ref[...] = grad[:, :half]
    away_ref[...] = grad[:, half:]


def mlp_up(idx, held, own_up, og, normed):
    length, width = normed.shape
    ff = own_up.shape[1]
    half = width // 2
    wide = cols_of(length, width)
    picked = pl.BlockSpec((None, length, width), lambda i, idx: (idx[2], 0, 0), pipeline_mode=pl.Buffered(1))
    return call(
        up_kernel,
        (ff // width,),
        [ANY] * 9 + [picked, whole((length, width))],
        [wide, wide, rows_of(width, half), rows_of(width, half)],
        [sds((length, ff), bf16), sds((length, ff), bf16), sds((ff, half), bf16), sds((ff, half), bf16)],
        [pltpu.VMEM((width, ff), bf16), pltpu.VMEM((length, width), bf16), SEMS],
        (idx, *held, own_up, og, normed),
        4 * length * width * ff,
        2 * (2 * length * width + 2 * width * ff + 2 * length * ff),
        prefetch=1,
    )


def down_kernel(idx, *refs):
    held, (own_up, own_down, og_ref, act0_ref, normed_ref, hidden_ref, slope_ref, gated_ref, gain_ref,
           act1_ref, ag_ref, branch_ref, gg_ref, near_ref, away_ref, near_out, away_out,
           wu_ref, wd_ref, acc, gn, branch, turned, sem_u, sem_d) = refs[:16], refs[16:]
    length, width = og_ref.shape
    half = width // 2
    c = pl.program_id(0)
    live = live_rows(idx, length)

    @pl.when(c == 0)
    def _():
        ups = up_copies(idx, own_up, held[:4], held[4:8], wu_ref)
        downs = down_copies(idx, own_down, held[8:12], held[12:], wd_ref)
        start_all(downs, sem_d)
        start_all(ups, sem_u)
        branch[...] = (live * og_ref[...].astype(f32)).astype(bf16)
        acc[...] = act0_ref[...].astype(f32)
        gn[...] = jnp.zeros((length, width), f32)
        wait_all(downs, sem_d)
        wait_all(ups, sem_u)

    at = pl.ds(pl.multiple_of(c * width, width), width)
    pre = (slope_ref[...].astype(f32) * dot(branch[...], wd_ref[at, :], 1, 1)).astype(bf16)
    for n, cols in enumerate(near_first(idx, turned, half)):
        turned[:, cols] = pre[:, n * half : (n + 1) * half]
    acc[...] += dot(hidden_ref[...], wd_ref[at, :])
    gn[...] += dot(pre, wu_ref[:, at], 1, 1)
    grad = dot(normed_ref[...], turned[...], 0, 0).astype(bf16)
    near_ref[...] = grad[:, :half]
    away_ref[...] = grad[:, half:]

    @pl.when(c == pl.num_programs(0) - 1)
    def _():
        act1_ref[...] = (live * acc[...]).astype(bf16)
        hat, inv = norm_parts(act0_ref[...].astype(f32))
        gg_ref[...] = jnp.sum(gn[...] * hat, axis=0, keepdims=True)
        ag = live * og_ref[...].astype(f32) + norm_back(gn[...], hat, inv, gain_ref[...])
        ag_ref[...] = ag
        branch_ref[...] = (live * ag).astype(bf16)
        for n, cols in enumerate(near_first(idx, branch_ref, half)):
            turned[:, n * half : (n + 1) * half] = branch_ref[:, cols]
        g_out = dot(gated_ref[...], turned[...], 0, 0).astype(bf16)
        near_out[...] = g_out[:, :half]
        away_out[...] = g_out[:, half:]


def mlp_down(idx, held_up, held_down, own_up, own_down, og, act0, normed, hidden, slope, gated, gain):
    length, width = act0.shape
    ff = own_up.shape[1]
    half = width // 2
    picked = pl.BlockSpec((None, length, width), lambda i, idx: (idx[2], 0, 0), pipeline_mode=pl.Buffered(1))
    one = whole((length, width))
    wide = cols_of(length, width)
    full = sds((length, width), bf16)
    col = pltpu.VMEM((length, width), f32)
    low = pltpu.VMEM((length, width), bf16)
    return call(
        down_kernel,
        (ff // width,),
        [ANY] * 18 + [picked, one, one, wide, wide, one, whole(gain.shape)],
        [one, one, one, whole((1, width)), cols_of(width, half), cols_of(width, half), whole((width, half)), whole((width, half))],
        [full, sds((length, width), f32), full, sds((1, width), f32), sds((width, ff // 2), bf16), sds((width, ff // 2), bf16),
         sds((width, half), bf16), sds((width, half), bf16)],
        [pltpu.VMEM((width, ff), bf16), pltpu.VMEM((ff, width), bf16), col, col, low, low, SEMS, SEMS],
        (idx, *held_up, *held_down, own_up, own_down, og, act0, normed, hidden, slope, gated, gain),
        8 * length * width * ff,
        2 * (8 * length * width + 3 * width * ff + 2 * length * ff),
        prefetch=1,
    )


def conv_back_kernel(idx, *refs):
    held, (own_out, branch_in, normed_in, m_in, qkv_in, conv_in, spec_in, sspec_in, basis_in, back_in, taps,
           g_o, near_o, away_o, gtaps_ref,
           w_s, branch_s, normed_s, m_s, qkv_s, conv_s, spec_s, sspec_s, basis_s, back_s,
           gpad0, gpad1, sig_s, s0, s1, y0, y1, both_s, gm0, gm1, g0_s, g1_s, kern0, kern1, near0, near1, away0, away1,
           sems) = refs[:8], refs[8:]
    gpads, s_s, y_s, gms, g_s, kerns, near_s, away_s = ((gpad0, gpad1), (s0, s1), (y0, y1), (gm0, gm1), (g0_s, g1_s),
                                                        (kern0, kern1), (near0, near1), (away0, away1))
    length, width = branch_s.shape
    half = width // 2
    hl = length // 2
    R = 256
    nb = width // CH
    go = Mover(sems)
    branch_c = go.start(branch_in, branch_s)
    w_c = go.pieces(out_copies(idx, own_out, held[:4], held[4:], w_s))
    basis_c = go.start(basis_in, basis_s)

    def fetch(i):
        c = blocks_of(i)
        return [go.start(qkv_in.at[:, :, c], qkv_s.at[:, :, c]), go.start(conv_in.at[:, c], conv_s.at[:, c])]

    def fetch_spectra(i):
        c = blocks_of(i)
        return [go.start(spec_in.at[:, c], spec_s.at[:, c]), go.start(sspec_in.at[:, c], sspec_s.at[:, c])]

    def fetch_mixed(i):
        c = blocks_of(i)
        return go.start(m_in.at[:, :, c], m_s.at[:, :, c])

    for p in gpads:
        p[length : length + 8] = jnp.zeros((8, 3 * CH), f32)
    sent = [[], []]
    settle(branch_c, w_c)
    first_c = fetch(0)

    def spread_back(i):
        s_s[i % 2][0:length] = dot(branch_s[...], w_s[blocks_of(i), :], 1, 1)

    def gate(i):
        c = blocks_of(i)
        for r in range(0, length, R):
            at = slice(r, r + R)
            gg = s_s[i % 2][at]
            sig_s[at, c] = (gg * qkv_s[0, at, c].astype(f32)).astype(bf16)
            gpads[i % 2][at, 0:CH] = gg * conv_s[at, c].astype(f32)

    def forth(i):
        s_s[i % 2][...] = dot(basis_s[...], sig_s[:, blocks_of(i)])

    def times(i):
        c = blocks_of(i)
        y = y_s[i % 2]
        for r in range(0, length, R):
            at, lo = slice(r, r + R), slice(length + r, length + r + R)
            gc, gs = s_s[i % 2][at], s_s[i % 2][lo]
            kc, ks = spec_s[at, c].astype(f32), spec_s[lo, c].astype(f32)
            y[at, 0:CH] = (kc * gc + ks * gs).astype(bf16)
            y[lo, 0:CH] = (kc * gs - ks * gc).astype(bf16)
            sc, ss = sspec_s[at, c].astype(f32), sspec_s[lo, c].astype(f32)
            y[at, CH:] = (sc * gc + ss * gs).astype(bf16)
            y[lo, CH:] = (sc * gs - ss * gc).astype(bf16)

    def back(i):
        both_s[...] = dot(back_s[...], y_s[i % 2][...])

    def unsmooth(i):
        b = blocks_of(i)
        gpad, gm, kern = gpads[i % 2], gms[i % 2], kerns[i % 2]
        settle(sent[i % 2])
        for r in range(0, length, R):
            at = slice(r, r + R)
            g_sig = both_s[at, :CH]
            gpad[at, CH : 2 * CH] = g_sig * qkv_s[2, at, b].astype(f32)
            gpad[at, 2 * CH :] = g_sig * qkv_s[1, at, b].astype(f32)
            position = (lax.broadcasted_iota(jnp.int32, (R, 1), 0) + r).astype(f32)
            kern[:, at] = (both_s[at, CH:] * (jnp.exp(-decay_rate * position) / length)).T.astype(bf16)
        sums = [[jnp.zeros((1, CH), f32)] * 3 for _ in range(3)]
        for r in range(0, length, R):
            at = slice(r, r + R)
            for p in range(3):
                c = blocks_of(p)
                t = slice(p * width + i * CH, p * width + (i + 1) * CH)
                now = [gpad[r + n : r + n + R, c] for n in range(3)]
                g = (taps[0:1, t] * now[0] + taps[3:4, t] * now[1] + taps[6:7, t] * now[2]).astype(bf16)
                g_s[i % 2][p, at] = g
                for n in range(2):
                    to = jnp.where(idx[2] == n, 0, half) + p * (CH // 2)
                    gm[at, pl.ds(pl.multiple_of(to, 128), CH // 2)] = g[:, n * (CH // 2) : (n + 1) * (CH // 2)]
                mixed = m_s[p, at, b].astype(f32)
                sums[p] = [sums[p][n] + jnp.sum(now[n] * mixed, axis=0, keepdims=True) for n in range(3)]
        for p in range(3):
            for n in range(3):
                gtaps_ref[3 * p + n : 3 * p + n + 1, b] = sums[p][n]
        side = slice(3 * half, 3 * half + hl)
        mine, other = near_first(idx, kern, hl)
        sent[i % 2] = [go.start(g_s[i % 2], g_o.at[:, :, b]), go.start(kern.at[:, mine], near_o.at[b, side]),
                       go.start(kern.at[:, other], away_o.at[b, side])]

    def grad(i):
        g = dot(normed_s[...], gms[i % 2][...], 0, 0).astype(bf16)
        near_s[i % 2][...] = g[:, :half]
        away_s[i % 2][...] = g[:, half:]
        c = slice(i * half, (i + 1) * half)
        sent[i % 2] += [go.start(near_s[i % 2], near_o.at[:, c]), go.start(away_s[i % 2], away_o.at[:, c])]

    spread_back(0)
    spread_back(1)
    settle(basis_c, first_c)
    spectra_c = fetch_spectra(0)
    gate(0)
    forth(0)
    settle(spectra_c)
    back_c = go.start(back_in, back_s)
    next_c = fetch(1)
    times(0)
    settle(next_c, back_c)
    spectra_c = fetch_spectra(1)
    mixed_c = fetch_mixed(0)
    normed_c = go.start(normed_in, normed_s)
    back(0)
    gate(1)
    forth(1)
    spread_back(2)
    settle(spectra_c, mixed_c, normed_c)
    next_c = fetch(2)
    mixed_c = fetch_mixed(1)
    spectra_c = fetch_spectra(2)
    unsmooth(0)
    times(1)
    back(1)
    grad(0)
    settle(next_c, mixed_c, spectra_c)
    mixed_c = fetch_mixed(2)
    gate(2)
    forth(2)
    unsmooth(1)
    times(2)
    grad(1)
    back(2)
    settle(mixed_c)
    unsmooth(2)
    grad(2)
    settle(sent)


def conv_backward(idx, held, own_out, branch, normed, mixed, qkv, taps, conv, spec, sspec, basis, back):
    length, width = branch.shape
    half = width // 2
    mix = (width, 3 * half + length // 2)
    V = pltpu.VMEM
    low, three, tall = (length, width), (3, length, width), (2 * length, width)
    twice = lambda s, t: [V(s, t)] * 2
    return manual(
        conv_back_kernel,
        18,
        (taps,),
        [sds(three, bf16), sds(mix, bf16), sds(mix, bf16), sds((9, width), f32)],
        [ANY] * 3 + [whole((9, width))],
        [V(s, bf16) for s in ((width, width), low, low, three, three, low, tall, tall, basis.shape, back.shape)]
        + twice((length + 8, 3 * CH), f32) + [V(low, bf16)] + twice((2 * length, CH), f32) + twice((2 * length, 2 * CH), bf16)
        + [V((length, 2 * CH), f32)] + twice((length, 3 * CH), bf16) + twice((3, length, CH), bf16) + twice((CH, length), bf16)
        + twice((width, half), bf16) + twice((width, half), bf16),
        64,
        (idx, *held, own_out, branch, normed, mixed, qkv, conv, spec, sspec, basis, back),
        8 * length * width * width + 12 * length * length * width,
        2 * (22 * length * width + 2 * basis.size + 2 * mix[0] * mix[1]),
    )


def norm_back_kernel(idx, *refs):
    held, (own_ref, g_ref, x_ref, masked_ref, gain_ref, ag_ref, gg_ref, wi_ref, sems) = refs[:8], refs[8:]
    width = x_ref.shape[1]

    @pl.when(pl.program_id(0) == 0)
    def _():
        copies = in_copies(idx, own_ref, held[:4], held[4:], wi_ref)
        start_all(copies, sems)
        wait_all(copies, sems)

    gn = dot(jnp.concatenate([g_ref[p] for p in range(3)], 1), wi_ref[...], 1, 1)
    hat, inv = norm_parts(x_ref[...].astype(f32))
    part = jnp.sum(gn * hat, axis=0, keepdims=True)

    @pl.when(pl.program_id(0) == 0)
    def _():
        gg_ref[...] = part

    @pl.when(pl.program_id(0) > 0)
    def _():
        gg_ref[...] += part

    ag_ref[...] = masked_ref[...].astype(f32) + norm_back(gn, hat, inv, gain_ref[...])


def input_backward(idx, held, own_in, g_mixed, x, masked, gain):
    length, width = masked.shape
    R = 512
    blk = rows_of(R, width)
    return call(
        norm_back_kernel,
        (length // R,),
        [ANY] * 9 + [pl.BlockSpec((3, R, width), lambda i, *_: (0, i, 0)),
                     pl.BlockSpec((None, R, width), lambda i, idx: (idx[2], i, 0)), blk, whole(gain.shape)],
        [blk, pl.BlockSpec((1, width), lambda *_: (0, 0))],
        [sds((length, width), f32), sds((1, width), f32)],
        [pltpu.VMEM((width, 3 * width), bf16), SEMS],
        (idx, *held, own_in, g_mixed, x, masked, gain),
        6 * length * width * width,
        2 * (7 * length * width + 3 * width * width),
        prefetch=1,
    )


def unpack_mlp_kernel(idx, all_ref, up, down, out):
    part = up.shape[0]
    q = up.shape[1] // 4
    h = down.shape[1] // 2
    r = part // 4
    for n in range(8):
        d, side = n // 2, n % 2
        cols = slice(side * h, side * h + h)
        down[d * part : (d + 1) * part, cols] = all_ref[n, 0:part].astype(f32)
        up[:, d * q + side * h : d * q + side * h + h] = all_ref[n, part : 2 * part].astype(f32)
        out[d * r : (d + 1) * r, cols] = all_ref[n, 2 * part :].astype(f32)


def unpack_mix_kernel(idx, *refs):
    held, (g_in, g_kern) = refs[:8], refs[8:]
    part, length = g_kern.shape
    width = 4 * part
    r = part // 4
    h = width // 2
    b = CH // 2
    for e in range(4):
        at = pl.ds(pl.multiple_of((idx[1] ^ e) * r, 16), r)
        for ref, side in ((held[e], idx[2]), (held[4 + e], 1 - idx[2])):
            for i in range(width // CH):
                for p in range(3):
                    c = i * h + p * b
                    g_in[at, pl.ds(pl.multiple_of(p * width + i * CH + side * b, 128), b)] = ref[:, c : c + b].astype(f32)
            g_kern[at, pl.ds(pl.multiple_of(side * (length // 2), 128), length // 2)] = ref[:, 3 * h :].astype(f32)


def unpack(kernel, idx, held, shapes):
    return call(
        kernel,
        (1,),
        [whole(h.shape) for h in held],
        [whole(s) for s in shapes],
        [sds(s, f32) for s in shapes],
        [],
        (idx, *held),
        0,
        sum(6 * math.prod(s) for s in shapes),
        prefetch=1,
    )


SWAP = [(0, 1), (1, 0)]


def shift(k):
    return [(i, (i + k) % 4) for i in range(4)]


def flip(e):
    return [(i, i ^ e) for i in range(4)]


def tie(value, *others):
    return lax.optimization_barrier((value, *others))[0]


def over_line(piece):
    return jnp.concatenate([lax.ppermute(piece, "chan", shift(k)) for k in SHIFTS], 0)


def over_plane(near):
    return [near] + [lax.ppermute(near, "dp", flip(e)) for e in (1, 2, 3)]


def over_chip(mine):
    return mine + [lax.ppermute(m, "section", SWAP) for m in mine]


def total(parts):
    out = parts[0].astype(f32)
    for p in parts[1:]:
        out += p.astype(f32)
    return out.astype(bf16)


def fold_plane(parts):
    return total([parts[0]] + [lax.ppermute(parts[e], "dp", flip(e)) for e in (1, 2, 3)])


def fold_line(held, z):
    def at(k):
        return lax.dynamic_index_in_dim(held, (z + k) % 4, 0, keepdims=False)

    return total([at(0)] + [lax.ppermute(at(k), "chan", shift(k)) for k in SHIFTS])


def cut(v, at, size, axis):
    return lax.dynamic_slice_in_dim(v, at, size, axis)


def fast_body(inputs, lengths, out_grad, ln_mix_gain, w_in, short_taps, long_taps, w_out, ln_mlp_gain, w_up, w_down):
    z, d, s = lax.axis_index("chan"), lax.axis_index("dp"), lax.axis_index("section")
    length = inputs.shape[2]
    width = inputs.shape[3]
    part = w_in.shape[1]
    ff = w_up.shape[2]
    half = width // 2
    hl = length // 2
    r = part // 4
    count = lax.dynamic_index_in_dim(lengths[:, 0], s, 0, keepdims=False)
    idx = jnp.stack([z, d, s, count]).astype(jnp.int32)
    x, og = inputs[:, 0], out_grad[:, 0]
    table = odd_basis(length)
    basis, back = jnp.asarray(table), jnp.asarray(np.ascontiguousarray(table.T))
    first = s == 0

    def after(parts, values):
        return lax.optimization_barrier((list(parts), list(values)))

    def both_cores(near, away):
        return total([near, lax.ppermute(away, "section", SWAP)])

    def stacked(own_first, own_second, other, dtype):
        keep = jnp.where(first, own_first, own_second).astype(dtype)
        other = other.astype(dtype)
        both = jnp.stack([jnp.where(first, keep, other), jnp.where(first, other, keep)])
        return both[None, :, None]

    def to_plane(parts):
        return [parts[0]] + [lax.ppermute(parts[e], "dp", flip(e)) for e in (1, 2, 3)]

    def line_sum(held):
        return lax.psum_scatter(held, "chan", scatter_dimension=0, tiled=False)

    own_in, own_out, own_up, own_down = w_in[0], w_out[0], w_up[0], w_down[0]
    own_taps = long_taps[0].T
    small = jnp.concatenate([ln_mix_gain, ln_mlp_gain, short_taps[0].reshape(9, part)], 0)
    own_small = jnp.pad(small.T, ((0, 0), (0, 128 - 11)))
    piece = jnp.concatenate([cut(own_taps, s * hl, hl, 1), own_small], 1)
    split = piece.shape[1]
    piece = jnp.concatenate([cut(piece, d * r, r, 0), cut(cut(own_in, d * r, r, 0), s * 3 * half, 3 * half, 1)], 1)
    near = over_line(piece)
    near_rest, near_in = near[:, :split], near[:, split:]
    plane_rest = over_plane(near_rest)
    plane_in = over_plane(near_in)
    piece_mlp = jnp.concatenate(
        [
            cut(cut(own_down, d * part, part, 0), s * half, half, 1),
            cut(own_up, s * (ff // 2) + d * (ff // 8), ff // 8, 1),
            cut(cut(own_out, d * r, r, 0), s * half, half, 1),
        ],
        0,
    )
    line_mlp = lax.all_gather(tie(piece_mlp, near), "chan", axis=0)
    held_rest = over_chip(plane_rest)

    plane_in, (spec, small, taps) = after(
        plane_in, kernel_spectra(idx, held_rest, tie(own_taps, near_in), own_small, basis)
    )
    held_in = over_chip(plane_in)
    gain_mix, gain_mlp = small[0:1], small[1:2]
    line_mlp = [lax.dynamic_index_in_dim(line_mlp, (z + 4 - k) % 4, 0, keepdims=False) for k in SHIFTS]
    near_up = jnp.concatenate([v[part:] for v in line_mlp], 0)
    near_down = jnp.concatenate([v[:part] for v in line_mlp], 0)
    plane_up = over_plane(near_up)
    plane_down = over_plane(near_down)
    plane_up, (normed0, mixed, qkv, sspec, conv, gated) = after(
        plane_up, mixer_front(idx, held_in, own_in, x, gain_mix, taps, tie(spec, near_up, near_down), basis, back)
    )
    held_up = over_chip(plane_up)
    act0, normed1 = mixer_out(idx, held_up, own_out, x, gated, gain_mlp)
    plane_down, (hidden, slope, near, away) = after(plane_down, mlp_up(idx, held_up, own_up, og, normed1))
    held_down = over_chip(plane_down)

    h_down = both_cores(near, away).reshape(4, 4, part, half)
    sent_down = [lax.dynamic_index_in_dim(h_down, d ^ e, 1, keepdims=False) for e in range(4)]
    got_down = to_plane(sent_down)
    got_down, (act1, ag1, branch0, g_gain_mlp, near, away, near_out, away_out) = after(
        got_down,
        mlp_down(
            idx, held_up, held_down, own_up, own_down, og, act0, normed1, hidden, tie(slope, *sent_down), gated, gain_mlp
        ),
    )
    h_up = both_cores(near, away).reshape(4, part, ff // 2)
    h_out = both_cores(near_out, away_out).reshape(4, 4, r, half)
    sent_up = [
        jnp.concatenate([cut(h_up, (d ^ e) * half, half, 2), lax.dynamic_index_in_dim(h_out, d ^ e, 1, keepdims=False)], 1)
        for e in range(4)
    ]
    got_up = to_plane(sent_up)

    branch_late = tie(branch0, *sent_up)
    got_up, (g_mixed, near, away, g_taps) = after(
        got_up,
        conv_backward(idx, held_up, own_out, branch_late, normed0, mixed, qkv, taps, conv, spec, sspec, basis, back),
    )
    u_mlp = jnp.concatenate([total(got_down), total(got_up)], 1)
    p_mlp = line_sum(u_mlp)
    h_mix = both_cores(near, away).reshape(4, 4, r, 3 * half + hl)
    sent_mix = [lax.dynamic_index_in_dim(h_mix, d ^ e, 1, keepdims=False) for e in range(4)]
    got_mix = to_plane(sent_mix)
    ag0, g_gain_mix = input_backward(idx, held_in, own_in, tie(g_mixed, u_mlp, *sent_mix), x, branch0, gain_mix)
    tiny = jnp.concatenate([g_gain_mix, g_gain_mlp, g_taps], 0)
    tiny += lax.ppermute(tiny, "section", SWAP)
    (*got_mix, p_mlp), (ag0, tiny) = after([*got_mix, p_mlp], [ag0, tiny])
    all_mlp = lax.all_gather(p_mlp, ("dp", "section"), axis=0)
    u_mix = total(got_mix)
    sent_line = [lax.dynamic_index_in_dim(u_mix, (z + k) % 4, 0, keepdims=False) for k in (0, *SHIFTS)]
    got_line = [sent_line[0]] + [lax.ppermute(v, "chan", shift(k)) for k, v in zip(SHIFTS, sent_line[1:])]
    tiny = tie(tiny, *sent_line)
    tiny += lax.ppermute(tiny, "dp", flip(1))
    ag0_late = tie(ag0, *sent_line)
    swapped = jnp.concatenate([jnp.where(first, act1, act0), jnp.where(first, ag1, ag0_late).astype(bf16)], 0)
    swapped = lax.ppermute(swapped, "section", SWAP)
    out_act = stacked(act0, act1, swapped[:length], bf16)
    out_ag = stacked(ag0_late, ag1, swapped[length:], f32)
    got_line, (tiny, out_act, out_ag) = after(got_line, [tiny, out_act, out_ag])
    g_up, g_down, g_out = unpack(unpack_mlp_kernel, idx, [all_mlp], [(part, ff), (4 * part, width), (part, width)])
    p_mix = total(got_line)
    plane_mix = over_plane(p_mix)
    tiny = tie(tiny, p_mix)
    tiny += lax.ppermute(tiny, "dp", flip(2))
    plane_mix, (tiny,) = after(plane_mix, [tiny])
    got_tiny = [lax.ppermute(tiny, "chan", flip(e)) for e in (1, 2, 3)]
    held_mix, (g_up, g_down, g_out) = after(over_chip(plane_mix), [g_up, g_down, g_out])
    g_in, g_kern = unpack(unpack_mix_kernel, idx, held_mix, [(part, 3 * width), (part, length)])
    got_tiny, (g_in, g_kern) = after(got_tiny, [g_in, g_kern])
    tiny = (tiny + got_tiny[0]) + (got_tiny[1] + got_tiny[2])

    mine = cut(tiny[0:2], z * part, part, 1)
    g_taps = tiny[2:11].reshape(3, 3, width).transpose(1, 0, 2).reshape(3, 3 * width)
    g_taps = cut(g_taps, z * 3 * part, 3 * part, 1)

    return (
        out_act,
        out_ag,
        mine[0:1],
        g_in[None],
        g_taps[None],
        g_kern.T[None],
        g_out[None],
        mine[1:2],
        g_up[None],
        g_down[None],
    )


def fits(mesh):
    return mesh.shape["chan"] == 4 and mesh.shape["dp"] == 4 and mesh.shape["section"] == 2


def shift_down(v, n):
    return jnp.pad(v, ((n, 0), (0, 0)))[: v.shape[0]]


def shift_up(v, n):
    return jnp.pad(v, ((0, n), (0, 0)))[n:]


def plain_body(inputs, lengths, out_grad, ln_mix_gain, w_in, short_taps, long_taps, w_out, ln_mlp_gain, w_up, w_down):
    own = lax.axis_index("section")
    length, width = inputs.shape[2:]
    position = lax.broadcasted_iota(jnp.int32, (length, 1), 0)
    x = lax.dynamic_index_in_dim(inputs[:, 0], own, 0, keepdims=False).astype(f32)
    og = lax.dynamic_index_in_dim(out_grad[:, 0], own, 0, keepdims=False)
    live = (position < lax.dynamic_index_in_dim(lengths[:, 0], own, 0, keepdims=False)).astype(f32)

    def rows(w):
        return lax.all_gather(w[0], "chan", axis=0, tiled=True)

    def cols(w):
        return lax.all_gather(w[0], "chan", axis=1, tiled=True)

    gain_mix = cols(ln_mix_gain[None])[0].astype(f32)
    gain_mlp = cols(ln_mlp_gain[None])[0].astype(f32)
    taps = cols(short_taps).astype(f32)
    kern = cols(long_taps).astype(f32)
    proj_in, proj_out, proj_up, proj_down = rows(w_in), rows(w_out), rows(w_up), rows(w_down)

    basis = jnp.asarray(odd_basis(length))
    decay = jnp.exp(-decay_rate * position.astype(f32))
    half = length

    def spectrum(v):
        both = dot(basis, v)
        return both[:half], both[half:]

    def back(cos_part, sin_part):
        return dot(basis, jnp.concatenate([cos_part, sin_part], 0).astype(bf16), 0, 0)

    kc, ks = spectrum((kern * decay).astype(bf16))
    kc, ks = kc / length, ks / length
    hat0, inv0 = norm_parts(x)
    normed0 = (hat0 * gain_mix).astype(bf16)
    mixed = dot(normed0, proj_in)
    smooth = taps[0] * mixed + taps[1] * shift_down(mixed, 1) + taps[2] * shift_down(mixed, 2)
    query, key, value = smooth[:, :width], smooth[:, width : 2 * width], smooth[:, 2 * width :]
    sc, ss = spectrum((key * value).astype(bf16))
    conv = back(sc * kc - ss * ks, sc * ks + ss * kc)
    gated = (query * conv).astype(bf16)
    act0 = (live * (x + dot(gated, proj_out))).astype(bf16)
    x1 = act0.astype(f32)
    hat1, inv1 = norm_parts(x1)
    normed1 = (hat1 * gain_mlp).astype(bf16)
    pre = dot(normed1, proj_up)
    cdf = 0.5 * (1.0 + lax.erf(pre * math.sqrt(0.5)))
    hidden = (pre * cdf).astype(bf16)
    act1 = (live * (x1 + dot(hidden, proj_down))).astype(bf16)
    masked1 = live * og.astype(f32)
    branch1 = masked1.astype(bf16)
    g_down = dot(hidden, branch1, 0, 0)
    slope = cdf + pre * (jnp.exp(-0.5 * pre * pre) * (1.0 / math.sqrt(2.0 * math.pi)))
    pre_grad = (slope * dot(branch1, proj_down, 1, 1)).astype(bf16)
    g_up = dot(normed1, pre_grad, 0, 0)
    gn1 = dot(pre_grad, proj_up, 1, 1)
    g_gain_mlp = jnp.sum(gn1 * hat1, axis=0)
    ag1 = masked1 + norm_back(gn1, hat1, inv1, gain_mlp)
    ag1_low = ag1.astype(bf16)
    masked0 = live * ag1_low.astype(f32)
    branch0 = masked0.astype(bf16)
    g_out = dot(gated, branch0, 0, 0)
    grad_gated = dot(branch0, proj_out, 1, 1)
    gc, gs = spectrum((grad_gated * query).astype(bf16))
    g_kern = back(sc * gc + ss * gs, sc * gs - ss * gc) * (decay / length)
    g_sig = back(kc * gc + ks * gs, kc * gs - ks * gc)
    g_smooth = jnp.concatenate([grad_gated * conv, g_sig * value, g_sig * key], 1)
    g_taps = jnp.stack([jnp.sum(g_smooth * shift_down(mixed, n), axis=0) if n else jnp.sum(g_smooth * mixed, axis=0) for n in range(3)])
    g_mixed = (taps[0] * g_smooth + taps[1] * shift_up(g_smooth, 1) + taps[2] * shift_up(g_smooth, 2)).astype(bf16)
    g_in = dot(normed0, g_mixed, 0, 0)
    gn0 = dot(g_mixed, proj_in, 1, 1)
    g_gain_mix = jnp.sum(gn0 * hat0, axis=0)
    ag0 = masked0 + norm_back(gn0, hat0, inv0, gain_mix)

    swap = [(0, 1), (1, 0)]
    first = own == 0

    def exchange(own_first, own_second, dtype):
        keep = jnp.where(first, own_first, own_second).astype(dtype)
        other = lax.ppermute(jnp.where(first, own_second, own_first).astype(bf16), "section", swap).astype(dtype)
        both = jnp.stack([jnp.where(first, keep, other), jnp.where(first, other, keep)])
        return both[None, :, None]

    def reduced(g, dim):
        part = lax.psum_scatter(g.astype(bf16), "chan", scatter_dimension=dim, tiled=True)
        return lax.psum(part, ("section", "dp")).astype(f32)[None]

    return (
        exchange(act0, act1, bf16),
        exchange(ag0, ag1, f32),
        reduced(g_gain_mix, 0),
        reduced(g_in, 0),
        reduced(g_taps, 1),
        reduced(g_kern, 1),
        reduced(g_out, 0),
        reduced(g_gain_mlp, 0),
        reduced(g_up, 0),
        reduced(g_down, 0),
    )


def solution(mesh):
    return jax.shard_map(
        fast_body if fits(mesh) else plain_body,
        mesh=mesh,
        in_specs=(
            P(None, ("dp", "chan"), None, None),
            P(None, ("dp", "chan")),
            P(None, ("dp", "chan"), None, None),
            P(None, "chan"),
            P(None, "chan", None),
            P(None, None, "chan"),
            P(None, None, "chan"),
            P(None, "chan", None),
            P(None, "chan"),
            P(None, "chan", None),
            P(None, "chan", None),
        ),
        out_specs=(
            P("section", None, ("dp", "chan"), None, None),
            P("section", None, ("dp", "chan"), None, None),
            P(None, "chan"),
            P(None, "chan", None),
            P(None, None, "chan"),
            P(None, None, "chan"),
            P(None, "chan", None),
            P(None, "chan"),
            P(None, "chan", None),
            P(None, "chan", None),
        ),
        check_vma=False,
    )
```

```python
import math

import jax
import jax.numpy as jnp
import ml_dtypes
import numpy as np
from jax import lax
from jax.experimental import pallas as pl
from jax.experimental.pallas import tpu as pltpu
from jax.sharding import PartitionSpec as P

decay_rate = 0.003
bf16 = jnp.bfloat16
f32 = jnp.float32
MIB = 1 << 20


def odd_basis(length):
    phase = (2 * np.arange(length)[:, None] + 1) * np.arange(length)[None, :] % (4 * length)
    angle = phase * (math.pi / (2 * length))
    return np.concatenate([np.cos(angle), np.sin(angle)], 0).astype(ml_dtypes.bfloat16)


def dot(a, b, ca=1, cb=0):
    return lax.dot_general(a, b, (((ca,), (cb,)), ((), ())), preferred_element_type=f32)


def norm_parts(values):
    centered = values - jnp.mean(values, axis=-1, keepdims=True)
    spread = jnp.mean(centered * centered, axis=-1, keepdims=True)
    inv = lax.rsqrt(spread + 1e-05)
    return centered * inv, inv


def norm_back(grad_normed, hat, inv, gain):
    grad_hat = grad_normed * gain
    return inv * (
        grad_hat
        - jnp.mean(grad_hat, axis=-1, keepdims=True)
        - hat * jnp.mean(grad_hat * hat, axis=-1, keepdims=True)
    )


def call(kernel, grid, in_specs, out_specs, out_shape, scratch, args, flops, nbytes, limit=56, prefetch=0):
    spec = pltpu.PrefetchScalarGridSpec(
        num_scalar_prefetch=prefetch, grid=grid, in_specs=in_specs, out_specs=out_specs, scratch_shapes=scratch
    )
    return pl.pallas_call(
        kernel,
        grid_spec=spec,
        out_shape=out_shape,
        compiler_params=pltpu.CompilerParams(
            dimension_semantics=("arbitrary",) * len(grid), vmem_limit_bytes=limit * MIB
        ),
        cost_estimate=pl.CostEstimate(flops=flops, bytes_accessed=nbytes, transcendentals=0),
    )(*args)


def whole(shape):
    return pl.BlockSpec(shape, lambda *_: (0,) * len(shape), pipeline_mode=pl.Buffered(1))


def rows_of(r, c):
    return pl.BlockSpec((r, c), lambda i, *_: (i, 0))


def cols_of(r, c, start=0):
    return pl.BlockSpec((r, c), lambda i, *_: (0, i + start))


def sds(shape, dtype):
    return jax.ShapeDtypeStruct(shape, dtype)


ANY = pl.BlockSpec(memory_space=pl.ANY)
SHIFTS = (1, 3, 2)


def start_all(copies, sems):
    for n, (a, b) in enumerate(copies):
        pltpu.make_async_copy(a, b, sems.at[n]).start()


def wait_all(copies, sems):
    for n, (a, b) in enumerate(copies):
        pltpu.make_async_copy(a, b, sems.at[n]).wait()


def sources(idx, mine, other):
    z, d, s = idx[0], idx[1], idx[2]
    for e in range(4):
        for j, k in enumerate(SHIFTS):
            for ref, side in ((mine[e], s), (other[e], 1 - s)):
                yield ref, j, lax.rem(z + 4 - k, 4), d ^ e, side


def in_copies(idx, own, mine, other, dst):
    part, half = own.shape[0], own.shape[1] // 2
    r = part // 4
    out = [(own, dst.at[pl.ds(pl.multiple_of(idx[0] * part, 16), part), :])]
    for ref, j, z, d, side in sources(idx, mine, other):
        out.append((ref.at[pl.ds(j * r, r), :],
                    dst.at[pl.ds(pl.multiple_of(z * part + d * r, 16), r), pl.ds(pl.multiple_of(side * half, 128), half)]))
    return out


def up_copies(idx, own, mine, other, dst):
    part, ff = own.shape
    c = ff // 8
    step = part + part // 4
    out = [(own, dst.at[pl.ds(pl.multiple_of(idx[0] * part, 16), part), :])]
    for ref, j, z, d, side in sources(idx, mine, other):
        out.append((ref.at[pl.ds(j * step, part), :],
                    dst.at[pl.ds(pl.multiple_of(z * part, 16), part), pl.ds(pl.multiple_of(side * 4 * c + d * c, 128), c)]))
    return out


def down_copies(idx, own, mine, other, dst):
    q, width = own.shape
    r = q // 4
    h = width // 2
    out = [(own, dst.at[pl.ds(pl.multiple_of(idx[0] * q, 16), q), :])]
    for ref, j, z, d, side in sources(idx, mine, other):
        out.append((ref.at[pl.ds(j * r, r), :],
                    dst.at[pl.ds(pl.multiple_of(z * q + d * r, 16), r), pl.ds(pl.multiple_of(side * h, 128), h)]))
    return out


def out_copies(idx, own, mine, other, dst):
    part, width = own.shape
    r = part // 4
    h = width // 2
    out = [(own, dst.at[pl.ds(pl.multiple_of(idx[0] * part, 16), part), :])]
    for ref, j, z, d, side in sources(idx, mine, other):
        out.append((ref.at[pl.ds(j * 5 * r + part, r), :],
                    dst.at[pl.ds(pl.multiple_of(z * part + d * r, 16), r), pl.ds(pl.multiple_of(side * h, 128), h)]))
    return out


def rest_copies(idx, own, mine, other, dst, start, half):
    part = own.shape[0]
    r = part // 4
    out = [(own, dst.at[pl.ds(pl.multiple_of(idx[0] * part, 16), part), :])]
    for ref, j, z, d, side in sources(idx, mine, other):
        out.append((ref.at[pl.ds(j * r, r), pl.ds(start, half)],
                    dst.at[pl.ds(pl.multiple_of(z * part + d * r, 16), r), pl.ds(pl.multiple_of(side * half, 128), half)]))
    return out


SEMS = pltpu.SemaphoreType.DMA((25,))


CH = 256


def spectra_kernel(idx, *refs):
    held, (own_taps, own_small, basis_in, out_ref, small_ref, taps_ref, taps, small, tall, sig, basis_ref, sems, sems2, sem_b) = refs[:8], refs[8:]
    mine, other = held[:4], held[4:]
    length = taps.shape[1]

    @pl.when(pl.program_id(0) == 0)
    def _():
        copies = rest_copies(idx, own_taps, mine, other, taps, REST_TAPS, length // 2)
        part = own_small.shape[0]
        r = part // 4
        copies2 = [(own_small, small.at[pl.ds(pl.multiple_of(idx[0] * part, 16), part), :])]
        for e in range(4):
            for j, k in enumerate(SHIFTS):
                z = lax.rem(idx[0] + 4 - k, 4)
                copies2.append((mine[e].at[pl.ds(j * r, r), pl.ds(REST_SMALL, 128)],
                                small.at[pl.ds(pl.multiple_of(z * part + (idx[1] ^ e) * r, 16), r), :]))
        start_all(copies2, sems2)
        start_all(copies, sems)
        start_all([(basis_in, basis_ref)], sem_b)
        wait_all(copies2, sems2)
        wide = small[...].astype(f32)
        small_ref[...] = wide.T[0:8]
        for z in range(4):
            for q in range(3):
                tall[(3 * z + q) * part : (3 * z + q + 1) * part] = pltpu.roll(wide[z * part : (z + 1) * part], 126 - q, 1)
        taps_ref[...] = tall[...].T[0:8]
        wait_all(copies, sems)
        wait_all([(basis_in, basis_ref)], sem_b)

    position = lax.broadcasted_iota(jnp.int32, (1, length), 1).astype(f32)
    rows = pl.ds(pl.multiple_of(pl.program_id(0) * CH, CH), CH)
    sig[...] = (taps[rows, :].astype(f32) * (jnp.exp(-decay_rate * position) / length)).astype(bf16)
    out_ref[...] = dot(basis_ref[...], sig[...], 1, 1).astype(bf16)


REST_TAPS, REST_SMALL = 0, 512


def kernel_spectra(idx, rest, own_taps, own_small, basis):
    length = own_taps.shape[1]
    width = own_taps.shape[0] * 4
    return call(
        spectra_kernel,
        (width // CH,),
        [ANY] * 11,
        [cols_of(2 * length, CH), whole((8, width)), whole((8, 3 * width))],
        [sds((2 * length, width), bf16), sds((8, width), f32), sds((8, 3 * width), f32)],
        [pltpu.VMEM((width, length), bf16), pltpu.VMEM((width, 128), bf16), pltpu.VMEM((3 * width, 128), f32), pltpu.VMEM((CH, length), bf16),
         pltpu.VMEM(basis.shape, bf16), SEMS, SEMS, pltpu.SemaphoreType.DMA((1,))],
        (idx, *rest, own_taps, own_small, basis),
        4 * length * length * width,
        basis.size * 2 + 6 * length * width,
        prefetch=1,
    )


class Mover:
    def __init__(self, sems):
        self.sems, self.used = sems, 0

    def start(self, src, dst):
        copy = pltpu.make_async_copy(src, dst, self.sems.at[self.used])
        self.used += 1
        copy.start()
        return copy

    def pieces(self, pairs):
        return [self.start(a, b) for a, b in pairs]


def settle(*copies):
    for c in copies:
        if isinstance(c, list):
            settle(*c)
        else:
            c.wait()


def manual(kernel, n_in, vmem_in, out_shapes, out_specs, scratch, sems, args, flops, nbytes):
    return call(
        kernel,
        (1,),
        [ANY] * n_in + [whole(v.shape) for v in vmem_in],
        out_specs,
        out_shapes,
        [*scratch, pltpu.SemaphoreType.DMA((sems,))],
        (*args, *vmem_in),
        flops,
        nbytes,
        limit=60,
        prefetch=1,
    )


def blocks_of(i):
    return slice(i * CH, (i + 1) * CH)


def front_kernel(idx, *refs):
    held, (own, x_in, spec_in, basis_in, back_in, gain, taps, normed_o, m_o, qkv_o, sspec_o, conv_o, gated_o,
           x_s, w_s, spec_s, basis_s, back_s, normed_s, m_s, qkv_s, sspec_s, conv_s, gated_s,
           pad0, pad1, sig_s, s0, s1, y0, y1, sems) = refs[:8], refs[8:]
    pads, s_s, y_s = (pad0, pad1), (s0, s1), (y0, y1)
    length, width = x_s.shape
    R = 256
    go = Mover(sems)
    x_c = go.start(x_in.at[idx[2]], x_s)
    w_c = go.pieces(in_copies(idx, own, held[:4], held[4:], w_s))
    sent = []
    for p in pads:
        p[0:8] = jnp.zeros((8, 3 * CH), f32)
    settle(x_c)
    for r in range(0, length, R):
        hat, _ = norm_parts(x_s[r : r + R].astype(f32))
        normed_s[r : r + R] = (hat * gain[...]).astype(bf16)
    settle(w_c)
    basis_c = go.start(basis_in, basis_s)

    def mix(i):
        w = jnp.concatenate([w_s[:, p * width + i * CH : p * width + (i + 1) * CH] for p in range(3)], 1)
        pads[i % 2][8:] = dot(normed_s[...], w)

    def smooth(i):
        pad = pads[i % 2]
        for r in range(0, length, R):
            now = []
            for p in range(3):
                c = blocks_of(p)
                g = slice(p * width + i * CH, p * width + (i + 1) * CH)
                m_s[p, r : r + R, blocks_of(i)] = pad[8 + r : 8 + r + R, c].astype(bf16)
                now.append(taps[0:1, g] * pad[8 + r : 8 + r + R, c] + taps[3:4, g] * pad[7 + r : 7 + r + R, c]
                           + taps[6:7, g] * pad[6 + r : 6 + r + R, c])
                qkv_s[p, r : r + R, blocks_of(i)] = now[p].astype(bf16)
            sig_s[r : r + R, blocks_of(i)] = (now[1] * now[2]).astype(bf16)
        sent.append(go.start(m_s.at[:, :, blocks_of(i)], m_o.at[:, :, blocks_of(i)]))
        sent.append(go.start(qkv_s.at[:, :, blocks_of(i)], qkv_o.at[:, :, blocks_of(i)]))

    def forth(i):
        s_s[i % 2][...] = dot(basis_s[...], sig_s[:, blocks_of(i)])

    def times(i):
        c = blocks_of(i)
        for r in range(0, length, R):
            at, lo = slice(r, r + R), slice(length + r, length + r + R)
            sc, ss = s_s[i % 2][at], s_s[i % 2][lo]
            sspec_s[at, c] = sc.astype(bf16)
            sspec_s[lo, c] = ss.astype(bf16)
            kc, ks = spec_s[at, c].astype(f32), spec_s[lo, c].astype(f32)
            y_s[i % 2][at] = (sc * kc - ss * ks).astype(bf16)
            y_s[i % 2][lo] = (sc * ks + ss * kc).astype(bf16)
        sent.append(go.start(sspec_s.at[:, c], sspec_o.at[:, c]))

    def back(i):
        c = blocks_of(i)
        conv = dot(back_s[...], y_s[i % 2][...])
        conv_s[:, c] = conv.astype(bf16)
        gated_s[:, c] = (qkv_s[0, :, c].astype(f32) * conv).astype(bf16)
        sent.append(go.start(conv_s.at[:, c], conv_o.at[:, c]))
        sent.append(go.start(gated_s.at[:, c], gated_o.at[:, c]))

    mix(0)
    mix(1)
    settle(basis_c)
    spec_c = go.start(spec_in, spec_s)
    smooth(0)
    forth(0)
    mix(2)
    settle(spec_c)
    back_c = go.start(back_in, back_s)
    sent.append(go.start(normed_s, normed_o))
    smooth(1)
    times(0)
    forth(1)
    settle(back_c)
    back(0)
    smooth(2)
    times(1)
    forth(2)
    back(1)
    times(2)
    back(2)
    settle(sent)


def mixer_front(idx, held, own_in, x, gain, taps, spec, basis, back):
    length, width = x.shape[1:]
    V = pltpu.VMEM
    low, three, tall = (length, width), (3, length, width), (2 * length, width)
    outs = [low, three, three, tall, low, low]
    return manual(
        front_kernel,
        13,
        (gain, taps),
        [sds(s, bf16) for s in outs],
        [ANY] * 6,
        [V(s, bf16) for s in (low, (width, 3 * width), tall, basis.shape, back.shape, *outs)]
        + [V((length + 8, 3 * CH), f32)] * 2 + [V(low, bf16)] + [V((2 * length, CH), f32)] * 2 + [V((2 * length, CH), bf16)] * 2,
        48,
        (idx, *held, own_in, x, spec, basis, back),
        6 * length * width * width + 8 * length * length * width,
        2 * (16 * length * width + 3 * width * width + 2 * basis.size),
    )


def gelu_parts(pre):
    cdf = 0.5 * (1.0 + lax.erf(pre * math.sqrt(0.5)))
    slope = cdf + pre * (jnp.exp(-0.5 * pre * pre) * (1.0 / math.sqrt(2.0 * math.pi)))
    return pre * cdf, slope


def live_rows(idx, rows, start=0):
    return (lax.broadcasted_iota(jnp.int32, (rows, 1), 0) + start < idx[3]).astype(f32)


def near_first(idx, ref, half):
    return (pl.ds(pl.multiple_of(idx[2] * half, 128), half), pl.ds(pl.multiple_of((1 - idx[2]) * half, 128), half))


def out_kernel(idx, *refs):
    rest, (own_out, x_ref, gated_ref, gain_ref, act0_ref, normed_ref, wo_ref, sem_o) = refs[:8], refs[8:]
    R, width = x_ref.shape
    start = pl.program_id(0) * R

    @pl.when(pl.program_id(0) == 0)
    def _():
        outs = out_copies(idx, own_out, rest[:4], rest[4:], wo_ref)
        start_all(outs, sem_o)
        wait_all(outs, sem_o)

    live = live_rows(idx, R, start)
    act0 = (live * (x_ref[...].astype(f32) + dot(gated_ref[...], wo_ref[...]))).astype(bf16)
    act0_ref[...] = act0
    hat, _ = norm_parts(act0.astype(f32))
    normed_ref[...] = (hat * gain_ref[...]).astype(bf16)


def mixer_out(idx, rest, own_out, x, gated, gain):
    length, width = gated.shape
    R = 512
    blk = rows_of(R, width)
    return call(
        out_kernel,
        (length // R,),
        [ANY] * 9 + [pl.BlockSpec((None, R, width), lambda i, idx: (idx[2], i, 0)), blk, whole(gain.shape)],
        [blk, blk],
        [sds((length, width), bf16)] * 2,
        [pltpu.VMEM((width, width), bf16), SEMS],
        (idx, *rest, own_out, x, gated, gain),
        2 * length * width * width,
        2 * (4 * length * width + width * width),
        prefetch=1,
    )


def up_kernel(idx, *refs):
    held, (own_up, og_ref, normed_ref, hidden_ref, slope_ref, near_ref, away_ref, wu_ref, turned, sem_u) = refs[:8], refs[8:]
    length, width = og_ref.shape
    half = width // 2
    c = pl.program_id(0)

    @pl.when(c == 0)
    def _():
        ups = up_copies(idx, own_up, held[:4], held[4:], wu_ref)
        start_all(ups, sem_u)
        live = live_rows(idx, length)
        for n, cols in enumerate(near_first(idx, og_ref, half)):
            turned[:, n * half : (n + 1) * half] = (live * og_ref[:, cols].astype(f32)).astype(bf16)
        wait_all(ups, sem_u)

    at = pl.ds(pl.multiple_of(c * width, width), width)
    hid, slope = gelu_parts(dot(normed_ref[...], wu_ref[:, at]))
    hid = hid.astype(bf16)
    hidden_ref[...] = hid
    slope_ref[...] = slope.astype(bf16)
    grad = dot(hid, turned[...], 0, 0).astype(bf16)
    near_ref[...] = grad[:, :half]
    away_ref[...] = grad[:, half:]


def mlp_up(idx, held, own_up, og, normed):
    length, width = normed.shape
    ff = own_up.shape[1]
    half = width // 2
    wide = cols_of(length, width)
    picked = pl.BlockSpec((None, length, width), lambda i, idx: (idx[2], 0, 0), pipeline_mode=pl.Buffered(1))
    return call(
        up_kernel,
        (ff // width,),
        [ANY] * 9 + [picked, whole((length, width))],
        [wide, wide, rows_of(width, half), rows_of(width, half)],
        [sds((length, ff), bf16), sds((length, ff), bf16), sds((ff, half), bf16), sds((ff, half), bf16)],
        [pltpu.VMEM((width, ff), bf16), pltpu.VMEM((length, width), bf16), SEMS],
        (idx, *held, own_up, og, normed),
        4 * length * width * ff,
        2 * (2 * length * width + 2 * width * ff + 2 * length * ff),
        prefetch=1,
    )


def down_kernel(idx, *refs):
    held, (own_up, own_down, act0_in, normed_in, gated_in, og_ref, slope_ref, gain_ref,
           ag_ref, branch_ref, gg_ref, near_ref, away_ref, near_out, away_out,
           wu_ref, wd_ref, gn, branch, turned, act0_ref, normed_ref, gated_ref, sem_u, sem_d, sem_l, sem_m) = refs[:16], refs[16:]
    length, width = og_ref.shape
    half = width // 2
    c = pl.program_id(0)
    live = live_rows(idx, length)
    ups = up_copies(idx, own_up, held[:4], held[4:8], wu_ref)
    late = [(normed_in, normed_ref), (act0_in, act0_ref), (gated_in, gated_ref)]

    @pl.when(c == 0)
    def _():
        downs = down_copies(idx, own_down, held[8:12], held[12:], wd_ref)
        start_all(downs, sem_d)
        branch[...] = (live * og_ref[...].astype(f32)).astype(bf16)
        gn[...] = jnp.zeros((length, width), f32)
        wait_all(downs, sem_d)
        start_all(ups, sem_u)
        start_all(late[:1], sem_l)

    at = pl.ds(pl.multiple_of(c * width, width), width)
    pre = (slope_ref[...].astype(f32) * dot(branch[...], wd_ref[at, :], 1, 1)).astype(bf16)
    for n, cols in enumerate(near_first(idx, turned, half)):
        turned[:, cols] = pre[:, n * half : (n + 1) * half]

    @pl.when(c == 0)
    def _():
        wait_all(ups, sem_u)
        wait_all(late[:1], sem_l)
        start_all(late[1:], sem_m)

    gn[...] += dot(pre, wu_ref[:, at], 1, 1)
    grad = dot(normed_ref[...], turned[...], 0, 0).astype(bf16)
    near_ref[...] = grad[:, :half]
    away_ref[...] = grad[:, half:]

    @pl.when(c == pl.num_programs(0) - 1)
    def _():
        wait_all(late[1:], sem_m)
        hat, inv = norm_parts(act0_ref[...].astype(f32))
        gg_ref[...] = jnp.sum(gn[...] * hat, axis=0, keepdims=True)
        ag = live * og_ref[...].astype(f32) + norm_back(gn[...], hat, inv, gain_ref[...])
        ag_ref[...] = ag
        branch_ref[...] = (live * ag).astype(bf16)
        for n, cols in enumerate(near_first(idx, branch_ref, half)):
            turned[:, n * half : (n + 1) * half] = branch_ref[:, cols]
        g_out = dot(gated_ref[...], turned[...], 0, 0).astype(bf16)
        near_out[...] = g_out[:, :half]
        away_out[...] = g_out[:, half:]


def mlp_down(idx, held_up, held_down, own_up, own_down, og, act0, normed, slope, gated, gain):
    length, width = act0.shape
    ff = own_up.shape[1]
    half = width // 2
    picked = pl.BlockSpec((None, length, width), lambda i, idx: (idx[2], 0, 0), pipeline_mode=pl.Buffered(1))
    one = whole((length, width))
    wide = cols_of(length, width)
    full = sds((length, width), bf16)
    col = pltpu.VMEM((length, width), f32)
    low = pltpu.VMEM((length, width), bf16)
    return call(
        down_kernel,
        (ff // width,),
        [ANY] * 21 + [picked, wide, whole(gain.shape)],
        [one, one, whole((1, width)), cols_of(width, half), cols_of(width, half), whole((width, half)), whole((width, half))],
        [sds((length, width), f32), full, sds((1, width), f32), sds((width, ff // 2), bf16), sds((width, ff // 2), bf16),
         sds((width, half), bf16), sds((width, half), bf16)],
        [pltpu.VMEM((width, ff), bf16), pltpu.VMEM((ff, width), bf16), col, low, low, low, low, low, SEMS, SEMS,
         pltpu.SemaphoreType.DMA((1,)), pltpu.SemaphoreType.DMA((2,))],
        (idx, *held_up, *held_down, own_up, own_down, act0, normed, gated, og, slope, gain),
        6 * length * width * ff,
        2 * (7 * length * width + 3 * width * ff + length * ff),
        prefetch=1,
    )


def last_kernel(idx, *refs):
    held, (own_down, hidden_ref, act0_ref, act1_ref, wd_ref, acc, sem_d) = refs[:8], refs[8:]
    length, width = act0_ref.shape
    c = pl.program_id(0)

    @pl.when(c == 0)
    def _():
        downs = down_copies(idx, own_down, held[:4], held[4:], wd_ref)
        start_all(downs, sem_d)
        acc[...] = act0_ref[...].astype(f32)
        wait_all(downs, sem_d)

    acc[...] += dot(hidden_ref[...], wd_ref[pl.ds(pl.multiple_of(c * width, width), width), :])

    @pl.when(c == pl.num_programs(0) - 1)
    def _():
        act1_ref[...] = (live_rows(idx, length) * acc[...]).astype(bf16)


def mlp_last(idx, held, own_down, hidden, act0):
    length, width = act0.shape
    ff = own_down.shape[0] * 4
    one = whole((length, width))
    return call(
        last_kernel,
        (ff // width,),
        [ANY] * 9 + [cols_of(length, width), one],
        one,
        sds((length, width), bf16),
        [pltpu.VMEM((ff, width), bf16), pltpu.VMEM((length, width), f32), SEMS],
        (idx, *held, own_down, hidden, act0),
        2 * length * width * ff,
        2 * (2 * length * width + width * ff + length * ff),
        prefetch=1,
    )


def conv_back_kernel(idx, *refs):
    held, (own_out, branch_in, normed_in, m_in, qkv_in, conv_in, spec_in, sspec_in, basis_in, back_in, taps,
           g_o, near_o, away_o, gtaps_ref,
           w_s, branch_s, normed_s, m_s, qkv_s, conv_s, spec_s, sspec_s, basis_s, back_s,
           gpad0, gpad1, sig_s, s0, s1, y0, y1, both_s, gm0, gm1, g0_s, g1_s, kern0, kern1, near0, near1, away0, away1,
           sems) = refs[:8], refs[8:]
    gpads, s_s, y_s, gms, g_s, kerns, near_s, away_s = ((gpad0, gpad1), (s0, s1), (y0, y1), (gm0, gm1), (g0_s, g1_s),
                                                        (kern0, kern1), (near0, near1), (away0, away1))
    length, width = branch_s.shape
    half = width // 2
    hl = length // 2
    R = 256
    nb = width // CH
    go = Mover(sems)
    branch_c = go.start(branch_in, branch_s)
    w_c = go.pieces(out_copies(idx, own_out, held[:4], held[4:], w_s))
    basis_c = go.start(basis_in, basis_s)

    def fetch(i):
        c = blocks_of(i)
        return [go.start(qkv_in.at[:, :, c], qkv_s.at[:, :, c]), go.start(conv_in.at[:, c], conv_s.at[:, c])]

    def fetch_spectra(i):
        c = blocks_of(i)
        return [go.start(spec_in.at[:, c], spec_s.at[:, c]), go.start(sspec_in.at[:, c], sspec_s.at[:, c])]

    def fetch_mixed(i):
        c = blocks_of(i)
        return go.start(m_in.at[:, :, c], m_s.at[:, :, c])

    for p in gpads:
        p[length : length + 8] = jnp.zeros((8, 3 * CH), f32)
    sent = [[], []]
    settle(branch_c, w_c)
    first_c = fetch(0)

    def spread_back(i):
        s_s[i % 2][0:length] = dot(branch_s[...], w_s[blocks_of(i), :], 1, 1)

    def gate(i):
        c = blocks_of(i)
        for r in range(0, length, R):
            at = slice(r, r + R)
            gg = s_s[i % 2][at]
            sig_s[at, c] = (gg * qkv_s[0, at, c].astype(f32)).astype(bf16)
            gpads[i % 2][at, 0:CH] = gg * conv_s[at, c].astype(f32)

    def forth(i):
        s_s[i % 2][...] = dot(basis_s[...], sig_s[:, blocks_of(i)])

    def times(i):
        c = blocks_of(i)
        y = y_s[i % 2]
        for r in range(0, length, R):
            at, lo = slice(r, r + R), slice(length + r, length + r + R)
            gc, gs = s_s[i % 2][at], s_s[i % 2][lo]
            kc, ks = spec_s[at, c].astype(f32), spec_s[lo, c].astype(f32)
            y[at, 0:CH] = (kc * gc + ks * gs).astype(bf16)
            y[lo, 0:CH] = (kc * gs - ks * gc).astype(bf16)
            sc, ss = sspec_s[at, c].astype(f32), sspec_s[lo, c].astype(f32)
            y[at, CH:] = (sc * gc + ss * gs).astype(bf16)
            y[lo, CH:] = (sc * gs - ss * gc).astype(bf16)

    def back(i):
        both_s[...] = dot(back_s[...], y_s[i % 2][...])

    def unsmooth(i):
        b = blocks_of(i)
        gpad, gm, kern = gpads[i % 2], gms[i % 2], kerns[i % 2]
        settle(sent[i % 2])
        for r in range(0, length, R):
            at = slice(r, r + R)
            g_sig = both_s[at, :CH]
            gpad[at, CH : 2 * CH] = g_sig * qkv_s[2, at, b].astype(f32)
            gpad[at, 2 * CH :] = g_sig * qkv_s[1, at, b].astype(f32)
            position = (lax.broadcasted_iota(jnp.int32, (R, 1), 0) + r).astype(f32)
            kern[:, at] = (both_s[at, CH:] * (jnp.exp(-decay_rate * position) / length)).T.astype(bf16)
        sums = [[jnp.zeros((1, CH), f32)] * 3 for _ in range(3)]
        for r in range(0, length, R):
            at = slice(r, r + R)
            for p in range(3):
                c = blocks_of(p)
                t = slice(p * width + i * CH, p * width + (i + 1) * CH)
                now = [gpad[r + n : r + n + R, c] for n in range(3)]
                g = (taps[0:1, t] * now[0] + taps[3:4, t] * now[1] + taps[6:7, t] * now[2]).astype(bf16)
                g_s[i % 2][p, at] = g
                for n in range(2):
                    to = jnp.where(idx[2] == n, 0, half) + p * (CH // 2)
                    gm[at, pl.ds(pl.multiple_of(to, 128), CH // 2)] = g[:, n * (CH // 2) : (n + 1) * (CH // 2)]
                mixed = m_s[p, at, b].astype(f32)
                sums[p] = [sums[p][n] + jnp.sum(now[n] * mixed, axis=0, keepdims=True) for n in range(3)]
        for p in range(3):
            for n in range(3):
                gtaps_ref[3 * p + n : 3 * p + n + 1, b] = sums[p][n]
        side = slice(3 * half, 3 * half + hl)
        mine, other = near_first(idx, kern, hl)
        sent[i % 2] = [go.start(g_s[i % 2], g_o.at[:, :, b]), go.start(kern.at[:, mine], near_o.at[b, side]),
                       go.start(kern.at[:, other], away_o.at[b, side])]

    def grad(i):
        g = dot(normed_s[...], gms[i % 2][...], 0, 0).astype(bf16)
        near_s[i % 2][...] = g[:, :half]
        away_s[i % 2][...] = g[:, half:]
        c = slice(i * half, (i + 1) * half)
        sent[i % 2] += [go.start(near_s[i % 2], near_o.at[:, c]), go.start(away_s[i % 2], away_o.at[:, c])]

    spread_back(0)
    spread_back(1)
    settle(basis_c, first_c)
    spectra_c = fetch_spectra(0)
    gate(0)
    forth(0)
    settle(spectra_c)
    back_c = go.start(back_in, back_s)
    next_c = fetch(1)
    times(0)
    settle(next_c, back_c)
    spectra_c = fetch_spectra(1)
    mixed_c = fetch_mixed(0)
    normed_c = go.start(normed_in, normed_s)
    back(0)
    gate(1)
    forth(1)
    spread_back(2)
    settle(spectra_c, mixed_c, normed_c)
    next_c = fetch(2)
    mixed_c = fetch_mixed(1)
    spectra_c = fetch_spectra(2)
    unsmooth(0)
    times(1)
    back(1)
    grad(0)
    settle(next_c, mixed_c, spectra_c)
    mixed_c = fetch_mixed(2)
    gate(2)
    forth(2)
    unsmooth(1)
    times(2)
    grad(1)
    back(2)
    settle(mixed_c)
    unsmooth(2)
    grad(2)
    settle(sent)


def conv_backward(idx, held, own_out, branch, normed, mixed, qkv, taps, conv, spec, sspec, basis, back):
    length, width = branch.shape
    half = width // 2
    mix = (width, 3 * half + length // 2)
    V = pltpu.VMEM
    low, three, tall = (length, width), (3, length, width), (2 * length, width)
    twice = lambda s, t: [V(s, t)] * 2
    return manual(
        conv_back_kernel,
        18,
        (taps,),
        [sds(three, bf16), sds(mix, bf16), sds(mix, bf16), sds((9, width), f32)],
        [ANY] * 3 + [whole((9, width))],
        [V(s, bf16) for s in ((width, width), low, low, three, three, low, tall, tall, basis.shape, back.shape)]
        + twice((length + 8, 3 * CH), f32) + [V(low, bf16)] + twice((2 * length, CH), f32) + twice((2 * length, 2 * CH), bf16)
        + [V((length, 2 * CH), f32)] + twice((length, 3 * CH), bf16) + twice((3, length, CH), bf16) + twice((CH, length), bf16)
        + twice((width, half), bf16) + twice((width, half), bf16),
        64,
        (idx, *held, own_out, branch, normed, mixed, qkv, conv, spec, sspec, basis, back),
        8 * length * width * width + 12 * length * length * width,
        2 * (22 * length * width + 2 * basis.size + 2 * mix[0] * mix[1]),
    )


def norm_back_kernel(idx, *refs):
    held, (own_ref, g_ref, x_ref, masked_ref, gain_ref, ag_ref, gg_ref, wi_ref, sems) = refs[:8], refs[8:]
    width = x_ref.shape[1]

    @pl.when(pl.program_id(0) == 0)
    def _():
        copies = in_copies(idx, own_ref, held[:4], held[4:], wi_ref)
        start_all(copies, sems)
        wait_all(copies, sems)

    gn = dot(jnp.concatenate([g_ref[p] for p in range(3)], 1), wi_ref[...], 1, 1)
    hat, inv = norm_parts(x_ref[...].astype(f32))
    part = jnp.sum(gn * hat, axis=0, keepdims=True)

    @pl.when(pl.program_id(0) == 0)
    def _():
        gg_ref[...] = part

    @pl.when(pl.program_id(0) > 0)
    def _():
        gg_ref[...] += part

    ag_ref[...] = masked_ref[...].astype(f32) + norm_back(gn, hat, inv, gain_ref[...])


def input_backward(idx, held, own_in, g_mixed, x, masked, gain):
    length, width = masked.shape
    R = 512
    blk = rows_of(R, width)
    return call(
        norm_back_kernel,
        (length // R,),
        [ANY] * 9 + [pl.BlockSpec((3, R, width), lambda i, *_: (0, i, 0)),
                     pl.BlockSpec((None, R, width), lambda i, idx: (idx[2], i, 0)), blk, whole(gain.shape)],
        [blk, pl.BlockSpec((1, width), lambda *_: (0, 0))],
        [sds((length, width), f32), sds((1, width), f32)],
        [pltpu.VMEM((width, 3 * width), bf16), SEMS],
        (idx, *held, own_in, g_mixed, x, masked, gain),
        6 * length * width * width,
        2 * (7 * length * width + 3 * width * width),
        prefetch=1,
    )


def unpack_mlp_kernel(idx, all_ref, up, down, out):
    part = up.shape[0]
    q = up.shape[1] // 4
    h = down.shape[1] // 2
    r = part // 4
    for n in range(8):
        d, side = n // 2, n % 2
        cols = slice(side * h, side * h + h)
        down[d * part : (d + 1) * part, cols] = all_ref[n, 0:part].astype(f32)
        up[:, d * q + side * h : d * q + side * h + h] = all_ref[n, part : 2 * part].astype(f32)
        out[d * r : (d + 1) * r, cols] = all_ref[n, 2 * part :].astype(f32)


def unpack_mix_kernel(idx, *refs):
    held, (g_in, g_kern) = refs[:8], refs[8:]
    part, length = g_kern.shape
    width = 4 * part
    r = part // 4
    h = width // 2
    b = CH // 2
    for e in range(4):
        at = pl.ds(pl.multiple_of((idx[1] ^ e) * r, 16), r)
        for ref, side in ((held[e], idx[2]), (held[4 + e], 1 - idx[2])):
            for i in range(width // CH):
                for p in range(3):
                    c = i * h + p * b
                    g_in[at, pl.ds(pl.multiple_of(p * width + i * CH + side * b, 128), b)] = ref[:, c : c + b].astype(f32)
            g_kern[at, pl.ds(pl.multiple_of(side * (length // 2), 128), length // 2)] = ref[:, 3 * h :].astype(f32)


def unpack(kernel, idx, held, shapes):
    return call(
        kernel,
        (1,),
        [whole(h.shape) for h in held],
        [whole(s) for s in shapes],
        [sds(s, f32) for s in shapes],
        [],
        (idx, *held),
        0,
        sum(6 * math.prod(s) for s in shapes),
        prefetch=1,
    )


SWAP = [(0, 1), (1, 0)]


def shift(k):
    return [(i, (i + k) % 4) for i in range(4)]


def flip(e):
    return [(i, i ^ e) for i in range(4)]


def tie(value, *others):
    return lax.optimization_barrier((value, *others))[0]


def over_line(piece):
    return jnp.concatenate([lax.ppermute(piece, "chan", shift(k)) for k in SHIFTS], 0)


def over_plane(near):
    return [near] + [lax.ppermute(near, "dp", flip(e)) for e in (1, 2, 3)]


def over_chip(mine):
    return mine + [lax.ppermute(m, "section", SWAP) for m in mine]


def total(parts):
    out = parts[0].astype(f32)
    for p in parts[1:]:
        out += p.astype(f32)
    return out.astype(bf16)


def fold_plane(parts):
    return total([parts[0]] + [lax.ppermute(parts[e], "dp", flip(e)) for e in (1, 2, 3)])


def fold_line(held, z):
    def at(k):
        return lax.dynamic_index_in_dim(held, (z + k) % 4, 0, keepdims=False)

    return total([at(0)] + [lax.ppermute(at(k), "chan", shift(k)) for k in SHIFTS])


def cut(v, at, size, axis):
    return lax.dynamic_slice_in_dim(v, at, size, axis)


def fast_body(inputs, lengths, out_grad, ln_mix_gain, w_in, short_taps, long_taps, w_out, ln_mlp_gain, w_up, w_down):
    z, d, s = lax.axis_index("chan"), lax.axis_index("dp"), lax.axis_index("section")
    length = inputs.shape[2]
    width = inputs.shape[3]
    part = w_in.shape[1]
    ff = w_up.shape[2]
    half = width // 2
    hl = length // 2
    r = part // 4
    count = lax.dynamic_index_in_dim(lengths[:, 0], s, 0, keepdims=False)
    idx = jnp.stack([z, d, s, count]).astype(jnp.int32)
    x, og = inputs[:, 0], out_grad[:, 0]
    table = odd_basis(length)
    basis, back = jnp.asarray(table), jnp.asarray(np.ascontiguousarray(table.T))
    first = s == 0

    def after(parts, values):
        return lax.optimization_barrier((list(parts), list(values)))

    def both_cores(near, away):
        return total([near, lax.ppermute(away, "section", SWAP)])

    def stacked(own_first, own_second, other, dtype):
        keep = jnp.where(first, own_first, own_second).astype(dtype)
        other = other.astype(dtype)
        both = jnp.stack([jnp.where(first, keep, other), jnp.where(first, other, keep)])
        return both[None, :, None]

    def to_plane(parts):
        return [parts[0]] + [lax.ppermute(parts[e], "dp", flip(e)) for e in (1, 2, 3)]

    def line_sum(held):
        return lax.psum_scatter(held, "chan", scatter_dimension=0, tiled=False)

    own_in, own_out, own_up, own_down = w_in[0], w_out[0], w_up[0], w_down[0]
    own_taps = long_taps[0].T
    small = jnp.concatenate([ln_mix_gain, ln_mlp_gain, short_taps[0].reshape(9, part)], 0)
    own_small = jnp.pad(small.T, ((0, 0), (0, 128 - 11)))
    piece = jnp.concatenate([cut(own_taps, s * hl, hl, 1), own_small], 1)
    split = piece.shape[1]
    piece = jnp.concatenate([cut(piece, d * r, r, 0), cut(cut(own_in, d * r, r, 0), s * 3 * half, 3 * half, 1)], 1)
    near = over_line(piece)
    near_rest, near_in = near[:, :split], near[:, split:]
    plane_rest = over_plane(near_rest)
    plane_in = over_plane(near_in)
    piece_mlp = jnp.concatenate(
        [
            cut(cut(own_down, d * part, part, 0), s * half, half, 1),
            cut(own_up, s * (ff // 2) + d * (ff // 8), ff // 8, 1),
            cut(cut(own_out, d * r, r, 0), s * half, half, 1),
        ],
        0,
    )
    line_mlp = lax.all_gather(tie(piece_mlp, near), "chan", axis=0)
    held_rest = over_chip(plane_rest)

    plane_in, (spec, small, taps) = after(
        plane_in, kernel_spectra(idx, held_rest, tie(own_taps, near_in), own_small, basis)
    )
    held_in = over_chip(plane_in)
    gain_mix, gain_mlp = small[0:1], small[1:2]
    line_mlp = [lax.dynamic_index_in_dim(line_mlp, (z + 4 - k) % 4, 0, keepdims=False) for k in SHIFTS]
    near_up = jnp.concatenate([v[part:] for v in line_mlp], 0)
    near_down = jnp.concatenate([v[:part] for v in line_mlp], 0)
    plane_up = over_plane(near_up)
    plane_down = over_plane(near_down)
    plane_up, (normed0, mixed, qkv, sspec, conv, gated) = after(
        plane_up, mixer_front(idx, held_in, own_in, x, gain_mix, taps, tie(spec, near_up, near_down), basis, back)
    )
    held_up = over_chip(plane_up)
    act0, normed1 = mixer_out(idx, held_up, own_out, x, gated, gain_mlp)
    plane_down, (hidden, slope, near, away) = after(plane_down, mlp_up(idx, held_up, own_up, og, normed1))
    held_down = over_chip(plane_down)

    h_down = both_cores(near, away).reshape(4, 4, part, half)
    sent_down = [lax.dynamic_index_in_dim(h_down, d ^ e, 1, keepdims=False) for e in range(4)]
    got_down = to_plane(sent_down)
    got_down, (ag1, branch0, g_gain_mlp, near, away, near_out, away_out) = after(
        got_down,
        mlp_down(
            idx, held_up, held_down, own_up, own_down, og, act0, normed1, tie(slope, *sent_down), gated, gain_mlp
        ),
    )
    h_up = both_cores(near, away).reshape(4, part, ff // 2)
    h_out = both_cores(near_out, away_out).reshape(4, 4, r, half)
    sent_up = [
        jnp.concatenate([cut(h_up, (d ^ e) * half, half, 2), lax.dynamic_index_in_dim(h_out, d ^ e, 1, keepdims=False)], 1)
        for e in range(4)
    ]
    got_up = to_plane(sent_up)

    branch_late = tie(branch0, *sent_up)
    got_up, (g_mixed, near, away, g_taps) = after(
        got_up,
        conv_backward(idx, held_up, own_out, branch_late, normed0, mixed, qkv, taps, conv, spec, sspec, basis, back),
    )
    u_mlp = jnp.concatenate([total(got_down), total(got_up)], 1)
    p_mlp = line_sum(u_mlp)
    h_mix = both_cores(near, away).reshape(4, 4, r, 3 * half + hl)
    sent_mix = [lax.dynamic_index_in_dim(h_mix, d ^ e, 1, keepdims=False) for e in range(4)]
    got_mix = to_plane(sent_mix)
    ag0, g_gain_mix = input_backward(idx, held_in, own_in, tie(g_mixed, u_mlp, *sent_mix), x, branch0, gain_mix)
    act1 = mlp_last(idx, held_down, own_down, hidden, tie(act0, ag0))
    tiny = jnp.concatenate([g_gain_mix, g_gain_mlp, g_taps], 0)
    tiny += lax.ppermute(tiny, "section", SWAP)
    swapped = jnp.concatenate([jnp.where(first, act1, act0), jnp.where(first, ag1, ag0).astype(bf16)], 0)
    (*got_mix, p_mlp), (ag0, tiny, swapped) = after([*got_mix, p_mlp], [ag0, tiny, swapped])
    all_mlp = lax.all_gather(p_mlp, ("dp", "section"), axis=0)
    u_mix = total(got_mix)
    sent_line = [lax.dynamic_index_in_dim(u_mix, (z + k) % 4, 0, keepdims=False) for k in (0, *SHIFTS)]
    got_line = [sent_line[0]] + [lax.ppermute(v, "chan", shift(k)) for k, v in zip(SHIFTS, sent_line[1:])]
    tiny = tie(tiny, *sent_line)
    tiny += lax.ppermute(tiny, "dp", flip(1))
    tiny += lax.ppermute(tiny, "dp", flip(2))
    ag0_late = tie(ag0, *sent_line)
    swapped = lax.ppermute(swapped, "section", SWAP)
    out_act = stacked(act0, act1, swapped[:length], bf16)
    out_ag = stacked(ag0_late, ag1, swapped[length:], f32)
    got_line, (tiny, out_act, out_ag) = after(got_line, [tiny, out_act, out_ag])
    g_up, g_down, g_out = unpack(unpack_mlp_kernel, idx, [all_mlp], [(part, ff), (4 * part, width), (part, width)])
    p_mix = total(got_line)
    plane_mix = over_plane(p_mix)
    tiny = tie(tiny, p_mix)
    tiny += lax.ppermute(tiny, "chan", flip(1))
    plane_mix, (tiny,) = after(plane_mix, [tiny])
    got_tiny = [lax.ppermute(tiny, "chan", flip(2))]
    held_mix, (g_up, g_down, g_out) = after(over_chip(plane_mix), [g_up, g_down, g_out])
    g_in, g_kern = unpack(unpack_mix_kernel, idx, held_mix, [(part, 3 * width), (part, length)])
    got_tiny, (g_in, g_kern) = after(got_tiny, [g_in, g_kern])
    tiny += got_tiny[0]

    mine = cut(tiny[0:2], z * part, part, 1)
    g_taps = tiny[2:11].reshape(3, 3, width).transpose(1, 0, 2).reshape(3, 3 * width)
    g_taps = cut(g_taps, z * 3 * part, 3 * part, 1)

    return (
        out_act,
        out_ag,
        mine[0:1],
        g_in[None],
        g_taps[None],
        g_kern.T[None],
        g_out[None],
        mine[1:2],
        g_up[None],
        g_down[None],
    )


def fits(mesh):
    return mesh.shape["chan"] == 4 and mesh.shape["dp"] == 4 and mesh.shape["section"] == 2


def shift_down(v, n):
    return jnp.pad(v, ((n, 0), (0, 0)))[: v.shape[0]]


def shift_up(v, n):
    return jnp.pad(v, ((0, n), (0, 0)))[n:]


def plain_body(inputs, lengths, out_grad, ln_mix_gain, w_in, short_taps, long_taps, w_out, ln_mlp_gain, w_up, w_down):
    own = lax.axis_index("section")
    length, width = inputs.shape[2:]
    position = lax.broadcasted_iota(jnp.int32, (length, 1), 0)
    x = lax.dynamic_index_in_dim(inputs[:, 0], own, 0, keepdims=False).astype(f32)
    og = lax.dynamic_index_in_dim(out_grad[:, 0], own, 0, keepdims=False)
    live = (position < lax.dynamic_index_in_dim(lengths[:, 0], own, 0, keepdims=False)).astype(f32)

    def rows(w):
        return lax.all_gather(w[0], "chan", axis=0, tiled=True)

    def cols(w):
        return lax.all_gather(w[0], "chan", axis=1, tiled=True)

    gain_mix = cols(ln_mix_gain[None])[0].astype(f32)
    gain_mlp = cols(ln_mlp_gain[None])[0].astype(f32)
    taps = cols(short_taps).astype(f32)
    kern = cols(long_taps).astype(f32)
    proj_in, proj_out, proj_up, proj_down = rows(w_in), rows(w_out), rows(w_up), rows(w_down)

    basis = jnp.asarray(odd_basis(length))
    decay = jnp.exp(-decay_rate * position.astype(f32))
    half = length

    def spectrum(v):
        both = dot(basis, v)
        return both[:half], both[half:]

    def back(cos_part, sin_part):
        return dot(basis, jnp.concatenate([cos_part, sin_part], 0).astype(bf16), 0, 0)

    kc, ks = spectrum((kern * decay).astype(bf16))
    kc, ks = kc / length, ks / length
    hat0, inv0 = norm_parts(x)
    normed0 = (hat0 * gain_mix).astype(bf16)
    mixed = dot(normed0, proj_in)
    smooth = taps[0] * mixed + taps[1] * shift_down(mixed, 1) + taps[2] * shift_down(mixed, 2)
    query, key, value = smooth[:, :width], smooth[:, width : 2 * width], smooth[:, 2 * width :]
    sc, ss = spectrum((key * value).astype(bf16))
    conv = back(sc * kc - ss * ks, sc * ks + ss * kc)
    gated = (query * conv).astype(bf16)
    act0 = (live * (x + dot(gated, proj_out))).astype(bf16)
    x1 = act0.astype(f32)
    hat1, inv1 = norm_parts(x1)
    normed1 = (hat1 * gain_mlp).astype(bf16)
    pre = dot(normed1, proj_up)
    cdf = 0.5 * (1.0 + lax.erf(pre * math.sqrt(0.5)))
    hidden = (pre * cdf).astype(bf16)
    act1 = (live * (x1 + dot(hidden, proj_down))).astype(bf16)
    masked1 = live * og.astype(f32)
    branch1 = masked1.astype(bf16)
    g_down = dot(hidden, branch1, 0, 0)
    slope = cdf + pre * (jnp.exp(-0.5 * pre * pre) * (1.0 / math.sqrt(2.0 * math.pi)))
    pre_grad = (slope * dot(branch1, proj_down, 1, 1)).astype(bf16)
    g_up = dot(normed1, pre_grad, 0, 0)
    gn1 = dot(pre_grad, proj_up, 1, 1)
    g_gain_mlp = jnp.sum(gn1 * hat1, axis=0)
    ag1 = masked1 + norm_back(gn1, hat1, inv1, gain_mlp)
    ag1_low = ag1.astype(bf16)
    masked0 = live * ag1_low.astype(f32)
    branch0 = masked0.astype(bf16)
    g_out = dot(gated, branch0, 0, 0)
    grad_gated = dot(branch0, proj_out, 1, 1)
    gc, gs = spectrum((grad_gated * query).astype(bf16))
    g_kern = back(sc * gc + ss * gs, sc * gs - ss * gc) * (decay / length)
    g_sig = back(kc * gc + ks * gs, kc * gs - ks * gc)
    g_smooth = jnp.concatenate([grad_gated * conv, g_sig * value, g_sig * key], 1)
    g_taps = jnp.stack([jnp.sum(g_smooth * shift_down(mixed, n), axis=0) if n else jnp.sum(g_smooth * mixed, axis=0) for n in range(3)])
    g_mixed = (taps[0] * g_smooth + taps[1] * shift_up(g_smooth, 1) + taps[2] * shift_up(g_smooth, 2)).astype(bf16)
    g_in = dot(normed0, g_mixed, 0, 0)
    gn0 = dot(g_mixed, proj_in, 1, 1)
    g_gain_mix = jnp.sum(gn0 * hat0, axis=0)
    ag0 = masked0 + norm_back(gn0, hat0, inv0, gain_mix)

    swap = [(0, 1), (1, 0)]
    first = own == 0

    def exchange(own_first, own_second, dtype):
        keep = jnp.where(first, own_first, own_second).astype(dtype)
        other = lax.ppermute(jnp.where(first, own_second, own_first).astype(bf16), "section", swap).astype(dtype)
        both = jnp.stack([jnp.where(first, keep, other), jnp.where(first, other, keep)])
        return both[None, :, None]

    def reduced(g, dim):
        part = lax.psum_scatter(g.astype(bf16), "chan", scatter_dimension=dim, tiled=True)
        return lax.psum(part, ("section", "dp")).astype(f32)[None]

    return (
        exchange(act0, act1, bf16),
        exchange(ag0, ag1, f32),
        reduced(g_gain_mix, 0),
        reduced(g_in, 0),
        reduced(g_taps, 1),
        reduced(g_kern, 1),
        reduced(g_out, 0),
        reduced(g_gain_mlp, 0),
        reduced(g_up, 0),
        reduced(g_down, 0),
    )


def solution(mesh):
    return jax.shard_map(
        fast_body if fits(mesh) else plain_body,
        mesh=mesh,
        in_specs=(
            P(None, ("dp", "chan"), None, None),
            P(None, ("dp", "chan")),
            P(None, ("dp", "chan"), None, None),
            P(None, "chan"),
            P(None, "chan", None),
            P(None, None, "chan"),
            P(None, None, "chan"),
            P(None, "chan", None),
            P(None, "chan"),
            P(None, "chan", None),
            P(None, "chan", None),
        ),
        out_specs=(
            P("section", None, ("dp", "chan"), None, None),
            P("section", None, ("dp", "chan"), None, None),
            P(None, "chan"),
            P(None, "chan", None),
            P(None, None, "chan"),
            P(None, None, "chan"),
            P(None, "chan", None),
            P(None, "chan"),
            P(None, "chan", None),
            P(None, "chan", None),
        ),
        check_vma=False,
    )
```

```python
import math

import jax
import jax.numpy as jnp
import ml_dtypes
import numpy as np
from jax import lax
from jax.experimental import pallas as pl
from jax.experimental.pallas import tpu as pltpu
from jax.sharding import PartitionSpec as P

decay_rate = 0.003
bf16 = jnp.bfloat16
f32 = jnp.float32
MIB = 1 << 20


def odd_basis(length):
    phase = (2 * np.arange(length)[:, None] + 1) * np.arange(length)[None, :] % (4 * length)
    angle = phase * (math.pi / (2 * length))
    return np.concatenate([np.cos(angle), np.sin(angle)], 0).astype(ml_dtypes.bfloat16)


def dot(a, b, ca=1, cb=0):
    return lax.dot_general(a, b, (((ca,), (cb,)), ((), ())), preferred_element_type=f32)


def norm_parts(values):
    centered = values - jnp.mean(values, axis=-1, keepdims=True)
    spread = jnp.mean(centered * centered, axis=-1, keepdims=True)
    inv = lax.rsqrt(spread + 1e-05)
    return centered * inv, inv


def norm_back(grad_normed, hat, inv, gain):
    grad_hat = grad_normed * gain
    return inv * (
        grad_hat
        - jnp.mean(grad_hat, axis=-1, keepdims=True)
        - hat * jnp.mean(grad_hat * hat, axis=-1, keepdims=True)
    )


def call(kernel, grid, in_specs, out_specs, out_shape, scratch, args, flops, nbytes, limit=56, prefetch=0):
    spec = pltpu.PrefetchScalarGridSpec(
        num_scalar_prefetch=prefetch, grid=grid, in_specs=in_specs, out_specs=out_specs, scratch_shapes=scratch
    )
    return pl.pallas_call(
        kernel,
        grid_spec=spec,
        out_shape=out_shape,
        compiler_params=pltpu.CompilerParams(
            dimension_semantics=("arbitrary",) * len(grid), vmem_limit_bytes=limit * MIB
        ),
        cost_estimate=pl.CostEstimate(flops=flops, bytes_accessed=nbytes, transcendentals=0),
    )(*args)


def whole(shape):
    return pl.BlockSpec(shape, lambda *_: (0,) * len(shape), pipeline_mode=pl.Buffered(1))


def rows_of(r, c):
    return pl.BlockSpec((r, c), lambda i, *_: (i, 0))


def cols_of(r, c, start=0):
    return pl.BlockSpec((r, c), lambda i, *_: (0, i + start))


def sds(shape, dtype):
    return jax.ShapeDtypeStruct(shape, dtype)


ANY = pl.BlockSpec(memory_space=pl.ANY)
SHIFTS = (1, 3, 2)


def start_all(copies, sems):
    for n, (a, b) in enumerate(copies):
        pltpu.make_async_copy(a, b, sems.at[n]).start()


def wait_all(copies, sems):
    for n, (a, b) in enumerate(copies):
        pltpu.make_async_copy(a, b, sems.at[n]).wait()


def sources(idx, mine, other):
    z, d, s = idx[0], idx[1], idx[2]
    for e in range(4):
        for j, k in enumerate(SHIFTS):
            for ref, side in ((mine[e], s), (other[e], 1 - s)):
                yield ref, j, lax.rem(z + 4 - k, 4), d ^ e, side


def in_copies(idx, own, mine, other, dst):
    part, half = own.shape[0], own.shape[1] // 2
    r = part // 4
    out = [(own, dst.at[pl.ds(pl.multiple_of(idx[0] * part, 16), part), :])]
    for ref, j, z, d, side in sources(idx, mine, other):
        out.append((ref.at[pl.ds(j * r, r), :],
                    dst.at[pl.ds(pl.multiple_of(z * part + d * r, 16), r), pl.ds(pl.multiple_of(side * half, 128), half)]))
    return out


def up_copies(idx, own, mine, other, dst):
    part, ff = own.shape
    c = ff // 8
    step = part + part // 4
    out = [(own, dst.at[pl.ds(pl.multiple_of(idx[0] * part, 16), part), :])]
    for ref, j, z, d, side in sources(idx, mine, other):
        out.append((ref.at[pl.ds(j * step, part), :],
                    dst.at[pl.ds(pl.multiple_of(z * part, 16), part), pl.ds(pl.multiple_of(side * 4 * c + d * c, 128), c)]))
    return out


def down_copies(idx, own, mine, other, dst):
    q, width = own.shape
    r = q // 4
    h = width // 2
    out = [(own, dst.at[pl.ds(pl.multiple_of(idx[0] * q, 16), q), :])]
    for ref, j, z, d, side in sources(idx, mine, other):
        out.append((ref.at[pl.ds(j * r, r), :],
                    dst.at[pl.ds(pl.multiple_of(z * q + d * r, 16), r), pl.ds(pl.multiple_of(side * h, 128), h)]))
    return out


def out_copies(idx, own, mine, other, dst):
    part, width = own.shape
    r = part // 4
    h = width // 2
    out = [(own, dst.at[pl.ds(pl.multiple_of(idx[0] * part, 16), part), :])]
    for ref, j, z, d, side in sources(idx, mine, other):
        out.append((ref.at[pl.ds(j * 5 * r + part, r), :],
                    dst.at[pl.ds(pl.multiple_of(z * part + d * r, 16), r), pl.ds(pl.multiple_of(side * h, 128), h)]))
    return out


def rest_copies(idx, own, mine, other, dst, start, half):
    part = own.shape[0]
    r = part // 4
    out = [(own, dst.at[pl.ds(pl.multiple_of(idx[0] * part, 16), part), :])]
    for ref, j, z, d, side in sources(idx, mine, other):
        out.append((ref.at[pl.ds(j * r, r), pl.ds(start, half)],
                    dst.at[pl.ds(pl.multiple_of(z * part + d * r, 16), r), pl.ds(pl.multiple_of(side * half, 128), half)]))
    return out


SEMS = pltpu.SemaphoreType.DMA((25,))


CH = 256


def spectra_kernel(idx, *refs):
    held, (own_taps, own_small, basis_in, out_ref, small_ref, taps_ref, taps, small, tall, sig, basis_ref, sems, sems2, sem_b) = refs[:8], refs[8:]
    mine, other = held[:4], held[4:]
    length = taps.shape[1]

    @pl.when(pl.program_id(0) == 0)
    def _():
        copies = rest_copies(idx, own_taps, mine, other, taps, REST_TAPS, length // 2)
        part = own_small.shape[0]
        r = part // 4
        copies2 = [(own_small, small.at[pl.ds(pl.multiple_of(idx[0] * part, 16), part), :])]
        for e in range(4):
            for j, k in enumerate(SHIFTS):
                z = lax.rem(idx[0] + 4 - k, 4)
                copies2.append((mine[e].at[pl.ds(j * r, r), pl.ds(REST_SMALL, 128)],
                                small.at[pl.ds(pl.multiple_of(z * part + (idx[1] ^ e) * r, 16), r), :]))
        start_all(copies2, sems2)
        start_all(copies, sems)
        start_all([(basis_in, basis_ref)], sem_b)
        wait_all(copies2, sems2)
        wide = small[...].astype(f32)
        small_ref[...] = wide.T[0:8]
        for z in range(4):
            for q in range(3):
                tall[(3 * z + q) * part : (3 * z + q + 1) * part] = pltpu.roll(wide[z * part : (z + 1) * part], 126 - q, 1)
        taps_ref[...] = tall[...].T[0:8]
        wait_all(copies, sems)
        wait_all([(basis_in, basis_ref)], sem_b)

    position = lax.broadcasted_iota(jnp.int32, (1, length), 1).astype(f32)
    rows = pl.ds(pl.multiple_of(pl.program_id(0) * CH, CH), CH)
    sig[...] = (taps[rows, :].astype(f32) * (jnp.exp(-decay_rate * position) / length)).astype(bf16)
    out_ref[...] = dot(basis_ref[...], sig[...], 1, 1).astype(bf16)


REST_TAPS, REST_SMALL = 0, 512


def kernel_spectra(idx, rest, own_taps, own_small, basis):
    length = own_taps.shape[1]
    width = own_taps.shape[0] * 4
    return call(
        spectra_kernel,
        (width // CH,),
        [ANY] * 11,
        [cols_of(2 * length, CH), whole((8, width)), whole((8, 3 * width))],
        [sds((2 * length, width), bf16), sds((8, width), f32), sds((8, 3 * width), f32)],
        [pltpu.VMEM((width, length), bf16), pltpu.VMEM((width, 128), bf16), pltpu.VMEM((3 * width, 128), f32), pltpu.VMEM((CH, length), bf16),
         pltpu.VMEM(basis.shape, bf16), SEMS, SEMS, pltpu.SemaphoreType.DMA((1,))],
        (idx, *rest, own_taps, own_small, basis),
        4 * length * length * width,
        basis.size * 2 + 6 * length * width,
        prefetch=1,
    )


class Mover:
    def __init__(self, sems):
        self.sems, self.used = sems, 0

    def start(self, src, dst):
        copy = pltpu.make_async_copy(src, dst, self.sems.at[self.used])
        self.used += 1
        copy.start()
        return copy

    def pieces(self, pairs):
        return [self.start(a, b) for a, b in pairs]


def settle(*copies):
    for c in copies:
        if isinstance(c, list):
            settle(*c)
        else:
            c.wait()


def manual(kernel, n_in, vmem_in, out_shapes, out_specs, scratch, sems, args, flops, nbytes):
    return call(
        kernel,
        (1,),
        [ANY] * n_in + [whole(v.shape) for v in vmem_in],
        out_specs,
        out_shapes,
        [*scratch, pltpu.SemaphoreType.DMA((sems,))],
        (*args, *vmem_in),
        flops,
        nbytes,
        limit=60,
        prefetch=1,
    )


def blocks_of(i):
    return slice(i * CH, (i + 1) * CH)


def front_kernel(idx, *refs):
    held, (own, x_in, spec_in, basis_in, back_in, gain, taps, normed_o, m_o, qkv_o, sspec_o, conv_o, gated_o,
           x_s, w_s, spec_s, basis_s, back_s, normed_s, m_s, qkv_s, sspec_s, conv_s, gated_s,
           pad0, pad1, sig_s, s0, s1, y0, y1, sems) = refs[:8], refs[8:]
    pads, s_s, y_s = (pad0, pad1), (s0, s1), (y0, y1)
    length, width = x_s.shape
    R = 256
    go = Mover(sems)
    x_c = go.start(x_in.at[idx[2]], x_s)
    w_c = go.pieces(in_copies(idx, own, held[:4], held[4:], w_s))
    sent = []
    for p in pads:
        p[0:8] = jnp.zeros((8, 3 * CH), f32)
    settle(x_c)
    for r in range(0, length, R):
        hat, _ = norm_parts(x_s[r : r + R].astype(f32))
        normed_s[r : r + R] = (hat * gain[0:1]).astype(bf16)
    settle(w_c)
    basis_c = go.start(basis_in, basis_s)

    def mix(i):
        w = jnp.concatenate([w_s[:, p * width + i * CH : p * width + (i + 1) * CH] for p in range(3)], 1)
        pads[i % 2][8:] = dot(normed_s[...], w)

    def smooth(i):
        pad = pads[i % 2]
        for r in range(0, length, R):
            now = []
            for p in range(3):
                c = blocks_of(p)
                g = slice(p * width + i * CH, p * width + (i + 1) * CH)
                m_s[p, r : r + R, blocks_of(i)] = pad[8 + r : 8 + r + R, c].astype(bf16)
                now.append(taps[0:1, g] * pad[8 + r : 8 + r + R, c] + taps[3:4, g] * pad[7 + r : 7 + r + R, c]
                           + taps[6:7, g] * pad[6 + r : 6 + r + R, c])
                qkv_s[p, r : r + R, blocks_of(i)] = now[p].astype(bf16)
            sig_s[r : r + R, blocks_of(i)] = (now[1] * now[2]).astype(bf16)
        sent.append(go.start(m_s.at[:, :, blocks_of(i)], m_o.at[:, :, blocks_of(i)]))
        sent.append(go.start(qkv_s.at[:, :, blocks_of(i)], qkv_o.at[:, :, blocks_of(i)]))

    def forth(i):
        s_s[i % 2][...] = dot(basis_s[...], sig_s[:, blocks_of(i)])

    def times(i):
        c = blocks_of(i)
        for r in range(0, length, R):
            at, lo = slice(r, r + R), slice(length + r, length + r + R)
            sc, ss = s_s[i % 2][at], s_s[i % 2][lo]
            sspec_s[at, c] = sc.astype(bf16)
            sspec_s[lo, c] = ss.astype(bf16)
            kc, ks = spec_s[at, c].astype(f32), spec_s[lo, c].astype(f32)
            y_s[i % 2][at] = (sc * kc - ss * ks).astype(bf16)
            y_s[i % 2][lo] = (sc * ks + ss * kc).astype(bf16)
        sent.append(go.start(sspec_s.at[:, c], sspec_o.at[:, c]))

    def back(i):
        c = blocks_of(i)
        conv = dot(back_s[...], y_s[i % 2][...])
        conv_s[:, c] = conv.astype(bf16)
        gated_s[:, c] = (qkv_s[0, :, c].astype(f32) * conv).astype(bf16)
        sent.append(go.start(conv_s.at[:, c], conv_o.at[:, c]))
        sent.append(go.start(gated_s.at[:, c], gated_o.at[:, c]))

    mix(0)
    mix(1)
    settle(basis_c)
    spec_c = go.start(spec_in, spec_s)
    smooth(0)
    forth(0)
    mix(2)
    settle(spec_c)
    back_c = go.start(back_in, back_s)
    sent.append(go.start(normed_s, normed_o))
    smooth(1)
    times(0)
    forth(1)
    settle(back_c)
    back(0)
    smooth(2)
    times(1)
    forth(2)
    back(1)
    times(2)
    back(2)
    settle(sent)


def mixer_front(idx, held, own_in, x, gain, taps, spec, basis, back):
    length, width = x.shape[1:]
    V = pltpu.VMEM
    low, three, tall = (length, width), (3, length, width), (2 * length, width)
    outs = [low, three, three, tall, low, low]
    return manual(
        front_kernel,
        13,
        (gain, taps),
        [sds(s, bf16) for s in outs],
        [ANY] * 6,
        [V(s, bf16) for s in (low, (width, 3 * width), tall, basis.shape, back.shape, *outs)]
        + [V((length + 8, 3 * CH), f32)] * 2 + [V(low, bf16)] + [V((2 * length, CH), f32)] * 2 + [V((2 * length, CH), bf16)] * 2,
        48,
        (idx, *held, own_in, x, spec, basis, back),
        6 * length * width * width + 8 * length * length * width,
        2 * (16 * length * width + 3 * width * width + 2 * basis.size),
    )


def gelu_parts(pre):
    cdf = 0.5 * (1.0 + lax.erf(pre * math.sqrt(0.5)))
    slope = cdf + pre * (jnp.exp(-0.5 * pre * pre) * (1.0 / math.sqrt(2.0 * math.pi)))
    return pre * cdf, slope


def live_rows(idx, rows, start=0):
    return (lax.broadcasted_iota(jnp.int32, (rows, 1), 0) + start < idx[3]).astype(f32)


def near_first(idx, ref, half):
    return (pl.ds(pl.multiple_of(idx[2] * half, 128), half), pl.ds(pl.multiple_of((1 - idx[2]) * half, 128), half))


def out_kernel(idx, *refs):
    rest, (own_out, x_ref, gated_ref, gain_ref, act0_ref, normed_ref, wo_ref, sem_o) = refs[:8], refs[8:]
    R, width = x_ref.shape
    start = pl.program_id(0) * R

    @pl.when(pl.program_id(0) == 0)
    def _():
        outs = out_copies(idx, own_out, rest[:4], rest[4:], wo_ref)
        start_all(outs, sem_o)
        wait_all(outs, sem_o)

    live = live_rows(idx, R, start)
    act0 = (live * (x_ref[...].astype(f32) + dot(gated_ref[...], wo_ref[...]))).astype(bf16)
    act0_ref[...] = act0
    hat, _ = norm_parts(act0.astype(f32))
    normed_ref[...] = (hat * gain_ref[1:2]).astype(bf16)


def mixer_out(idx, rest, own_out, x, gated, gain):
    length, width = gated.shape
    R = 512
    blk = rows_of(R, width)
    return call(
        out_kernel,
        (length // R,),
        [ANY] * 9 + [pl.BlockSpec((None, R, width), lambda i, idx: (idx[2], i, 0)), blk, whole(gain.shape)],
        [blk, blk],
        [sds((length, width), bf16)] * 2,
        [pltpu.VMEM((width, width), bf16), SEMS],
        (idx, *rest, own_out, x, gated, gain),
        2 * length * width * width,
        2 * (4 * length * width + width * width),
        prefetch=1,
    )


def up_kernel(idx, *refs):
    held, (own_up, og_ref, normed_ref, hidden_ref, slope_ref, near_ref, away_ref, wu_ref, turned, sem_u) = refs[:8], refs[8:]
    length, width = og_ref.shape
    half = width // 2
    c = pl.program_id(0)

    @pl.when(c == 0)
    def _():
        ups = up_copies(idx, own_up, held[:4], held[4:], wu_ref)
        start_all(ups, sem_u)
        live = live_rows(idx, length)
        for n, cols in enumerate(near_first(idx, og_ref, half)):
            turned[:, n * half : (n + 1) * half] = (live * og_ref[:, cols].astype(f32)).astype(bf16)
        wait_all(ups, sem_u)

    at = pl.ds(pl.multiple_of(c * width, width), width)
    hid, slope = gelu_parts(dot(normed_ref[...], wu_ref[:, at]))
    hid = hid.astype(bf16)
    hidden_ref[...] = hid
    slope_ref[...] = slope.astype(bf16)
    grad = dot(hid, turned[...], 0, 0).astype(bf16)
    near_ref[...] = grad[:, :half]
    away_ref[...] = grad[:, half:]


def mlp_up(idx, held, own_up, og, normed):
    length, width = normed.shape
    ff = own_up.shape[1]
    half = width // 2
    wide = cols_of(length, width)
    picked = pl.BlockSpec((None, length, width), lambda i, idx: (idx[2], 0, 0), pipeline_mode=pl.Buffered(1))
    return call(
        up_kernel,
        (ff // width,),
        [ANY] * 9 + [picked, whole((length, width))],
        [wide, wide, rows_of(width, half), rows_of(width, half)],
        [sds((length, ff), bf16), sds((length, ff), bf16), sds((ff, half), bf16), sds((ff, half), bf16)],
        [pltpu.VMEM((width, ff), bf16), pltpu.VMEM((length, width), bf16), SEMS],
        (idx, *held, own_up, og, normed),
        4 * length * width * ff,
        2 * (2 * length * width + 2 * width * ff + 2 * length * ff),
        prefetch=1,
    )


def down_kernel(idx, *refs):
    held, (own_up, own_down, act0_in, normed_in, gated_in, og_ref, slope_ref, gain_ref,
           ag_ref, branch_ref, gg_ref, near_ref, away_ref, near_out, away_out,
           wu_ref, wd_ref, gn, branch, turned, act0_ref, normed_ref, gated_ref, sem_u, sem_d, sem_l, sem_m) = refs[:16], refs[16:]
    length, width = og_ref.shape
    half = width // 2
    c = pl.program_id(0)
    live = live_rows(idx, length)
    ups = up_copies(idx, own_up, held[:4], held[4:8], wu_ref)
    late = [(normed_in, normed_ref), (act0_in, act0_ref), (gated_in, gated_ref)]

    @pl.when(c == 0)
    def _():
        downs = down_copies(idx, own_down, held[8:12], held[12:], wd_ref)
        start_all(downs, sem_d)
        branch[...] = (live * og_ref[...].astype(f32)).astype(bf16)
        gn[...] = jnp.zeros((length, width), f32)
        wait_all(downs, sem_d)
        start_all(ups, sem_u)
        start_all(late[:1], sem_l)

    at = pl.ds(pl.multiple_of(c * width, width), width)
    pre = (slope_ref[...].astype(f32) * dot(branch[...], wd_ref[at, :], 1, 1)).astype(bf16)
    for n, cols in enumerate(near_first(idx, turned, half)):
        turned[:, cols] = pre[:, n * half : (n + 1) * half]

    @pl.when(c == 0)
    def _():
        wait_all(ups, sem_u)
        wait_all(late[:1], sem_l)
        start_all(late[1:], sem_m)

    gn[...] += dot(pre, wu_ref[:, at], 1, 1)
    grad = dot(normed_ref[...], turned[...], 0, 0).astype(bf16)
    near_ref[...] = grad[:, :half]
    away_ref[...] = grad[:, half:]

    @pl.when(c == pl.num_programs(0) - 1)
    def _():
        wait_all(late[1:], sem_m)
        hat, inv = norm_parts(act0_ref[...].astype(f32))
        gg_ref[...] = jnp.sum(gn[...] * hat, axis=0, keepdims=True)
        ag = live * og_ref[...].astype(f32) + norm_back(gn[...], hat, inv, gain_ref[1:2])
        ag_ref[...] = ag
        branch_ref[...] = (live * ag).astype(bf16)
        for n, cols in enumerate(near_first(idx, branch_ref, half)):
            turned[:, n * half : (n + 1) * half] = branch_ref[:, cols]
        g_out = dot(gated_ref[...], turned[...], 0, 0).astype(bf16)
        near_out[...] = g_out[:, :half]
        away_out[...] = g_out[:, half:]


def mlp_down(idx, held_up, held_down, own_up, own_down, og, act0, normed, slope, gated, gain):
    length, width = act0.shape
    ff = own_up.shape[1]
    half = width // 2
    picked = pl.BlockSpec((None, length, width), lambda i, idx: (idx[2], 0, 0), pipeline_mode=pl.Buffered(1))
    one = whole((length, width))
    wide = cols_of(length, width)
    full = sds((length, width), bf16)
    col = pltpu.VMEM((length, width), f32)
    low = pltpu.VMEM((length, width), bf16)
    return call(
        down_kernel,
        (ff // width,),
        [ANY] * 21 + [picked, wide, whole(gain.shape)],
        [one, one, whole((1, width)), cols_of(width, half), cols_of(width, half), whole((width, half)), whole((width, half))],
        [sds((length, width), f32), full, sds((1, width), f32), sds((width, ff // 2), bf16), sds((width, ff // 2), bf16),
         sds((width, half), bf16), sds((width, half), bf16)],
        [pltpu.VMEM((width, ff), bf16), pltpu.VMEM((ff, width), bf16), col, low, low, low, low, low, SEMS, SEMS,
         pltpu.SemaphoreType.DMA((1,)), pltpu.SemaphoreType.DMA((2,))],
        (idx, *held_up, *held_down, own_up, own_down, act0, normed, gated, og, slope, gain),
        6 * length * width * ff,
        2 * (7 * length * width + 3 * width * ff + length * ff),
        prefetch=1,
    )


def last_kernel(idx, *refs):
    held, (own_down, hidden_ref, act0_ref, keep_ref, hand_ref, wd_ref, acc, sem_d) = refs[:8], refs[8:]
    length, width = act0_ref.shape
    c = pl.program_id(0)

    @pl.when(c == 0)
    def _():
        downs = down_copies(idx, own_down, held[:4], held[4:], wd_ref)
        start_all(downs, sem_d)
        acc[...] = act0_ref[...].astype(f32)
        wait_all(downs, sem_d)

    acc[...] += dot(hidden_ref[...], wd_ref[pl.ds(pl.multiple_of(c * width, width), width), :])

    @pl.when(c == pl.num_programs(0) - 1)
    def _():
        act1 = (live_rows(idx, length) * acc[...]).astype(bf16)

        @pl.when(idx[2] == 0)
        def _():
            keep_ref[...] = act0_ref[...]
            hand_ref[...] = act1

        @pl.when(idx[2] != 0)
        def _():
            keep_ref[...] = act1
            hand_ref[...] = act0_ref[...]


def mlp_last(idx, held, own_down, hidden, act0):
    length, width = act0.shape
    ff = own_down.shape[0] * 4
    one = whole((length, width))
    return call(
        last_kernel,
        (ff // width,),
        [ANY] * 9 + [cols_of(length, width), one],
        [one, one],
        [sds((length, width), bf16)] * 2,
        [pltpu.VMEM((ff, width), bf16), pltpu.VMEM((length, width), f32), SEMS],
        (idx, *held, own_down, hidden, act0),
        2 * length * width * ff,
        2 * (2 * length * width + width * ff + length * ff),
        prefetch=1,
    )


def conv_back_kernel(idx, *refs):
    held, (own_out, branch_in, normed_in, m_in, qkv_in, conv_in, spec_in, sspec_in, basis_in, back_in, taps,
           g_o, near_o, away_o, gtaps_ref,
           w_s, branch_s, normed_s, m_s, qkv_s, conv_s, spec_s, sspec_s, basis_s, back_s,
           gpad0, gpad1, sig_s, s0, s1, y0, y1, both_s, gm0, gm1, g0_s, g1_s, kern0, kern1, near0, near1, away0, away1,
           sems) = refs[:8], refs[8:]
    gpads, s_s, y_s, gms, g_s, kerns, near_s, away_s = ((gpad0, gpad1), (s0, s1), (y0, y1), (gm0, gm1), (g0_s, g1_s),
                                                        (kern0, kern1), (near0, near1), (away0, away1))
    length, width = branch_s.shape
    half = width // 2
    hl = length // 2
    R = 256
    nb = width // CH
    go = Mover(sems)
    branch_c = go.start(branch_in, branch_s)
    w_c = go.pieces(out_copies(idx, own_out, held[:4], held[4:], w_s))
    basis_c = go.start(basis_in, basis_s)

    def fetch(i):
        c = blocks_of(i)
        return [go.start(qkv_in.at[:, :, c], qkv_s.at[:, :, c]), go.start(conv_in.at[:, c], conv_s.at[:, c])]

    def fetch_spectra(i):
        c = blocks_of(i)
        return [go.start(spec_in.at[:, c], spec_s.at[:, c]), go.start(sspec_in.at[:, c], sspec_s.at[:, c])]

    def fetch_mixed(i):
        c = blocks_of(i)
        return go.start(m_in.at[:, :, c], m_s.at[:, :, c])

    for p in gpads:
        p[length : length + 8] = jnp.zeros((8, 3 * CH), f32)
    sent = [[], []]
    settle(branch_c, w_c)
    first_c = fetch(0)

    def spread_back(i):
        s_s[i % 2][0:length] = dot(branch_s[...], w_s[blocks_of(i), :], 1, 1)

    def gate(i):
        c = blocks_of(i)
        for r in range(0, length, R):
            at = slice(r, r + R)
            gg = s_s[i % 2][at]
            sig_s[at, c] = (gg * qkv_s[0, at, c].astype(f32)).astype(bf16)
            gpads[i % 2][at, 0:CH] = gg * conv_s[at, c].astype(f32)

    def forth(i):
        s_s[i % 2][...] = dot(basis_s[...], sig_s[:, blocks_of(i)])

    def times(i):
        c = blocks_of(i)
        y = y_s[i % 2]
        for r in range(0, length, R):
            at, lo = slice(r, r + R), slice(length + r, length + r + R)
            gc, gs = s_s[i % 2][at], s_s[i % 2][lo]
            kc, ks = spec_s[at, c].astype(f32), spec_s[lo, c].astype(f32)
            y[at, 0:CH] = (kc * gc + ks * gs).astype(bf16)
            y[lo, 0:CH] = (kc * gs - ks * gc).astype(bf16)
            sc, ss = sspec_s[at, c].astype(f32), sspec_s[lo, c].astype(f32)
            y[at, CH:] = (sc * gc + ss * gs).astype(bf16)
            y[lo, CH:] = (sc * gs - ss * gc).astype(bf16)

    def back(i):
        both_s[...] = dot(back_s[...], y_s[i % 2][...])

    def unsmooth(i):
        b = blocks_of(i)
        gpad, gm, kern = gpads[i % 2], gms[i % 2], kerns[i % 2]
        settle(sent[i % 2])
        for r in range(0, length, R):
            at = slice(r, r + R)
            g_sig = both_s[at, :CH]
            gpad[at, CH : 2 * CH] = g_sig * qkv_s[2, at, b].astype(f32)
            gpad[at, 2 * CH :] = g_sig * qkv_s[1, at, b].astype(f32)
            position = (lax.broadcasted_iota(jnp.int32, (R, 1), 0) + r).astype(f32)
            kern[:, at] = (both_s[at, CH:] * (jnp.exp(-decay_rate * position) / length)).T.astype(bf16)
        sums = [[jnp.zeros((1, CH), f32)] * 3 for _ in range(3)]
        for r in range(0, length, R):
            at = slice(r, r + R)
            for p in range(3):
                c = blocks_of(p)
                t = slice(p * width + i * CH, p * width + (i + 1) * CH)
                now = [gpad[r + n : r + n + R, c] for n in range(3)]
                g = (taps[0:1, t] * now[0] + taps[3:4, t] * now[1] + taps[6:7, t] * now[2]).astype(bf16)
                g_s[i % 2][p, at] = g
                for n in range(2):
                    to = jnp.where(idx[2] == n, 0, half) + p * (CH // 2)
                    gm[at, pl.ds(pl.multiple_of(to, 128), CH // 2)] = g[:, n * (CH // 2) : (n + 1) * (CH // 2)]
                mixed = m_s[p, at, b].astype(f32)
                sums[p] = [sums[p][n] + jnp.sum(now[n] * mixed, axis=0, keepdims=True) for n in range(3)]
        for p in range(3):
            for n in range(3):
                gtaps_ref[3 * p + n : 3 * p + n + 1, b] = sums[p][n]
        side = slice(3 * half, 3 * half + hl)
        mine, other = near_first(idx, kern, hl)
        sent[i % 2] = [go.start(g_s[i % 2], g_o.at[:, :, b]), go.start(kern.at[:, mine], near_o.at[b, side]),
                       go.start(kern.at[:, other], away_o.at[b, side])]

    def grad(i):
        g = dot(normed_s[...], gms[i % 2][...], 0, 0).astype(bf16)
        near_s[i % 2][...] = g[:, :half]
        away_s[i % 2][...] = g[:, half:]
        c = slice(i * half, (i + 1) * half)
        sent[i % 2] += [go.start(near_s[i % 2], near_o.at[:, c]), go.start(away_s[i % 2], away_o.at[:, c])]

    spread_back(0)
    spread_back(1)
    settle(basis_c, first_c)
    spectra_c = fetch_spectra(0)
    gate(0)
    forth(0)
    settle(spectra_c)
    back_c = go.start(back_in, back_s)
    next_c = fetch(1)
    times(0)
    settle(next_c, back_c)
    spectra_c = fetch_spectra(1)
    mixed_c = fetch_mixed(0)
    normed_c = go.start(normed_in, normed_s)
    back(0)
    gate(1)
    forth(1)
    spread_back(2)
    settle(spectra_c, mixed_c, normed_c)
    next_c = fetch(2)
    mixed_c = fetch_mixed(1)
    spectra_c = fetch_spectra(2)
    unsmooth(0)
    times(1)
    back(1)
    grad(0)
    settle(next_c, mixed_c, spectra_c)
    mixed_c = fetch_mixed(2)
    gate(2)
    forth(2)
    unsmooth(1)
    times(2)
    grad(1)
    back(2)
    settle(mixed_c)
    unsmooth(2)
    grad(2)
    settle(sent)


def conv_backward(idx, held, own_out, branch, normed, mixed, qkv, taps, conv, spec, sspec, basis, back):
    length, width = branch.shape
    half = width // 2
    mix = (width, 3 * half + length // 2)
    V = pltpu.VMEM
    low, three, tall = (length, width), (3, length, width), (2 * length, width)
    twice = lambda s, t: [V(s, t)] * 2
    return manual(
        conv_back_kernel,
        18,
        (taps,),
        [sds(three, bf16), sds(mix, bf16), sds(mix, bf16), sds((9, width), f32)],
        [ANY] * 3 + [whole((9, width))],
        [V(s, bf16) for s in ((width, width), low, low, three, three, low, tall, tall, basis.shape, back.shape)]
        + twice((length + 8, 3 * CH), f32) + [V(low, bf16)] + twice((2 * length, CH), f32) + twice((2 * length, 2 * CH), bf16)
        + [V((length, 2 * CH), f32)] + twice((length, 3 * CH), bf16) + twice((3, length, CH), bf16) + twice((CH, length), bf16)
        + twice((width, half), bf16) + twice((width, half), bf16),
        64,
        (idx, *held, own_out, branch, normed, mixed, qkv, conv, spec, sspec, basis, back),
        8 * length * width * width + 12 * length * length * width,
        2 * (22 * length * width + 2 * basis.size + 2 * mix[0] * mix[1]),
    )


def norm_back_kernel(idx, *refs):
    held, (own_ref, g_ref, x_ref, masked_ref, gain_ref, ag_ref, gg_ref, wi_ref, sems) = refs[:8], refs[8:]
    width = x_ref.shape[1]

    @pl.when(pl.program_id(0) == 0)
    def _():
        copies = in_copies(idx, own_ref, held[:4], held[4:], wi_ref)
        start_all(copies, sems)
        wait_all(copies, sems)

    gn = dot(jnp.concatenate([g_ref[p] for p in range(3)], 1), wi_ref[...], 1, 1)
    hat, inv = norm_parts(x_ref[...].astype(f32))
    part = jnp.sum(gn * hat, axis=0, keepdims=True)

    @pl.when(pl.program_id(0) == 0)
    def _():
        gg_ref[...] = part

    @pl.when(pl.program_id(0) > 0)
    def _():
        gg_ref[...] += part

    ag_ref[...] = masked_ref[...].astype(f32) + norm_back(gn, hat, inv, gain_ref[0:1])


def input_backward(idx, held, own_in, g_mixed, x, masked, gain):
    length, width = masked.shape
    R = 512
    blk = rows_of(R, width)
    return call(
        norm_back_kernel,
        (length // R,),
        [ANY] * 9 + [pl.BlockSpec((3, R, width), lambda i, *_: (0, i, 0)),
                     pl.BlockSpec((None, R, width), lambda i, idx: (idx[2], i, 0)), blk, whole(gain.shape)],
        [blk, pl.BlockSpec((1, width), lambda *_: (0, 0))],
        [sds((length, width), f32), sds((1, width), f32)],
        [pltpu.VMEM((width, 3 * width), bf16), SEMS],
        (idx, *held, own_in, g_mixed, x, masked, gain),
        6 * length * width * width,
        2 * (7 * length * width + 3 * width * width),
        prefetch=1,
    )


def unpack_mlp_kernel(idx, all_ref, up, down, out):
    part = up.shape[0]
    q = up.shape[1] // 4
    h = down.shape[1] // 2
    r = part // 4
    for n in range(8):
        d, side = n // 2, n % 2
        cols = slice(side * h, side * h + h)
        down[d * part : (d + 1) * part, cols] = all_ref[n, 0:part].astype(f32)
        up[:, d * q + side * h : d * q + side * h + h] = all_ref[n, part : 2 * part].astype(f32)
        out[d * r : (d + 1) * r, cols] = all_ref[n, 2 * part :].astype(f32)


def unpack_mix_kernel(idx, *refs):
    held, (g_in, g_kern) = refs[:8], refs[8:]
    part, length = g_kern.shape
    width = 4 * part
    r = part // 4
    h = width // 2
    b = CH // 2
    for e in range(4):
        at = pl.ds(pl.multiple_of((idx[1] ^ e) * r, 16), r)
        for ref, side in ((held[e], idx[2]), (held[4 + e], 1 - idx[2])):
            for i in range(width // CH):
                for p in range(3):
                    c = i * h + p * b
                    g_in[at, pl.ds(pl.multiple_of(p * width + i * CH + side * b, 128), b)] = ref[:, c : c + b].astype(f32)
            g_kern[at, pl.ds(pl.multiple_of(side * (length // 2), 128), length // 2)] = ref[:, 3 * h :].astype(f32)


def unpack(kernel, idx, held, shapes):
    return call(
        kernel,
        (1,),
        [whole(h.shape) for h in held],
        [whole(s) for s in shapes],
        [sds(s, f32) for s in shapes],
        [],
        (idx, *held),
        0,
        sum(6 * math.prod(s) for s in shapes),
        prefetch=1,
    )


SWAP = [(0, 1), (1, 0)]


def shift(k):
    return [(i, (i + k) % 4) for i in range(4)]


def flip(e):
    return [(i, i ^ e) for i in range(4)]


def tie(value, *others):
    return lax.optimization_barrier((value, *others))[0]


def over_line(piece):
    return jnp.concatenate([lax.ppermute(piece, "chan", shift(k)) for k in SHIFTS], 0)


def over_plane(near):
    return [near] + [lax.ppermute(near, "dp", flip(e)) for e in (1, 2, 3)]


def over_chip(mine):
    return mine + [lax.ppermute(m, "section", SWAP) for m in mine]


def total(parts):
    out = parts[0].astype(f32)
    for p in parts[1:]:
        out += p.astype(f32)
    return out.astype(bf16)


def fold_plane(parts):
    return total([parts[0]] + [lax.ppermute(parts[e], "dp", flip(e)) for e in (1, 2, 3)])


def fold_line(held, z):
    def at(k):
        return lax.dynamic_index_in_dim(held, (z + k) % 4, 0, keepdims=False)

    return total([at(0)] + [lax.ppermute(at(k), "chan", shift(k)) for k in SHIFTS])


def cut(v, at, size, axis):
    return lax.dynamic_slice_in_dim(v, at, size, axis)


def fast_body(inputs, lengths, out_grad, ln_mix_gain, w_in, short_taps, long_taps, w_out, ln_mlp_gain, w_up, w_down):
    z, d, s = lax.axis_index("chan"), lax.axis_index("dp"), lax.axis_index("section")
    length = inputs.shape[2]
    width = inputs.shape[3]
    part = w_in.shape[1]
    ff = w_up.shape[2]
    half = width // 2
    hl = length // 2
    r = part // 4
    count = lax.dynamic_index_in_dim(lengths[:, 0], s, 0, keepdims=False)
    idx = jnp.stack([z, d, s, count]).astype(jnp.int32)
    x, og = inputs[:, 0], out_grad[:, 0]
    table = odd_basis(length)
    basis, back = jnp.asarray(table), jnp.asarray(np.ascontiguousarray(table.T))
    first = s == 0

    def after(parts, values):
        return lax.optimization_barrier((list(parts), list(values)))

    def both_cores(near, away):
        return total([near, lax.ppermute(away, "section", SWAP)])

    def stacked(keep, other, dtype):
        other = other.astype(dtype)
        both = jnp.stack([jnp.where(first, keep, other), jnp.where(first, other, keep)])
        return both[None, :, None]

    def to_plane(parts):
        return [parts[0]] + [lax.ppermute(parts[e], "dp", flip(e)) for e in (1, 2, 3)]

    def line_sum(held):
        return lax.psum_scatter(held, "chan", scatter_dimension=0, tiled=False)

    own_in, own_out, own_up, own_down = w_in[0], w_out[0], w_up[0], w_down[0]
    own_taps = long_taps[0].T
    small = jnp.concatenate([ln_mix_gain, ln_mlp_gain, short_taps[0].reshape(9, part)], 0)
    own_small = jnp.pad(small.T, ((0, 0), (0, 128 - 11)))
    piece = jnp.concatenate([cut(own_taps, s * hl, hl, 1), own_small], 1)
    split = piece.shape[1]
    piece = jnp.concatenate([cut(piece, d * r, r, 0), cut(cut(own_in, d * r, r, 0), s * 3 * half, 3 * half, 1)], 1)
    near, idx = lax.optimization_barrier((over_line(piece), idx))
    near_rest, near_in = near[:, :split], near[:, split:]
    plane_rest = over_plane(near_rest)
    plane_in = over_plane(near_in)
    piece_mlp = jnp.concatenate(
        [
            cut(cut(own_down, d * part, part, 0), s * half, half, 1),
            cut(own_up, s * (ff // 2) + d * (ff // 8), ff // 8, 1),
            cut(cut(own_out, d * r, r, 0), s * half, half, 1),
        ],
        0,
    )
    line_mlp = lax.all_gather(tie(piece_mlp, near), "chan", axis=0)
    held_rest = over_chip(plane_rest)

    plane_in, (spec, small, taps) = after(
        plane_in, kernel_spectra(idx, held_rest, tie(own_taps, near_in), own_small, basis)
    )
    held_in = over_chip(plane_in)
    line_mlp = [lax.dynamic_index_in_dim(line_mlp, (z + 4 - k) % 4, 0, keepdims=False) for k in SHIFTS]
    near_up = jnp.concatenate([v[part:] for v in line_mlp], 0)
    near_down = jnp.concatenate([v[:part] for v in line_mlp], 0)
    plane_up = over_plane(near_up)
    plane_down = over_plane(near_down)
    plane_up, (normed0, mixed, qkv, sspec, conv, gated) = after(
        plane_up, mixer_front(idx, held_in, own_in, x, small, taps, tie(spec, near_up, near_down), basis, back)
    )
    held_up = over_chip(plane_up)
    act0, normed1 = mixer_out(idx, held_up, own_out, x, gated, small)
    plane_down, (hidden, slope, near, away) = after(plane_down, mlp_up(idx, held_up, own_up, og, normed1))
    held_down = over_chip(plane_down)

    h_down = both_cores(near, away).reshape(4, 4, part, half)
    sent_down = [lax.dynamic_index_in_dim(h_down, d ^ e, 1, keepdims=False) for e in range(4)]
    got_down = to_plane(sent_down)
    got_down, (ag1, branch0, g_gain_mlp, near, away, near_out, away_out) = after(
        got_down,
        mlp_down(
            idx, held_up, held_down, own_up, own_down, og, act0, normed1, tie(slope, *sent_down), gated, small
        ),
    )
    h_up = both_cores(near, away).reshape(4, part, ff // 2)
    h_out = both_cores(near_out, away_out).reshape(4, 4, r, half)
    sent_up = [
        jnp.concatenate([cut(h_up, (d ^ e) * half, half, 2), lax.dynamic_index_in_dim(h_out, d ^ e, 1, keepdims=False)], 1)
        for e in range(4)
    ]
    got_up = to_plane(sent_up)

    branch_late = tie(branch0, *sent_up)
    got_up, (g_mixed, near, away, g_taps) = after(
        got_up,
        conv_backward(idx, held_up, own_out, branch_late, normed0, mixed, qkv, taps, conv, spec, sspec, basis, back),
    )
    u_mlp = jnp.concatenate([total(got_down), total(got_up)], 1)
    p_mlp = line_sum(u_mlp)
    h_mix = both_cores(near, away).reshape(4, 4, r, 3 * half + hl)
    sent_mix = [lax.dynamic_index_in_dim(h_mix, d ^ e, 1, keepdims=False) for e in range(4)]
    got_mix = to_plane(sent_mix)
    ag0, g_gain_mix = input_backward(idx, held_in, own_in, tie(g_mixed, u_mlp, *sent_mix), x, branch0, small)
    keep_act, hand_act = mlp_last(idx, held_down, own_down, hidden, tie(act0, ag0))
    tiny = jnp.concatenate([g_gain_mix, g_gain_mlp, g_taps], 0)
    tiny += lax.ppermute(tiny, "section", SWAP)
    swapped = jnp.concatenate([hand_act, jnp.where(first, ag1, ag0).astype(bf16)], 0)
    (*got_mix, p_mlp), (ag0, tiny, swapped) = after([*got_mix, p_mlp], [ag0, tiny, swapped])
    all_mlp = lax.all_gather(p_mlp, ("dp", "section"), axis=0)
    u_mix = total(got_mix)
    sent_line = [lax.dynamic_index_in_dim(u_mix, (z + k) % 4, 0, keepdims=False) for k in (0, *SHIFTS)]
    got_line = [sent_line[0]] + [lax.ppermute(v, "chan", shift(k)) for k, v in zip(SHIFTS, sent_line[1:])]
    tiny = tie(tiny, *sent_line)
    tiny += lax.ppermute(tiny, "dp", flip(1))
    tiny += lax.ppermute(tiny, "dp", flip(2))
    ag0_late = tie(ag0, *sent_line)
    swapped = lax.ppermute(swapped, "section", SWAP)
    out_act = stacked(keep_act, swapped[:length], bf16)
    out_ag = stacked(jnp.where(first, ag0_late, ag1), swapped[length:], f32)
    got_line, (tiny, out_act, out_ag) = after(got_line, [tiny, out_act, out_ag])
    g_up, g_down, g_out = unpack(unpack_mlp_kernel, idx, [all_mlp], [(part, ff), (4 * part, width), (part, width)])
    p_mix = total(got_line)
    plane_mix = over_plane(p_mix)
    tiny = tie(tiny, p_mix)
    tiny += lax.ppermute(tiny, "chan", flip(1))
    plane_mix, (tiny, g_up, g_down, g_out) = after(plane_mix, [tiny, g_up, g_down, g_out])
    got_tiny = [lax.ppermute(tiny, "chan", flip(2))]
    g_in, g_kern = unpack(unpack_mix_kernel, idx, over_chip(plane_mix), [(part, 3 * width), (part, length)])
    got_tiny, (g_in, g_kern) = after(got_tiny, [g_in, g_kern])
    tiny += got_tiny[0]

    mine = cut(tiny[0:2], z * part, part, 1)
    g_taps = tiny[2:11].reshape(3, 3, width).transpose(1, 0, 2).reshape(3, 3 * width)
    g_taps = cut(g_taps, z * 3 * part, 3 * part, 1)

    return (
        out_act,
        out_ag,
        mine[0:1],
        g_in[None],
        g_taps[None],
        g_kern.T[None],
        g_out[None],
        mine[1:2],
        g_up[None],
        g_down[None],
    )


def fits(mesh):
    return mesh.shape["chan"] == 4 and mesh.shape["dp"] == 4 and mesh.shape["section"] == 2


def shift_down(v, n):
    return jnp.pad(v, ((n, 0), (0, 0)))[: v.shape[0]]


def shift_up(v, n):
    return jnp.pad(v, ((0, n), (0, 0)))[n:]


def plain_body(inputs, lengths, out_grad, ln_mix_gain, w_in, short_taps, long_taps, w_out, ln_mlp_gain, w_up, w_down):
    own = lax.axis_index("section")
    length, width = inputs.shape[2:]
    position = lax.broadcasted_iota(jnp.int32, (length, 1), 0)
    x = lax.dynamic_index_in_dim(inputs[:, 0], own, 0, keepdims=False).astype(f32)
    og = lax.dynamic_index_in_dim(out_grad[:, 0], own, 0, keepdims=False)
    live = (position < lax.dynamic_index_in_dim(lengths[:, 0], own, 0, keepdims=False)).astype(f32)

    def rows(w):
        return lax.all_gather(w[0], "chan", axis=0, tiled=True)

    def cols(w):
        return lax.all_gather(w[0], "chan", axis=1, tiled=True)

    gain_mix = cols(ln_mix_gain[None])[0].astype(f32)
    gain_mlp = cols(ln_mlp_gain[None])[0].astype(f32)
    taps = cols(short_taps).astype(f32)
    kern = cols(long_taps).astype(f32)
    proj_in, proj_out, proj_up, proj_down = rows(w_in), rows(w_out), rows(w_up), rows(w_down)

    basis = jnp.asarray(odd_basis(length))
    decay = jnp.exp(-decay_rate * position.astype(f32))
    half = length

    def spectrum(v):
        both = dot(basis, v)
        return both[:half], both[half:]

    def back(cos_part, sin_part):
        return dot(basis, jnp.concatenate([cos_part, sin_part], 0).astype(bf16), 0, 0)

    kc, ks = spectrum((kern * decay).astype(bf16))
    kc, ks = kc / length, ks / length
    hat0, inv0 = norm_parts(x)
    normed0 = (hat0 * gain_mix).astype(bf16)
    mixed = dot(normed0, proj_in)
    smooth = taps[0] * mixed + taps[1] * shift_down(mixed, 1) + taps[2] * shift_down(mixed, 2)
    query, key, value = smooth[:, :width], smooth[:, width : 2 * width], smooth[:, 2 * width :]
    sc, ss = spectrum((key * value).astype(bf16))
    conv = back(sc * kc - ss * ks, sc * ks + ss * kc)
    gated = (query * conv).astype(bf16)
    act0 = (live * (x + dot(gated, proj_out))).astype(bf16)
    x1 = act0.astype(f32)
    hat1, inv1 = norm_parts(x1)
    normed1 = (hat1 * gain_mlp).astype(bf16)
    pre = dot(normed1, proj_up)
    cdf = 0.5 * (1.0 + lax.erf(pre * math.sqrt(0.5)))
    hidden = (pre * cdf).astype(bf16)
    act1 = (live * (x1 + dot(hidden, proj_down))).astype(bf16)
    masked1 = live * og.astype(f32)
    branch1 = masked1.astype(bf16)
    g_down = dot(hidden, branch1, 0, 0)
    slope = cdf + pre * (jnp.exp(-0.5 * pre * pre) * (1.0 / math.sqrt(2.0 * math.pi)))
    pre_grad = (slope * dot(branch1, proj_down, 1, 1)).astype(bf16)
    g_up = dot(normed1, pre_grad, 0, 0)
    gn1 = dot(pre_grad, proj_up, 1, 1)
    g_gain_mlp = jnp.sum(gn1 * hat1, axis=0)
    ag1 = masked1 + norm_back(gn1, hat1, inv1, gain_mlp)
    ag1_low = ag1.astype(bf16)
    masked0 = live * ag1_low.astype(f32)
    branch0 = masked0.astype(bf16)
    g_out = dot(gated, branch0, 0, 0)
    grad_gated = dot(branch0, proj_out, 1, 1)
    gc, gs = spectrum((grad_gated * query).astype(bf16))
    g_kern = back(sc * gc + ss * gs, sc * gs - ss * gc) * (decay / length)
    g_sig = back(kc * gc + ks * gs, kc * gs - ks * gc)
    g_smooth = jnp.concatenate([grad_gated * conv, g_sig * value, g_sig * key], 1)
    g_taps = jnp.stack([jnp.sum(g_smooth * shift_down(mixed, n), axis=0) if n else jnp.sum(g_smooth * mixed, axis=0) for n in range(3)])
    g_mixed = (taps[0] * g_smooth + taps[1] * shift_up(g_smooth, 1) + taps[2] * shift_up(g_smooth, 2)).astype(bf16)
    g_in = dot(normed0, g_mixed, 0, 0)
    gn0 = dot(g_mixed, proj_in, 1, 1)
    g_gain_mix = jnp.sum(gn0 * hat0, axis=0)
    ag0 = masked0 + norm_back(gn0, hat0, inv0, gain_mix)

    swap = [(0, 1), (1, 0)]
    first = own == 0

    def exchange(own_first, own_second, dtype):
        keep = jnp.where(first, own_first, own_second).astype(dtype)
        other = lax.ppermute(jnp.where(first, own_second, own_first).astype(bf16), "section", swap).astype(dtype)
        both = jnp.stack([jnp.where(first, keep, other), jnp.where(first, other, keep)])
        return both[None, :, None]

    def reduced(g, dim):
        part = lax.psum_scatter(g.astype(bf16), "chan", scatter_dimension=dim, tiled=True)
        return lax.psum(part, ("section", "dp")).astype(f32)[None]

    return (
        exchange(act0, act1, bf16),
        exchange(ag0, ag1, f32),
        reduced(g_gain_mix, 0),
        reduced(g_in, 0),
        reduced(g_taps, 1),
        reduced(g_kern, 1),
        reduced(g_out, 0),
        reduced(g_gain_mlp, 0),
        reduced(g_up, 0),
        reduced(g_down, 0),
    )


def solution(mesh):
    return jax.shard_map(
        fast_body if fits(mesh) else plain_body,
        mesh=mesh,
        in_specs=(
            P(None, ("dp", "chan"), None, None),
            P(None, ("dp", "chan")),
            P(None, ("dp", "chan"), None, None),
            P(None, "chan"),
            P(None, "chan", None),
            P(None, None, "chan"),
            P(None, None, "chan"),
            P(None, "chan", None),
            P(None, "chan"),
            P(None, "chan", None),
            P(None, "chan", None),
        ),
        out_specs=(
            P("section", None, ("dp", "chan"), None, None),
            P("section", None, ("dp", "chan"), None, None),
            P(None, "chan"),
            P(None, "chan", None),
            P(None, None, "chan"),
            P(None, None, "chan"),
            P(None, "chan", None),
            P(None, "chan"),
            P(None, "chan", None),
            P(None, "chan", None),
        ),
        check_vma=False,
    )
```

```python
import math

import jax
import jax.numpy as jnp
import ml_dtypes
import numpy as np
from jax import lax
from jax.experimental import pallas as pl
from jax.experimental.pallas import tpu as pltpu
from jax.sharding import PartitionSpec as P

decay_rate = 0.003
bf16 = jnp.bfloat16
f32 = jnp.float32
MIB = 1 << 20


def odd_basis(length):
    phase = (2 * np.arange(length)[:, None] + 1) * np.arange(length)[None, :] % (4 * length)
    angle = phase * (math.pi / (2 * length))
    return np.concatenate([np.cos(angle), np.sin(angle)], 0).astype(ml_dtypes.bfloat16)


def dot(a, b, ca=1, cb=0):
    return lax.dot_general(a, b, (((ca,), (cb,)), ((), ())), preferred_element_type=f32)


def norm_parts(values):
    centered = values - jnp.mean(values, axis=-1, keepdims=True)
    spread = jnp.mean(centered * centered, axis=-1, keepdims=True)
    inv = lax.rsqrt(spread + 1e-05)
    return centered * inv, inv


def norm_back(grad_normed, hat, inv, gain):
    grad_hat = grad_normed * gain
    return inv * (
        grad_hat
        - jnp.mean(grad_hat, axis=-1, keepdims=True)
        - hat * jnp.mean(grad_hat * hat, axis=-1, keepdims=True)
    )


def call(kernel, grid, in_specs, out_specs, out_shape, scratch, args, flops, nbytes, limit=56, prefetch=0):
    spec = pltpu.PrefetchScalarGridSpec(
        num_scalar_prefetch=prefetch, grid=grid, in_specs=in_specs, out_specs=out_specs, scratch_shapes=scratch
    )
    return pl.pallas_call(
        kernel,
        grid_spec=spec,
        out_shape=out_shape,
        compiler_params=pltpu.CompilerParams(
            dimension_semantics=("arbitrary",) * len(grid), vmem_limit_bytes=limit * MIB
        ),
        cost_estimate=pl.CostEstimate(flops=flops, bytes_accessed=nbytes, transcendentals=0),
    )(*args)


def whole(shape):
    return pl.BlockSpec(shape, lambda *_: (0,) * len(shape), pipeline_mode=pl.Buffered(1))


def rows_of(r, c):
    return pl.BlockSpec((r, c), lambda i, *_: (i, 0))


def cols_of(r, c, start=0):
    return pl.BlockSpec((r, c), lambda i, *_: (0, i + start))


def sds(shape, dtype):
    return jax.ShapeDtypeStruct(shape, dtype)


ANY = pl.BlockSpec(memory_space=pl.ANY)
SHIFTS = (1, 3, 2)


def start_all(copies, sems):
    for n, (a, b) in enumerate(copies):
        pltpu.make_async_copy(a, b, sems.at[n]).start()


def wait_all(copies, sems):
    for n, (a, b) in enumerate(copies):
        pltpu.make_async_copy(a, b, sems.at[n]).wait()


def sources(idx, mine, other):
    z, d, s = idx[0], idx[1], idx[2]
    for e in range(4):
        for j, k in enumerate(SHIFTS):
            for ref, side in ((mine[e], s), (other[e], 1 - s)):
                yield ref, j, lax.rem(z + 4 - k, 4), d ^ e, side


def in_copies(idx, own, mine, other, dst):
    part, half = own.shape[0], own.shape[1] // 2
    r = part // 4
    out = [(own, dst.at[pl.ds(pl.multiple_of(idx[0] * part, 16), part), :])]
    for ref, j, z, d, side in sources(idx, mine, other):
        out.append((ref.at[pl.ds(j * r, r), :],
                    dst.at[pl.ds(pl.multiple_of(z * part + d * r, 16), r), pl.ds(pl.multiple_of(side * half, 128), half)]))
    return out


def up_copies(idx, own, mine, other, dst):
    part, ff = own.shape
    c = ff // 8
    step = part + part // 4
    out = [(own, dst.at[pl.ds(pl.multiple_of(idx[0] * part, 16), part), :])]
    for ref, j, z, d, side in sources(idx, mine, other):
        out.append((ref.at[pl.ds(j * step, part), :],
                    dst.at[pl.ds(pl.multiple_of(z * part, 16), part), pl.ds(pl.multiple_of(side * 4 * c + d * c, 128), c)]))
    return out


def down_copies(idx, own, mine, other, dst):
    q, width = own.shape
    r = q // 4
    h = width // 2
    out = [(own, dst.at[pl.ds(pl.multiple_of(idx[0] * q, 16), q), :])]
    for ref, j, z, d, side in sources(idx, mine, other):
        out.append((ref.at[pl.ds(j * r, r), :],
                    dst.at[pl.ds(pl.multiple_of(z * q + d * r, 16), r), pl.ds(pl.multiple_of(side * h, 128), h)]))
    return out


def out_copies(idx, own, mine, other, dst):
    part, width = own.shape
    r = part // 4
    h = width // 2
    out = [(own, dst.at[pl.ds(pl.multiple_of(idx[0] * part, 16), part), :])]
    for ref, j, z, d, side in sources(idx, mine, other):
        out.append((ref.at[pl.ds(j * 5 * r + part, r), :],
                    dst.at[pl.ds(pl.multiple_of(z * part + d * r, 16), r), pl.ds(pl.multiple_of(side * h, 128), h)]))
    return out


def rest_copies(idx, own, mine, other, dst, start, half):
    part = own.shape[0]
    r = part // 4
    out = [(own, dst.at[pl.ds(pl.multiple_of(idx[0] * part, 16), part), :])]
    for ref, j, z, d, side in sources(idx, mine, other):
        out.append((ref.at[pl.ds(j * r, r), pl.ds(start, half)],
                    dst.at[pl.ds(pl.multiple_of(z * part + d * r, 16), r), pl.ds(pl.multiple_of(side * half, 128), half)]))
    return out


SEMS = pltpu.SemaphoreType.DMA((25,))


CH = 256


def spectra_kernel(idx, *refs):
    held, (own_taps, own_small, basis_in, out_ref, small_ref, taps_ref, taps, small, tall, sig, basis_ref, sems, sems2, sem_b) = refs[:8], refs[8:]
    mine, other = held[:4], held[4:]
    length = taps.shape[1]

    @pl.when(pl.program_id(0) == 0)
    def _():
        copies = rest_copies(idx, own_taps, mine, other, taps, REST_TAPS, length // 2)
        part = own_small.shape[0]
        r = part // 4
        copies2 = [(own_small, small.at[pl.ds(pl.multiple_of(idx[0] * part, 16), part), :])]
        for e in range(4):
            for j, k in enumerate(SHIFTS):
                z = lax.rem(idx[0] + 4 - k, 4)
                copies2.append((mine[e].at[pl.ds(j * r, r), pl.ds(REST_SMALL, 128)],
                                small.at[pl.ds(pl.multiple_of(z * part + (idx[1] ^ e) * r, 16), r), :]))
        start_all(copies2, sems2)
        start_all(copies, sems)
        start_all([(basis_in, basis_ref)], sem_b)
        wait_all(copies2, sems2)
        wide = small[...].astype(f32)
        small_ref[...] = wide.T[0:8]
        for z in range(4):
            for q in range(3):
                tall[(3 * z + q) * part : (3 * z + q + 1) * part] = pltpu.roll(wide[z * part : (z + 1) * part], 126 - q, 1)
        taps_ref[...] = tall[...].T[0:8]
        wait_all(copies, sems)
        wait_all([(basis_in, basis_ref)], sem_b)

    position = lax.broadcasted_iota(jnp.int32, (1, length), 1).astype(f32)
    rows = pl.ds(pl.multiple_of(pl.program_id(0) * CH, CH), CH)
    sig[...] = (taps[rows, :].astype(f32) * (jnp.exp(-decay_rate * position) / length)).astype(bf16)
    out_ref[...] = dot(basis_ref[...], sig[...], 1, 1).astype(bf16)


REST_TAPS, REST_SMALL = 0, 512


def kernel_spectra(idx, rest, own_taps, own_small, basis):
    length = own_taps.shape[1]
    width = own_taps.shape[0] * 4
    return call(
        spectra_kernel,
        (width // CH,),
        [ANY] * 11,
        [cols_of(2 * length, CH), whole((8, width)), whole((8, 3 * width))],
        [sds((2 * length, width), bf16), sds((8, width), f32), sds((8, 3 * width), f32)],
        [pltpu.VMEM((width, length), bf16), pltpu.VMEM((width, 128), bf16), pltpu.VMEM((3 * width, 128), f32), pltpu.VMEM((CH, length), bf16),
         pltpu.VMEM(basis.shape, bf16), SEMS, SEMS, pltpu.SemaphoreType.DMA((1,))],
        (idx, *rest, own_taps, own_small, basis),
        4 * length * length * width,
        basis.size * 2 + 6 * length * width,
        prefetch=1,
    )


class Mover:
    def __init__(self, sems):
        self.sems, self.used = sems, 0

    def start(self, src, dst):
        copy = pltpu.make_async_copy(src, dst, self.sems.at[self.used])
        self.used += 1
        copy.start()
        return copy

    def pieces(self, pairs):
        return [self.start(a, b) for a, b in pairs]


def settle(*copies):
    for c in copies:
        if isinstance(c, list):
            settle(*c)
        else:
            c.wait()


def manual(kernel, n_in, vmem_in, out_shapes, out_specs, scratch, sems, args, flops, nbytes):
    return call(
        kernel,
        (1,),
        [ANY] * n_in + [whole(v.shape) for v in vmem_in],
        out_specs,
        out_shapes,
        [*scratch, pltpu.SemaphoreType.DMA((sems,))],
        (*args, *vmem_in),
        flops,
        nbytes,
        limit=60,
        prefetch=1,
    )


def blocks_of(i):
    return slice(i * CH, (i + 1) * CH)


def front_kernel(idx, *refs):
    held, (own, x_in, spec_in, basis_in, back_in, gain, taps, normed_o, m_o, qkv_o, sspec_o, conv_o, gated_o,
           x_s, w_s, spec_s, basis_s, back_s, normed_s, m_s, qkv_s, sspec_s, conv_s, gated_s,
           pad0, pad1, sig_s, s0, s1, y0, y1, sems) = refs[:8], refs[8:]
    pads, s_s, y_s = (pad0, pad1), (s0, s1), (y0, y1)
    length, width = x_s.shape
    R = 256
    go = Mover(sems)
    x_c = go.start(x_in.at[idx[2]], x_s)
    w_c = go.pieces(in_copies(idx, own, held[:4], held[4:], w_s))
    sent = []
    for p in pads:
        p[0:8] = jnp.zeros((8, 3 * CH), f32)
    settle(x_c)
    for r in range(0, length, R):
        hat, _ = norm_parts(x_s[r : r + R].astype(f32))
        normed_s[r : r + R] = (hat * gain[0:1]).astype(bf16)
    settle(w_c)
    basis_c = go.start(basis_in, basis_s)

    def mix(i):
        w = jnp.concatenate([w_s[:, p * width + i * CH : p * width + (i + 1) * CH] for p in range(3)], 1)
        pads[i % 2][8:] = dot(normed_s[...], w)

    def smooth(i):
        pad = pads[i % 2]
        for r in range(0, length, R):
            now = []
            for p in range(3):
                c = blocks_of(p)
                g = slice(p * width + i * CH, p * width + (i + 1) * CH)
                m_s[p, r : r + R, blocks_of(i)] = pad[8 + r : 8 + r + R, c].astype(bf16)
                now.append(taps[0:1, g] * pad[8 + r : 8 + r + R, c] + taps[3:4, g] * pad[7 + r : 7 + r + R, c]
                           + taps[6:7, g] * pad[6 + r : 6 + r + R, c])
                qkv_s[p, r : r + R, blocks_of(i)] = now[p].astype(bf16)
            sig_s[r : r + R, blocks_of(i)] = (now[1] * now[2]).astype(bf16)
        sent.append(go.start(m_s.at[:, :, blocks_of(i)], m_o.at[:, :, blocks_of(i)]))
        sent.append(go.start(qkv_s.at[:, :, blocks_of(i)], qkv_o.at[:, :, blocks_of(i)]))

    def forth(i):
        s_s[i % 2][...] = dot(basis_s[...], sig_s[:, blocks_of(i)])

    def times(i):
        c = blocks_of(i)
        for r in range(0, length, R):
            at, lo = slice(r, r + R), slice(length + r, length + r + R)
            sc, ss = s_s[i % 2][at], s_s[i % 2][lo]
            sspec_s[at, c] = sc.astype(bf16)
            sspec_s[lo, c] = ss.astype(bf16)
            kc, ks = spec_s[at, c].astype(f32), spec_s[lo, c].astype(f32)
            y_s[i % 2][at] = (sc * kc - ss * ks).astype(bf16)
            y_s[i % 2][lo] = (sc * ks + ss * kc).astype(bf16)
        sent.append(go.start(sspec_s.at[:, c], sspec_o.at[:, c]))

    def back(i):
        c = blocks_of(i)
        conv = dot(back_s[...], y_s[i % 2][...])
        conv_s[:, c] = conv.astype(bf16)
        gated_s[:, c] = (qkv_s[0, :, c].astype(f32) * conv).astype(bf16)
        sent.append(go.start(conv_s.at[:, c], conv_o.at[:, c]))
        sent.append(go.start(gated_s.at[:, c], gated_o.at[:, c]))

    mix(0)
    mix(1)
    settle(basis_c)
    spec_c = go.start(spec_in, spec_s)
    smooth(0)
    forth(0)
    mix(2)
    settle(spec_c)
    back_c = go.start(back_in, back_s)
    sent.append(go.start(normed_s, normed_o))
    smooth(1)
    times(0)
    forth(1)
    settle(back_c)
    back(0)
    smooth(2)
    times(1)
    forth(2)
    back(1)
    times(2)
    back(2)
    settle(sent)


def mixer_front(idx, held, own_in, x, gain, taps, spec, basis, back):
    length, width = x.shape[1:]
    V = pltpu.VMEM
    low, three, tall = (length, width), (3, length, width), (2 * length, width)
    outs = [low, three, three, tall, low, low]
    return manual(
        front_kernel,
        13,
        (gain, taps),
        [sds(s, bf16) for s in outs],
        [ANY] * 6,
        [V(s, bf16) for s in (low, (width, 3 * width), tall, basis.shape, back.shape, *outs)]
        + [V((length + 8, 3 * CH), f32)] * 2 + [V(low, bf16)] + [V((2 * length, CH), f32)] * 2 + [V((2 * length, CH), bf16)] * 2,
        48,
        (idx, *held, own_in, x, spec, basis, back),
        6 * length * width * width + 8 * length * length * width,
        2 * (16 * length * width + 3 * width * width + 2 * basis.size),
    )


def gelu_parts(pre):
    cdf = 0.5 * (1.0 + lax.erf(pre * math.sqrt(0.5)))
    slope = cdf + pre * (jnp.exp(-0.5 * pre * pre) * (1.0 / math.sqrt(2.0 * math.pi)))
    return pre * cdf, slope


def live_rows(idx, rows, start=0):
    return (lax.broadcasted_iota(jnp.int32, (rows, 1), 0) + start < idx[3]).astype(f32)


def near_first(idx, ref, half):
    return (pl.ds(pl.multiple_of(idx[2] * half, 128), half), pl.ds(pl.multiple_of((1 - idx[2]) * half, 128), half))


def out_kernel(idx, *refs):
    rest, (own_out, x_ref, gated_ref, gain_ref, act0_ref, normed_ref, wo_ref, sem_o) = refs[:8], refs[8:]
    R, width = x_ref.shape
    start = pl.program_id(0) * R

    @pl.when(pl.program_id(0) == 0)
    def _():
        outs = out_copies(idx, own_out, rest[:4], rest[4:], wo_ref)
        start_all(outs, sem_o)
        wait_all(outs, sem_o)

    live = live_rows(idx, R, start)
    act0 = (live * (x_ref[...].astype(f32) + dot(gated_ref[...], wo_ref[...]))).astype(bf16)
    act0_ref[...] = act0
    hat, _ = norm_parts(act0.astype(f32))
    normed_ref[...] = (hat * gain_ref[1:2]).astype(bf16)


def mixer_out(idx, rest, own_out, x, gated, gain):
    length, width = gated.shape
    R = 512
    blk = rows_of(R, width)
    return call(
        out_kernel,
        (length // R,),
        [ANY] * 9 + [pl.BlockSpec((None, R, width), lambda i, idx: (idx[2], i, 0)), blk, whole(gain.shape)],
        [blk, blk],
        [sds((length, width), bf16)] * 2,
        [pltpu.VMEM((width, width), bf16), SEMS],
        (idx, *rest, own_out, x, gated, gain),
        2 * length * width * width,
        2 * (4 * length * width + width * width),
        prefetch=1,
    )


def up_kernel(idx, *refs):
    held, (own_up, og_ref, normed_ref, hidden_ref, slope_ref, near_ref, away_ref, wu_ref, turned, sem_u) = refs[:8], refs[8:]
    length, width = og_ref.shape
    half = width // 2
    c = pl.program_id(0)

    @pl.when(c == 0)
    def _():
        ups = up_copies(idx, own_up, held[:4], held[4:], wu_ref)
        start_all(ups, sem_u)
        live = live_rows(idx, length)
        for n, cols in enumerate(near_first(idx, og_ref, half)):
            turned[:, n * half : (n + 1) * half] = (live * og_ref[:, cols].astype(f32)).astype(bf16)
        wait_all(ups, sem_u)

    at = pl.ds(pl.multiple_of(c * width, width), width)
    hid, slope = gelu_parts(dot(normed_ref[...], wu_ref[:, at]))
    hid = hid.astype(bf16)
    hidden_ref[...] = hid
    slope_ref[...] = slope.astype(bf16)
    grad = dot(hid, turned[...], 0, 0).astype(bf16)
    near_ref[...] = grad[:, :half]
    away_ref[...] = grad[:, half:]


def mlp_up(idx, held, own_up, og, normed):
    length, width = normed.shape
    ff = own_up.shape[1]
    half = width // 2
    wide = cols_of(length, width)
    picked = pl.BlockSpec((None, length, width), lambda i, idx: (idx[2], 0, 0), pipeline_mode=pl.Buffered(1))
    return call(
        up_kernel,
        (ff // width,),
        [ANY] * 9 + [picked, whole((length, width))],
        [wide, wide, rows_of(width, half), rows_of(width, half)],
        [sds((length, ff), bf16), sds((length, ff), bf16), sds((ff, half), bf16), sds((ff, half), bf16)],
        [pltpu.VMEM((width, ff), bf16), pltpu.VMEM((length, width), bf16), SEMS],
        (idx, *held, own_up, og, normed),
        4 * length * width * ff,
        2 * (2 * length * width + 2 * width * ff + 2 * length * ff),
        prefetch=1,
    )


def down_kernel(idx, *refs):
    held, (own_up, own_down, act0_in, normed_in, gated_in, og_ref, slope_ref, gain_ref,
           ag_ref, branch_ref, gg_ref, near_ref, away_ref, near_out, away_out,
           wu_ref, wd_ref, gn, branch, turned, act0_ref, normed_ref, gated_ref, sem_u, sem_d, sem_l, sem_m) = refs[:16], refs[16:]
    length, width = og_ref.shape
    half = width // 2
    c = pl.program_id(0)
    live = live_rows(idx, length)
    ups = up_copies(idx, own_up, held[:4], held[4:8], wu_ref)
    late = [(normed_in, normed_ref), (act0_in, act0_ref), (gated_in, gated_ref)]

    @pl.when(c == 0)
    def _():
        downs = down_copies(idx, own_down, held[8:12], held[12:], wd_ref)
        start_all(downs, sem_d)
        branch[...] = (live * og_ref[...].astype(f32)).astype(bf16)
        gn[...] = jnp.zeros((length, width), f32)
        wait_all(downs, sem_d)
        start_all(ups, sem_u)
        start_all(late[:1], sem_l)

    at = pl.ds(pl.multiple_of(c * width, width), width)
    pre = (slope_ref[...].astype(f32) * dot(branch[...], wd_ref[at, :], 1, 1)).astype(bf16)
    for n, cols in enumerate(near_first(idx, turned, half)):
        turned[:, cols] = pre[:, n * half : (n + 1) * half]

    @pl.when(c == 0)
    def _():
        wait_all(ups, sem_u)
        wait_all(late[:1], sem_l)
        start_all(late[1:], sem_m)

    gn[...] += dot(pre, wu_ref[:, at], 1, 1)
    grad = dot(normed_ref[...], turned[...], 0, 0).astype(bf16)
    near_ref[...] = grad[:, :half]
    away_ref[...] = grad[:, half:]

    @pl.when(c == pl.num_programs(0) - 1)
    def _():
        wait_all(late[1:], sem_m)
        hat, inv = norm_parts(act0_ref[...].astype(f32))
        gg_ref[...] = jnp.sum(gn[...] * hat, axis=0, keepdims=True)
        ag = live * og_ref[...].astype(f32) + norm_back(gn[...], hat, inv, gain_ref[1:2])
        ag_ref[...] = ag
        branch_ref[...] = (live * ag).astype(bf16)
        for n, cols in enumerate(near_first(idx, branch_ref, half)):
            turned[:, n * half : (n + 1) * half] = branch_ref[:, cols]
        g_out = dot(gated_ref[...], turned[...], 0, 0).astype(bf16)
        near_out[...] = g_out[:, :half]
        away_out[...] = g_out[:, half:]


def mlp_down(idx, held_up, held_down, own_up, own_down, og, act0, normed, slope, gated, gain):
    length, width = act0.shape
    ff = own_up.shape[1]
    half = width // 2
    picked = pl.BlockSpec((None, length, width), lambda i, idx: (idx[2], 0, 0), pipeline_mode=pl.Buffered(1))
    one = whole((length, width))
    wide = cols_of(length, width)
    full = sds((length, width), bf16)
    col = pltpu.VMEM((length, width), f32)
    low = pltpu.VMEM((length, width), bf16)
    return call(
        down_kernel,
        (ff // width,),
        [ANY] * 21 + [picked, wide, whole(gain.shape)],
        [one, one, whole((1, width)), cols_of(width, half), cols_of(width, half), whole((width, half)), whole((width, half))],
        [sds((length, width), f32), full, sds((1, width), f32), sds((width, ff // 2), bf16), sds((width, ff // 2), bf16),
         sds((width, half), bf16), sds((width, half), bf16)],
        [pltpu.VMEM((width, ff), bf16), pltpu.VMEM((ff, width), bf16), col, low, low, low, low, low, SEMS, SEMS,
         pltpu.SemaphoreType.DMA((1,)), pltpu.SemaphoreType.DMA((2,))],
        (idx, *held_up, *held_down, own_up, own_down, act0, normed, gated, og, slope, gain),
        6 * length * width * ff,
        2 * (7 * length * width + 3 * width * ff + length * ff),
        prefetch=1,
    )


def last_kernel(idx, *refs):
    held, (own_down, hidden_ref, act0_ref, keep_ref, hand_ref, wd_ref, acc, sem_d) = refs[:8], refs[8:]
    length, width = act0_ref.shape
    c = pl.program_id(0)

    @pl.when(c == 0)
    def _():
        downs = down_copies(idx, own_down, held[:4], held[4:], wd_ref)
        start_all(downs, sem_d)
        acc[...] = act0_ref[...].astype(f32)
        wait_all(downs, sem_d)

    acc[...] += dot(hidden_ref[...], wd_ref[pl.ds(pl.multiple_of(c * width, width), width), :])

    @pl.when(c == pl.num_programs(0) - 1)
    def _():
        act1 = (live_rows(idx, length) * acc[...]).astype(bf16)

        @pl.when(idx[2] == 0)
        def _():
            keep_ref[...] = act0_ref[...]
            hand_ref[...] = act1

        @pl.when(idx[2] != 0)
        def _():
            keep_ref[...] = act1
            hand_ref[...] = act0_ref[...]


def mlp_last(idx, held, own_down, hidden, act0):
    length, width = act0.shape
    ff = own_down.shape[0] * 4
    one = whole((length, width))
    return call(
        last_kernel,
        (ff // width,),
        [ANY] * 9 + [cols_of(length, width), one],
        [one, one],
        [sds((length, width), bf16)] * 2,
        [pltpu.VMEM((ff, width), bf16), pltpu.VMEM((length, width), f32), SEMS],
        (idx, *held, own_down, hidden, act0),
        2 * length * width * ff,
        2 * (2 * length * width + width * ff + length * ff),
        prefetch=1,
    )


def conv_back_kernel(idx, *refs):
    held, (own_out, branch_in, normed_in, m_in, qkv_in, conv_in, spec_in, sspec_in, basis_in, back_in, taps,
           g_o, near_o, away_o, gtaps_ref,
           w_s, branch_s, normed_s, m_s, qkv_s, conv_s, spec_s, sspec_s, basis_s, back_s,
           gpad0, gpad1, sig_s, s0, s1, y0, y1, both_s, gm0, gm1, g0_s, g1_s, kern0, kern1, near0, near1, away0, away1,
           sems) = refs[:8], refs[8:]
    gpads, s_s, y_s, gms, g_s, kerns, near_s, away_s = ((gpad0, gpad1), (s0, s1), (y0, y1), (gm0, gm1), (g0_s, g1_s),
                                                        (kern0, kern1), (near0, near1), (away0, away1))
    length, width = branch_s.shape
    half = width // 2
    hl = length // 2
    R = 256
    nb = width // CH
    go = Mover(sems)
    branch_c = go.start(branch_in, branch_s)
    w_c = go.pieces(out_copies(idx, own_out, held[:4], held[4:], w_s))
    basis_c = go.start(basis_in, basis_s)

    def fetch(i):
        c = blocks_of(i)
        return [go.start(qkv_in.at[:, :, c], qkv_s.at[:, :, c]), go.start(conv_in.at[:, c], conv_s.at[:, c])]

    def fetch_spectra(i):
        c = blocks_of(i)
        return [go.start(spec_in.at[:, c], spec_s.at[:, c]), go.start(sspec_in.at[:, c], sspec_s.at[:, c])]

    def fetch_mixed(i):
        c = blocks_of(i)
        return go.start(m_in.at[:, :, c], m_s.at[:, :, c])

    for p in gpads:
        p[length : length + 8] = jnp.zeros((8, 3 * CH), f32)
    sent = [[], []]
    settle(branch_c, w_c)
    first_c = fetch(0)

    def spread_back(i):
        s_s[i % 2][0:length] = dot(branch_s[...], w_s[blocks_of(i), :], 1, 1)

    def gate(i):
        c = blocks_of(i)
        for r in range(0, length, R):
            at = slice(r, r + R)
            gg = s_s[i % 2][at]
            sig_s[at, c] = (gg * qkv_s[0, at, c].astype(f32)).astype(bf16)
            gpads[i % 2][at, 0:CH] = gg * conv_s[at, c].astype(f32)

    def forth(i):
        s_s[i % 2][...] = dot(basis_s[...], sig_s[:, blocks_of(i)])

    def times(i):
        c = blocks_of(i)
        y = y_s[i % 2]
        for r in range(0, length, R):
            at, lo = slice(r, r + R), slice(length + r, length + r + R)
            gc, gs = s_s[i % 2][at], s_s[i % 2][lo]
            kc, ks = spec_s[at, c].astype(f32), spec_s[lo, c].astype(f32)
            y[at, 0:CH] = (kc * gc + ks * gs).astype(bf16)
            y[lo, 0:CH] = (kc * gs - ks * gc).astype(bf16)
            sc, ss = sspec_s[at, c].astype(f32), sspec_s[lo, c].astype(f32)
            y[at, CH:] = (sc * gc + ss * gs).astype(bf16)
            y[lo, CH:] = (sc * gs - ss * gc).astype(bf16)

    def back(i):
        both_s[...] = dot(back_s[...], y_s[i % 2][...])

    def unsmooth(i):
        b = blocks_of(i)
        gpad, gm, kern = gpads[i % 2], gms[i % 2], kerns[i % 2]
        settle(sent[i % 2])
        for r in range(0, length, R):
            at = slice(r, r + R)
            g_sig = both_s[at, :CH]
            gpad[at, CH : 2 * CH] = g_sig * qkv_s[2, at, b].astype(f32)
            gpad[at, 2 * CH :] = g_sig * qkv_s[1, at, b].astype(f32)
            position = (lax.broadcasted_iota(jnp.int32, (R, 1), 0) + r).astype(f32)
            kern[:, at] = (both_s[at, CH:] * (jnp.exp(-decay_rate * position) / length)).T.astype(bf16)
        sums = [[jnp.zeros((1, CH), f32)] * 3 for _ in range(3)]
        for r in range(0, length, R):
            at = slice(r, r + R)
            for p in range(3):
                c = blocks_of(p)
                t = slice(p * width + i * CH, p * width + (i + 1) * CH)
                now = [gpad[r + n : r + n + R, c] for n in range(3)]
                g = (taps[0:1, t] * now[0] + taps[3:4, t] * now[1] + taps[6:7, t] * now[2]).astype(bf16)
                g_s[i % 2][p, at] = g
                for n in range(2):
                    to = jnp.where(idx[2] == n, 0, half) + p * (CH // 2)
                    gm[at, pl.ds(pl.multiple_of(to, 128), CH // 2)] = g[:, n * (CH // 2) : (n + 1) * (CH // 2)]
                mixed = m_s[p, at, b].astype(f32)
                sums[p] = [sums[p][n] + jnp.sum(now[n] * mixed, axis=0, keepdims=True) for n in range(3)]
        for p in range(3):
            for n in range(3):
                gtaps_ref[3 * p + n : 3 * p + n + 1, b] = sums[p][n]
        side = slice(3 * half, 3 * half + hl)
        mine, other = near_first(idx, kern, hl)
        sent[i % 2] = [go.start(g_s[i % 2], g_o.at[:, :, b]), go.start(kern.at[:, mine], near_o.at[b, side]),
                       go.start(kern.at[:, other], away_o.at[b, side])]

    def grad(i):
        g = dot(normed_s[...], gms[i % 2][...], 0, 0).astype(bf16)
        near_s[i % 2][...] = g[:, :half]
        away_s[i % 2][...] = g[:, half:]
        c = slice(i * half, (i + 1) * half)
        sent[i % 2] += [go.start(near_s[i % 2], near_o.at[:, c]), go.start(away_s[i % 2], away_o.at[:, c])]

    spread_back(0)
    spread_back(1)
    settle(basis_c, first_c)
    spectra_c = fetch_spectra(0)
    gate(0)
    forth(0)
    settle(spectra_c)
    back_c = go.start(back_in, back_s)
    next_c = fetch(1)
    times(0)
    settle(next_c, back_c)
    spectra_c = fetch_spectra(1)
    mixed_c = fetch_mixed(0)
    normed_c = go.start(normed_in, normed_s)
    back(0)
    gate(1)
    forth(1)
    spread_back(2)
    settle(spectra_c, mixed_c, normed_c)
    next_c = fetch(2)
    mixed_c = fetch_mixed(1)
    spectra_c = fetch_spectra(2)
    unsmooth(0)
    times(1)
    back(1)
    grad(0)
    settle(next_c, mixed_c, spectra_c)
    mixed_c = fetch_mixed(2)
    gate(2)
    forth(2)
    unsmooth(1)
    times(2)
    grad(1)
    back(2)
    settle(mixed_c)
    unsmooth(2)
    grad(2)
    settle(sent)


def conv_backward(idx, held, own_out, branch, normed, mixed, qkv, taps, conv, spec, sspec, basis, back):
    length, width = branch.shape
    half = width // 2
    mix = (width, 3 * half + length // 2)
    V = pltpu.VMEM
    low, three, tall = (length, width), (3, length, width), (2 * length, width)
    twice = lambda s, t: [V(s, t)] * 2
    return manual(
        conv_back_kernel,
        18,
        (taps,),
        [sds(three, bf16), sds(mix, bf16), sds(mix, bf16), sds((9, width), f32)],
        [ANY] * 3 + [whole((9, width))],
        [V(s, bf16) for s in ((width, width), low, low, three, three, low, tall, tall, basis.shape, back.shape)]
        + twice((length + 8, 3 * CH), f32) + [V(low, bf16)] + twice((2 * length, CH), f32) + twice((2 * length, 2 * CH), bf16)
        + [V((length, 2 * CH), f32)] + twice((length, 3 * CH), bf16) + twice((3, length, CH), bf16) + twice((CH, length), bf16)
        + twice((width, half), bf16) + twice((width, half), bf16),
        64,
        (idx, *held, own_out, branch, normed, mixed, qkv, conv, spec, sspec, basis, back),
        8 * length * width * width + 12 * length * length * width,
        2 * (22 * length * width + 2 * basis.size + 2 * mix[0] * mix[1]),
    )


def norm_back_kernel(idx, *refs):
    held, (own_ref, g_ref, x_ref, masked_ref, gain_ref, ag_ref, gg_ref, wi_ref, sems) = refs[:8], refs[8:]
    width = x_ref.shape[1]

    @pl.when(pl.program_id(0) == 0)
    def _():
        copies = in_copies(idx, own_ref, held[:4], held[4:], wi_ref)
        start_all(copies, sems)
        wait_all(copies, sems)

    gn = dot(jnp.concatenate([g_ref[p] for p in range(3)], 1), wi_ref[...], 1, 1)
    hat, inv = norm_parts(x_ref[...].astype(f32))
    part = jnp.sum(gn * hat, axis=0, keepdims=True)

    @pl.when(pl.program_id(0) == 0)
    def _():
        gg_ref[...] = part

    @pl.when(pl.program_id(0) > 0)
    def _():
        gg_ref[...] += part

    ag_ref[...] = masked_ref[...].astype(f32) + norm_back(gn, hat, inv, gain_ref[0:1])


def input_backward(idx, held, own_in, g_mixed, x, masked, gain):
    length, width = masked.shape
    R = 512
    blk = rows_of(R, width)
    return call(
        norm_back_kernel,
        (length // R,),
        [ANY] * 9 + [pl.BlockSpec((3, R, width), lambda i, *_: (0, i, 0)),
                     pl.BlockSpec((None, R, width), lambda i, idx: (idx[2], i, 0)), blk, whole(gain.shape)],
        [blk, pl.BlockSpec((1, width), lambda *_: (0, 0))],
        [sds((length, width), f32), sds((1, width), f32)],
        [pltpu.VMEM((width, 3 * width), bf16), SEMS],
        (idx, *held, own_in, g_mixed, x, masked, gain),
        6 * length * width * width,
        2 * (7 * length * width + 3 * width * width),
        prefetch=1,
    )


def unpack_mlp_kernel(idx, all_ref, up, down, out):
    part = up.shape[0]
    q = up.shape[1] // 4
    h = down.shape[1] // 2
    r = part // 4
    for n in range(8):
        d, side = n // 2, n % 2
        cols = slice(side * h, side * h + h)
        down[d * part : (d + 1) * part, cols] = all_ref[n, 0:part].astype(f32)
        up[:, d * q + side * h : d * q + side * h + h] = all_ref[n, part : 2 * part].astype(f32)
        out[d * r : (d + 1) * r, cols] = all_ref[n, 2 * part :].astype(f32)


def unpack_mix_kernel(idx, *refs):
    held, (g_in, g_kern) = refs[:8], refs[8:]
    part, length = g_kern.shape
    width = 4 * part
    r = part // 4
    h = width // 2
    b = CH // 2
    for e in range(4):
        at = pl.ds(pl.multiple_of((idx[1] ^ e) * r, 16), r)
        for ref, side in ((held[e], idx[2]), (held[4 + e], 1 - idx[2])):
            for i in range(width // CH):
                for p in range(3):
                    c = i * h + p * b
                    g_in[at, pl.ds(pl.multiple_of(p * width + i * CH + side * b, 128), b)] = ref[:, c : c + b].astype(f32)
            g_kern[at, pl.ds(pl.multiple_of(side * (length // 2), 128), length // 2)] = ref[:, 3 * h :].astype(f32)


def unpack(kernel, idx, held, shapes):
    return call(
        kernel,
        (1,),
        [whole(h.shape) for h in held],
        [whole(s) for s in shapes],
        [sds(s, f32) for s in shapes],
        [],
        (idx, *held),
        0,
        sum(6 * math.prod(s) for s in shapes),
        prefetch=1,
    )


SWAP = [(0, 1), (1, 0)]


def shift(k):
    return [(i, (i + k) % 4) for i in range(4)]


def flip(e):
    return [(i, i ^ e) for i in range(4)]


def tie(value, *others):
    return lax.optimization_barrier((value, *others))[0]


def over_line(piece):
    return jnp.concatenate([lax.ppermute(piece, "chan", shift(k)) for k in SHIFTS], 0)


def over_plane(near):
    return [near] + [lax.ppermute(near, "dp", flip(e)) for e in (1, 2, 3)]


def over_chip(mine):
    return mine + [lax.ppermute(m, "section", SWAP) for m in mine]


def total(parts):
    out = parts[0].astype(f32)
    for p in parts[1:]:
        out += p.astype(f32)
    return out.astype(bf16)


def fold_plane(parts):
    return total([parts[0]] + [lax.ppermute(parts[e], "dp", flip(e)) for e in (1, 2, 3)])


def fold_line(held, z):
    def at(k):
        return lax.dynamic_index_in_dim(held, (z + k) % 4, 0, keepdims=False)

    return total([at(0)] + [lax.ppermute(at(k), "chan", shift(k)) for k in SHIFTS])


def cut(v, at, size, axis):
    return lax.dynamic_slice_in_dim(v, at, size, axis)


def fast_body(inputs, lengths, out_grad, ln_mix_gain, w_in, short_taps, long_taps, w_out, ln_mlp_gain, w_up, w_down):
    z, d, s = lax.axis_index("chan"), lax.axis_index("dp"), lax.axis_index("section")
    length = inputs.shape[2]
    width = inputs.shape[3]
    part = w_in.shape[1]
    ff = w_up.shape[2]
    half = width // 2
    hl = length // 2
    r = part // 4
    count = lax.dynamic_index_in_dim(lengths[:, 0], s, 0, keepdims=False)
    idx = jnp.stack([z, d, s, count]).astype(jnp.int32)
    x, og = inputs[:, 0], out_grad[:, 0]
    table = odd_basis(length)
    basis, back = jnp.asarray(table), jnp.asarray(np.ascontiguousarray(table.T))
    first = s == 0

    def after(parts, values):
        return lax.optimization_barrier((list(parts), list(values)))

    def both_cores(near, away):
        return total([near, lax.ppermute(away, "section", SWAP)])

    def stacked(keep, other, dtype):
        other = other.astype(dtype)
        both = jnp.stack([jnp.where(first, keep, other), jnp.where(first, other, keep)])
        return both[None, :, None]

    def to_plane(parts):
        return [parts[0]] + [lax.ppermute(parts[e], "dp", flip(e)) for e in (1, 2, 3)]

    def line_sum(held):
        return lax.psum_scatter(held, "chan", scatter_dimension=0, tiled=False)

    own_in, own_out, own_up, own_down = w_in[0], w_out[0], w_up[0], w_down[0]
    own_taps = long_taps[0].T
    small = jnp.concatenate([ln_mix_gain, ln_mlp_gain, short_taps[0].reshape(9, part)], 0)
    own_small = jnp.pad(small.T, ((0, 0), (0, 128 - 11)))
    piece = jnp.concatenate([cut(own_taps, s * hl, hl, 1), own_small], 1)
    split = piece.shape[1]
    piece = jnp.concatenate([cut(piece, d * r, r, 0), cut(cut(own_in, d * r, r, 0), s * 3 * half, 3 * half, 1)], 1)
    near, idx = lax.optimization_barrier((over_line(piece), idx))
    near_rest, near_in = near[:, :split], near[:, split:]
    plane_rest = over_plane(near_rest)
    plane_in = over_plane(near_in)
    piece_mlp = jnp.concatenate(
        [
            cut(cut(own_down, d * part, part, 0), s * half, half, 1),
            cut(own_up, s * (ff // 2) + d * (ff // 8), ff // 8, 1),
            cut(cut(own_out, d * r, r, 0), s * half, half, 1),
        ],
        0,
    )
    line_mlp = lax.all_gather(tie(piece_mlp, near), "chan", axis=0)
    held_rest = over_chip(plane_rest)

    plane_in, (spec, small, taps) = after(
        plane_in, kernel_spectra(idx, held_rest, tie(own_taps, near_in), own_small, basis)
    )
    held_in = over_chip(plane_in)
    line_mlp = [lax.dynamic_index_in_dim(line_mlp, (z + 4 - k) % 4, 0, keepdims=False) for k in SHIFTS]
    near_up = jnp.concatenate([v[part:] for v in line_mlp], 0)
    near_down = jnp.concatenate([v[:part] for v in line_mlp], 0)
    plane_up = over_plane(near_up)
    plane_down = over_plane(near_down)
    plane_up, (normed0, mixed, qkv, sspec, conv, gated) = after(
        plane_up, mixer_front(idx, held_in, own_in, x, small, taps, tie(spec, near_up, near_down), basis, back)
    )
    held_up = over_chip(plane_up)
    act0, normed1 = mixer_out(idx, held_up, own_out, x, gated, small)
    plane_down, (hidden, slope, near, away) = after(plane_down, mlp_up(idx, held_up, own_up, og, normed1))
    held_down = over_chip(plane_down)

    h_down = both_cores(near, away).reshape(4, 4, part, half)
    sent_down = [lax.dynamic_index_in_dim(h_down, d ^ e, 1, keepdims=False) for e in range(4)]
    got_down = to_plane(sent_down)
    got_down, (ag1, branch0, g_gain_mlp, near, away, near_out, away_out) = after(
        got_down,
        mlp_down(
            idx, held_up, held_down, own_up, own_down, og, act0, normed1, tie(slope, *sent_down), gated, small
        ),
    )
    h_up = both_cores(near, away).reshape(4, part, ff // 2)
    h_out = both_cores(near_out, away_out).reshape(4, 4, r, half)
    sent_up = [
        jnp.concatenate([cut(h_up, (d ^ e) * half, half, 2), lax.dynamic_index_in_dim(h_out, d ^ e, 1, keepdims=False)], 1)
        for e in range(4)
    ]
    got_up = to_plane(sent_up)

    branch_late = tie(branch0, *sent_up)
    got_up, (g_mixed, near, away, g_taps) = after(
        got_up,
        conv_backward(idx, held_up, own_out, branch_late, normed0, mixed, qkv, taps, conv, spec, sspec, basis, back),
    )
    u_mlp = jnp.concatenate([total(got_down), total(got_up)], 1)
    p_mlp = line_sum(u_mlp)
    h_mix = both_cores(near, away).reshape(4, 4, r, 3 * half + hl)
    sent_mix = [lax.dynamic_index_in_dim(h_mix, d ^ e, 1, keepdims=False) for e in range(4)]
    got_mix = to_plane(sent_mix)
    ag0, g_gain_mix = input_backward(idx, held_in, own_in, tie(g_mixed, u_mlp, *sent_mix), x, branch0, small)
    keep_act, hand_act = mlp_last(idx, held_down, own_down, hidden, tie(act0, ag0))
    tiny = jnp.concatenate([g_gain_mix, g_gain_mlp, g_taps], 0)
    tiny += lax.ppermute(tiny, "section", SWAP)
    tiny += lax.ppermute(tiny, "dp", flip(1))
    swapped = jnp.concatenate([hand_act, jnp.where(first, ag1, ag0).astype(bf16)], 0)
    (*got_mix, p_mlp), (ag0, tiny, swapped) = after([*got_mix, p_mlp], [ag0, tiny, swapped])
    all_mlp = lax.all_gather(p_mlp, ("dp", "section"), axis=0)
    u_mix = total(got_mix)
    sent_line = [lax.dynamic_index_in_dim(u_mix, (z + k) % 4, 0, keepdims=False) for k in (0, *SHIFTS)]
    got_line = [sent_line[0]] + [lax.ppermute(v, "chan", shift(k)) for k, v in zip(SHIFTS, sent_line[1:])]
    tiny = tie(tiny, *sent_line)
    tiny += lax.ppermute(tiny, "dp", flip(2))
    ag0_late = tie(ag0, *sent_line)
    swapped = lax.ppermute(swapped, "section", SWAP)
    out_act = stacked(keep_act, swapped[:length], bf16)
    out_ag = stacked(jnp.where(first, ag0_late, ag1), swapped[length:], f32)
    got_line, (tiny, out_act, out_ag) = after(got_line, [tiny, out_act, out_ag])
    g_up, g_down, g_out = unpack(unpack_mlp_kernel, idx, [all_mlp], [(part, ff), (4 * part, width), (part, width)])
    p_mix = total(got_line)
    plane_mix = over_plane(p_mix)
    tiny = tie(tiny, p_mix)
    tiny += lax.ppermute(tiny, "chan", flip(1))
    plane_mix, (tiny, g_up, g_down, g_out) = after(plane_mix, [tiny, g_up, g_down, g_out])
    got_tiny = [lax.ppermute(tiny, "chan", flip(2))]
    g_in, g_kern = unpack(unpack_mix_kernel, idx, over_chip(plane_mix), [(part, 3 * width), (part, length)])
    got_tiny, (g_in, g_kern) = after(got_tiny, [g_in, g_kern])
    tiny += got_tiny[0]

    mine = cut(tiny[0:2], z * part, part, 1)
    g_taps = tiny[2:11].reshape(3, 3, width).transpose(1, 0, 2).reshape(3, 3 * width)
    g_taps = cut(g_taps, z * 3 * part, 3 * part, 1)

    return (
        out_act,
        out_ag,
        mine[0:1],
        g_in[None],
        g_taps[None],
        g_kern.T[None],
        g_out[None],
        mine[1:2],
        g_up[None],
        g_down[None],
    )


def fits(mesh):
    return mesh.shape["chan"] == 4 and mesh.shape["dp"] == 4 and mesh.shape["section"] == 2


def shift_down(v, n):
    return jnp.pad(v, ((n, 0), (0, 0)))[: v.shape[0]]


def shift_up(v, n):
    return jnp.pad(v, ((0, n), (0, 0)))[n:]


def plain_body(inputs, lengths, out_grad, ln_mix_gain, w_in, short_taps, long_taps, w_out, ln_mlp_gain, w_up, w_down):
    own = lax.axis_index("section")
    length, width = inputs.shape[2:]
    position = lax.broadcasted_iota(jnp.int32, (length, 1), 0)
    x = lax.dynamic_index_in_dim(inputs[:, 0], own, 0, keepdims=False).astype(f32)
    og = lax.dynamic_index_in_dim(out_grad[:, 0], own, 0, keepdims=False)
    live = (position < lax.dynamic_index_in_dim(lengths[:, 0], own, 0, keepdims=False)).astype(f32)

    def rows(w):
        return lax.all_gather(w[0], "chan", axis=0, tiled=True)

    def cols(w):
        return lax.all_gather(w[0], "chan", axis=1, tiled=True)

    gain_mix = cols(ln_mix_gain[None])[0].astype(f32)
    gain_mlp = cols(ln_mlp_gain[None])[0].astype(f32)
    taps = cols(short_taps).astype(f32)
    kern = cols(long_taps).astype(f32)
    proj_in, proj_out, proj_up, proj_down = rows(w_in), rows(w_out), rows(w_up), rows(w_down)

    basis = jnp.asarray(odd_basis(length))
    decay = jnp.exp(-decay_rate * position.astype(f32))
    half = length

    def spectrum(v):
        both = dot(basis, v)
        return both[:half], both[half:]

    def back(cos_part, sin_part):
        return dot(basis, jnp.concatenate([cos_part, sin_part], 0).astype(bf16), 0, 0)

    kc, ks = spectrum((kern * decay).astype(bf16))
    kc, ks = kc / length, ks / length
    hat0, inv0 = norm_parts(x)
    normed0 = (hat0 * gain_mix).astype(bf16)
    mixed = dot(normed0, proj_in)
    smooth = taps[0] * mixed + taps[1] * shift_down(mixed, 1) + taps[2] * shift_down(mixed, 2)
    query, key, value = smooth[:, :width], smooth[:, width : 2 * width], smooth[:, 2 * width :]
    sc, ss = spectrum((key * value).astype(bf16))
    conv = back(sc * kc - ss * ks, sc * ks + ss * kc)
    gated = (query * conv).astype(bf16)
    act0 = (live * (x + dot(gated, proj_out))).astype(bf16)
    x1 = act0.astype(f32)
    hat1, inv1 = norm_parts(x1)
    normed1 = (hat1 * gain_mlp).astype(bf16)
    pre = dot(normed1, proj_up)
    cdf = 0.5 * (1.0 + lax.erf(pre * math.sqrt(0.5)))
    hidden = (pre * cdf).astype(bf16)
    act1 = (live * (x1 + dot(hidden, proj_down))).astype(bf16)
    masked1 = live * og.astype(f32)
    branch1 = masked1.astype(bf16)
    g_down = dot(hidden, branch1, 0, 0)
    slope = cdf + pre * (jnp.exp(-0.5 * pre * pre) * (1.0 / math.sqrt(2.0 * math.pi)))
    pre_grad = (slope * dot(branch1, proj_down, 1, 1)).astype(bf16)
    g_up = dot(normed1, pre_grad, 0, 0)
    gn1 = dot(pre_grad, proj_up, 1, 1)
    g_gain_mlp = jnp.sum(gn1 * hat1, axis=0)
    ag1 = masked1 + norm_back(gn1, hat1, inv1, gain_mlp)
    ag1_low = ag1.astype(bf16)
    masked0 = live * ag1_low.astype(f32)
    branch0 = masked0.astype(bf16)
    g_out = dot(gated, branch0, 0, 0)
    grad_gated = dot(branch0, proj_out, 1, 1)
    gc, gs = spectrum((grad_gated * query).astype(bf16))
    g_kern = back(sc * gc + ss * gs, sc * gs - ss * gc) * (decay / length)
    g_sig = back(kc * gc + ks * gs, kc * gs - ks * gc)
    g_smooth = jnp.concatenate([grad_gated * conv, g_sig * value, g_sig * key], 1)
    g_taps = jnp.stack([jnp.sum(g_smooth * shift_down(mixed, n), axis=0) if n else jnp.sum(g_smooth * mixed, axis=0) for n in range(3)])
    g_mixed = (taps[0] * g_smooth + taps[1] * shift_up(g_smooth, 1) + taps[2] * shift_up(g_smooth, 2)).astype(bf16)
    g_in = dot(normed0, g_mixed, 0, 0)
    gn0 = dot(g_mixed, proj_in, 1, 1)
    g_gain_mix = jnp.sum(gn0 * hat0, axis=0)
    ag0 = masked0 + norm_back(gn0, hat0, inv0, gain_mix)

    swap = [(0, 1), (1, 0)]
    first = own == 0

    def exchange(own_first, own_second, dtype):
        keep = jnp.where(first, own_first, own_second).astype(dtype)
        other = lax.ppermute(jnp.where(first, own_second, own_first).astype(bf16), "section", swap).astype(dtype)
        both = jnp.stack([jnp.where(first, keep, other), jnp.where(first, other, keep)])
        return both[None, :, None]

    def reduced(g, dim):
        part = lax.psum_scatter(g.astype(bf16), "chan", scatter_dimension=dim, tiled=True)
        return lax.psum(part, ("section", "dp")).astype(f32)[None]

    return (
        exchange(act0, act1, bf16),
        exchange(ag0, ag1, f32),
        reduced(g_gain_mix, 0),
        reduced(g_in, 0),
        reduced(g_taps, 1),
        reduced(g_kern, 1),
        reduced(g_out, 0),
        reduced(g_gain_mlp, 0),
        reduced(g_up, 0),
        reduced(g_down, 0),
    )


def solution(mesh):
    return jax.shard_map(
        fast_body if fits(mesh) else plain_body,
        mesh=mesh,
        in_specs=(
            P(None, ("dp", "chan"), None, None),
            P(None, ("dp", "chan")),
            P(None, ("dp", "chan"), None, None),
            P(None, "chan"),
            P(None, "chan", None),
            P(None, None, "chan"),
            P(None, None, "chan"),
            P(None, "chan", None),
            P(None, "chan"),
            P(None, "chan", None),
            P(None, "chan", None),
        ),
        out_specs=(
            P("section", None, ("dp", "chan"), None, None),
            P("section", None, ("dp", "chan"), None, None),
            P(None, "chan"),
            P(None, "chan", None),
            P(None, None, "chan"),
            P(None, None, "chan"),
            P(None, "chan", None),
            P(None, "chan"),
            P(None, "chan", None),
            P(None, "chan", None),
        ),
        check_vma=False,
    )
```
